32 devices in a mesh: dp: 8 (over z, y), tensor: 4 (over x, core).
Axes of the slice: x: 2, y: 2, z: 4, core: 2. Of those that a mesh axis runs over, the one named last changes fastest.
Arguments:
- tokens: bfloat16 [4096, 2048], P(('dp', 'tensor')), may hold values from -6 to 6
- segments: int32 [4096], P('dp'), may hold values from 0 to 15, never falling along the last dimension, each value on 1 to 1024 neighbouring positions
- attn_gain: float32 [2, 2048], replicated, may hold values from 0.5 to 1.5
- w_query: bfloat16 [2, 2048, 2048], P(None, 'dp', 'tensor'), may hold values from -0.125 to 0.125
- w_key: bfloat16 [2, 2048, 2048], P(None, 'dp', 'tensor'), may hold values from -0.125 to 0.125
- w_value: bfloat16 [2, 2048, 3456], P(None, 'dp', 'tensor'), may hold values from -0.125 to 0.125
- w_swish: bfloat16 [2, 2048, 3456], P(None, 'dp', 'tensor'), may hold values from -0.125 to 0.125
- w_output: bfloat16 [2, 3456, 2048], P(None, 'tensor', 'dp'), may hold values from -0.109375 to 0.109375
- ffn_gain: float32 [2, 2048], replicated, may hold values from 0.5 to 1.5
- w_gelu: bfloat16 [2, 2048, 3456], P(None, 'dp', 'tensor'), may hold values from -0.125 to 0.125
- w_up: bfloat16 [2, 2048, 3456], P(None, 'dp', 'tensor'), may hold values from -0.125 to 0.125
- w_down: bfloat16 [2, 3456, 2048], P(None, 'tensor', 'dp'), may hold values from -0.109375 to 0.109375
- cotangent: bfloat16 [4096, 2048], P(('dp', 'tensor')), may hold values from -6 to 6
Outputs:
- output: bfloat16 [4096, 2048], P(('dp', 'tensor'))
- input_grad: float32 [4096, 2048], P(('dp', 'tensor'))
- grad_attn_gain: float32 [2, 2048], replicated
- grad_query: float32 [2, 2048, 2048], P(None, 'dp', 'tensor')
- grad_key: float32 [2, 2048, 2048], P(None, 'dp', 'tensor')
- grad_value: float32 [2, 2048, 3456], P(None, 'dp', 'tensor')
- grad_swish: float32 [2, 2048, 3456], P(None, 'dp', 'tensor')
- grad_output: float32 [2, 3456, 2048], P(None, 'tensor', 'dp')
- grad_ffn_gain: float32 [2, 2048], replicated
- grad_gelu: float32 [2, 2048, 3456], P(None, 'dp', 'tensor')
- grad_up: float32 [2, 2048, 3456], P(None, 'dp', 'tensor')
- grad_down: float32 [2, 3456, 2048], P(None, 'tensor', 'dp')
The draws below stay inside these ranges and needn't reach their ends.
Inputs may be any that keep to these rules, and one draw needn't show every extreme that they name: `segments`: ids never fall along the tokens; each document covers 1 to min(2048, 1024) consecutive tokens, and one covers exactly that many.
All inputs are finite; a program needn't handle non-finite values.
Results may differ from the reference program's by a relative error of at most 0.035.
Values may be sent and summed in bfloat16 or wider, within the bound.
A program may use at most 256 MiB of HBM per device.

```python
import math
import jax
import jax.numpy as jnp
import numpy as np
from jax import lax

D = 2048
HEADS = 8
HEAD_QK = 256
HEAD_V = 432
FFN = 3456
LAYERS = 2
LEN = 512
TOKENS = 4096
QK = 2048
VAL = 3456


def level_of(key, shape, shards, least, high):
    level = 1.0
    for position, parts in shards:
        steps = jax.random.uniform(jax.random.fold_in(jax.random.fold_in(key, 6), position), (parts,), jnp.float32, least / len(shards), high / len(shards))
        level = level * jnp.repeat(jnp.exp(steps), shape[position] // parts).reshape((-1,) + (1,) * (len(shape) - 1 - position))
    return level


def length_profile(amount, total, limit, lean):
    portions = [(1 << 20) // math.isqrt(grade ** lean) + 1 for grade in range(2, amount + 1)]
    spare, given = total - limit - (amount - 1), [1] * (amount - 1)
    while spare > 0:
        movable = [i for i in range(amount - 1) if given[i] < limit]
        pool, budget = sum([portions[i] for i in movable]), spare
        for i in movable:
            more = min(limit - given[i], max(1, budget * portions[i] // pool), spare)
            given[i] = given[i] + more
            spare = spare - more
    return np.array([limit] + given)


def uneven_parts(stream_key, number_of, total, limit, slope):
    if number_of == 2:
        one = jax.random.randint(stream_key, (), max(1, total - limit), min(limit, total - 1) + 1)
        return jnp.stack([one, total - one])
    tallies = jnp.asarray(length_profile(number_of, total, limit, slope), jnp.int32)
    couples = (number_of - 1) // 2
    source_of, receiver = tallies[1:1 + 2 * couples:2], tallies[2:2 + 2 * couples:2]
    slack = jnp.minimum(source_of - 1, limit - receiver)
    shifted = jax.random.randint(jax.random.fold_in(stream_key, 1), (couples,), 0, 1 << 20) % (slack + 1)
    tallies = tallies.at[1:1 + 2 * couples:2].set(source_of - shifted).at[2:2 + 2 * couples:2].set(receiver + shifted)
    return tallies[jax.random.permutation(jax.random.fold_in(stream_key, 2), number_of)]


def normal_values(key, dims, spread, limit, cuts=(), kind=jnp.bfloat16):
    loudness = level_of(key, dims, cuts, -0.22, 0.18) if cuts else 1.0
    array = jax.random.normal(key, dims, jnp.float32) * spread * loudness
    return jnp.minimum(jnp.maximum(array, -limit), limit).astype(kind)


def setup_inputs(seed: int = 0) -> dict:
    splits = jax.random.split(jax.random.key(seed), 14)
    tokens = normal_values(splits[0], (TOKENS, D), 1.0, 6.0, ((0, 32),))
    segments = jnp.searchsorted(jnp.cumsum(uneven_parts(splits[1], max(8, TOKENS // 256), TOKENS, min(2048, TOKENS // 4), 1)), jnp.arange(TOKENS), side="right").astype(jnp.int32)
    attn_gain = jnp.clip(1.0 + 0.1 * jax.random.normal(splits[2], (LAYERS, D), jnp.float32), 0.5, 1.5)
    w_query = normal_values(splits[3], (LAYERS, D, QK), D ** -0.5, 0.125, ((1, 8), (2, 4)))
    w_key = normal_values(splits[4], (LAYERS, D, QK), D ** -0.5, 0.125, ((1, 8), (2, 4)))
    w_value = normal_values(splits[5], (LAYERS, D, VAL), D ** -0.5, 0.125, ((1, 8), (2, 4)))
    w_swish = normal_values(splits[6], (LAYERS, D, VAL), D ** -0.5, 0.125, ((1, 8), (2, 4)))
    w_output = normal_values(splits[7], (LAYERS, VAL, D), VAL ** -0.5, 0.109375, ((1, 4), (2, 8)))
    ffn_gain = jnp.clip(1.0 + 0.1 * jax.random.normal(splits[8], (LAYERS, D), jnp.float32), 0.5, 1.5)
    w_gelu = normal_values(splits[9], (LAYERS, D, FFN), D ** -0.5, 0.125, ((1, 8), (2, 4)))
    w_up = normal_values(splits[10], (LAYERS, D, FFN), D ** -0.5, 0.125, ((1, 8), (2, 4)))
    w_down = normal_values(splits[11], (LAYERS, FFN, D), FFN ** -0.5, 0.109375, ((1, 4), (2, 8)))
    cotangent = normal_values(splits[12], (TOKENS, D), 1.0, 6.0, ((0, 32),))
    return dict(tokens=tokens, segments=segments, attn_gain=attn_gain, w_query=w_query, w_key=w_key, w_value=w_value, w_swish=w_swish, w_output=w_output, ffn_gain=ffn_gain, w_gelu=w_gelu, w_up=w_up, w_down=w_down, cotangent=cotangent)


EPS = 1e-06
HEAD_FLOOR = 1.0
HIGHEST_ACCURACY = lax.Precision.HIGHEST

@jax.custom_vjp
def low(v):
    return lax.optimization_barrier(v.astype(jnp.bfloat16)).astype(jnp.float32)

@jax.custom_vjp
def low_back(v):
    return v

def low_keep(v):
    return (low(v), None)

def low_pass(kept, grad):
    return (grad,)

def back_keep(v):
    return (v, None)

def back_low(kept, grad):
    return (low(grad),)
low.defvjp(low_keep, low_pass)
low_back.defvjp(back_keep, back_low)

def norm_rows(values, gain):
    return values * lax.rsqrt(lax.optimization_barrier(jnp.mean(values * values, -1, keepdims=True)) + EPS) * gain

def norm_heads(values):
    return values * lax.rsqrt(lax.optimization_barrier(jnp.mean(values * values, -1, keepdims=True)) + HEAD_FLOOR)

def gelu_tanh(values):
    return jax.nn.gelu(values, approximate=True)

def rotation(length, width):
    half = width // 2
    place = jnp.arange(length, dtype=jnp.float32)
    freqs = 10000.0 ** (-jnp.arange(half, dtype=jnp.float32) / half)
    angle = place[:, None] * freqs[None, :]
    return (jnp.cos(angle)[:, None, :], jnp.sin(angle)[:, None, :])

def rotate(values, cosine, sine):
    half = values.shape[-1] // 2
    first = values[..., :half]
    second = values[..., half:]
    return jnp.concatenate([first * cosine - second * sine, second * cosine + first * sine], -1)

def decay_mask(seg_rows, head_ids, length):
    place = jnp.arange(length, dtype=jnp.int32)
    dist = place[:, None] - place[None, :]
    same = (seg_rows[:, :, None] == seg_rows[:, None, :]) & (dist >= 0)[None]
    rates = jnp.log1p(-2.0 ** (-5.0 - head_ids))
    decay = jnp.exp(jnp.maximum(dist, 0).astype(jnp.float32)[None] * rates[:, None, None])
    return jnp.where(same[:, None], decay[None], 0.0)

def matmul(left, right):
    return jnp.dot(left, right, precision=HIGHEST_ACCURACY, preferred_element_type=jnp.float32)

def reference(tokens, segments, attn_gain, w_query, w_key, w_value, w_swish, w_output, ffn_gain, w_gelu, w_up, w_down, cotangent):
    seqs = TOKENS // LEN
    seg_rows = segments.reshape(seqs, LEN)
    head_ids = jnp.arange(HEADS, dtype=jnp.float32)
    cosine, sine = rotation(LEN, HEAD_QK)
    score_scale = HEAD_QK ** (-0.5)

    def retain(pieces):
        rotated_query, rotated_key, vals, seg = pieces
        mask = decay_mask(seg[None], head_ids, LEN)[0]
        unnormalized_scores = low_back(jnp.einsum('eys,zys->yez', rotated_query, rotated_key, precision=HIGHEST_ACCURACY) * score_scale)
        probs = low(unnormalized_scores * mask)
        return low_back(jnp.einsum('hlm,mhv->lhv', probs, vals, precision=HIGHEST_ACCURACY))

    def forward(residual, a_gain, wq, wk, wv, ws, wo, f_gain, wg, wu, wd):
        for layer in range(LAYERS):
            normed = low(norm_rows(residual, a_gain[layer]))
            query = low_back(matmul(normed, wq[layer]))
            keys = low_back(matmul(normed, wk[layer]))
            vals = low(low_back(matmul(normed, wv[layer]))).reshape(seqs, LEN, HEADS, HEAD_V)
            swish = low_back(matmul(normed, ws[layer]))
            rotated_query = low(rotate(query.reshape(seqs, LEN, HEADS, HEAD_QK), cosine, sine))
            rotated_key = low(rotate(keys.reshape(seqs, LEN, HEADS, HEAD_QK), cosine, sine))
            mixed = lax.map(jax.checkpoint(retain), (rotated_query, rotated_key, vals, seg_rows))
            zed = norm_heads(mixed).reshape(TOKENS, HEADS * HEAD_V)
            gated = low(jax.nn.silu(swish) * zed)
            mid = residual + low_back(matmul(gated, wo[layer]))
            normed_ffn = low(norm_rows(mid, f_gain[layer]))
            gate_pre = low_back(matmul(normed_ffn, wg[layer]))
            up_pre = low_back(matmul(normed_ffn, wu[layer]))
            hidden = low(gelu_tanh(gate_pre) * up_pre)
            residual = mid + low_back(matmul(hidden, wd[layer]))
        return residual
    inputs = (tokens.astype(jnp.float32), attn_gain.astype(jnp.float32), w_query.astype(jnp.float32), w_key.astype(jnp.float32), w_value.astype(jnp.float32), w_swish.astype(jnp.float32), w_output.astype(jnp.float32), ffn_gain.astype(jnp.float32), w_gelu.astype(jnp.float32), w_up.astype(jnp.float32), w_down.astype(jnp.float32))
    result, pullback = jax.vjp(forward, *inputs)
    grads = pullback(cotangent.astype(jnp.float32))
    return (result.astype(jnp.bfloat16), grads[0], grads[1], grads[2], grads[3], grads[4], grads[5], grads[6], grads[7], grads[8], grads[9], grads[10])
```

```python
import functools

import jax
import jax.numpy as jnp
from jax import lax
from jax.experimental import pallas as pl
from jax.experimental.pallas import tpu as pltpu
from jax.sharding import PartitionSpec as P

HEAD_QK = 256
HEAD_V = 432
LEN = 512

EPS = 1e-06
HEAD_FLOOR = 1.0
NN = (((1,), (0,)), ((), ()))
NT = (((1,), (1,)), ((), ()))
TN = (((0,), (0,)), ((), ()))
MESH = pl.DeviceIdType.MESH
BF16 = jnp.bfloat16
F32 = jnp.float32
LOOK = 3
VMEM_LIMIT = 60 * 1024 * 1024


def dot(a, b, dims=NN):
    return lax.dot_general(a, b, dims, preferred_element_type=F32)


def loop(steps, body):
    lax.fori_loop(0, steps, lambda i, c: (body(i), c)[1], 0)


class Place:
    def __init__(self):
        dp, tensor = lax.axis_index("dp"), lax.axis_index("tensor")
        self.dp, self.tensor = dp, tensor
        self.z, self.y = lax.div(dp, 2), lax.rem(dp, 2)
        self.x, self.c = lax.div(tensor, 2), lax.rem(tensor, 2)
        self.half = lax.rem(self.z, 2)
        self.zn = self.z + 1 - 2 * self.half

    def at(self, z=None, y=None, x=None, c=None):
        z = self.z if z is None else z
        y = self.y if y is None else y
        x = self.x if x is None else x
        c = self.c if c is None else c
        return (z * 2 + y, x * 2 + c)

    def zplus(self, d):
        return lax.rem(self.z + d + 4, 4)

    def sib(self):
        return self.at(c=1 - self.c)

    def xn(self):
        return self.at(x=1 - self.x)

    def yn(self):
        return self.at(y=1 - self.y)

    def znb(self):
        return self.at(z=self.zn)

    def peers(self):
        return [self.sib(), self.xn(), self.yn()] + [self.at(z=self.zplus(d)) for d in (1, 2, 3)]

    def greet(self):
        bar = pltpu.get_barrier_semaphore()
        peers = self.peers()
        for p in peers:
            pl.semaphore_signal(bar, inc=1, device_id=p, device_id_type=MESH)
        pl.semaphore_wait(bar, len(peers))


def remote(src, dst, ssem, rsem, dev):
    return pltpu.make_async_remote_copy(
        src_ref=src, dst_ref=dst, send_sem=ssem, recv_sem=rsem, device_id=dev, device_id_type=MESH
    )


def block(half, tensor, rows):
    return pl.ds(pl.multiple_of((half * 4 + tensor) * rows, rows), rows)


def gather_acts(me, buf, rows, ssem, rsem, fill=()):
    fill = list(fill)

    def step():
        if fill:
            fill.pop(0)()

    def move(k, half, x, dev):
        r = block(half, x * 2 + me.c, rows)
        return remote(buf.at[r], buf.at[r], ssem.at[k], rsem.at[k], dev)

    h, x = me.half, me.x
    own_x = move(0, h, x, me.xn())
    own_z = move(1, h, x, me.znb())
    own_s = move(2, h, x, me.sib())
    own_x.start()
    own_z.start()
    own_s.start()
    step()
    own_z.wait_recv()
    z_x = move(3, 1 - h, x, me.xn())
    z_s = move(4, 1 - h, x, me.sib())
    z_x.start()
    z_s.start()
    own_x.wait_recv()
    x_s = move(5, h, 1 - x, me.sib())
    x_s.start()
    step()
    z_x.wait_recv()
    g_s = move(6, 1 - h, 1 - x, me.sib())
    g_s.start()
    for m in (own_s, z_s, x_s, g_s):
        m.wait_recv()
    for m in (own_x, own_z, own_s, z_x, z_s, x_s, g_s):
        m.wait_send()
    while fill:
        step()


def sum_acts(me, part, rows, sib_buf, x_buf, z_buf, ssem, rsem, body, fill=()):
    fill = list(fill)

    def step():
        if fill:
            fill.pop(0)()

    h, x = me.half, me.x
    order = [(1 - h, 1 - x), (h, 1 - x), (1 - h, x), (h, x)]
    sibs = []
    for j, (hh, xx) in enumerate(order):
        m = remote(part.at[block(hh, xx * 2 + 1 - me.c, rows)], sib_buf.at[j], ssem.at[j], rsem.at[j], me.sib())
        m.start()
        sibs.append(m)
    chunk = 64

    def mine(j, i):
        hh, xx = order[j]
        return pl.ds(pl.multiple_of((hh * 4 + xx * 2 + me.c) * rows + i * chunk, chunk), chunk)

    def add(j, extra=None):
        def go(i):
            r = mine(j, i)
            k = pl.ds(pl.multiple_of(i * chunk, chunk), chunk)
            v = part[r, :].astype(F32) + sib_buf[j, k, :].astype(F32)
            if extra is not None:
                v = v + extra[k, :].astype(F32)
            part[r, :] = v.astype(BF16)

        loop(rows // chunk, go)

    def my_block(j):
        hh, xx = order[j]
        return part.at[block(hh, xx * 2 + me.c, rows)]

    to_x = []
    for j in (0, 1):
        sibs[j].wait_recv()
        add(j)
        m = remote(my_block(j), x_buf.at[j], ssem.at[4 + j], rsem.at[4 + j], me.xn())
        m.start()
        to_x.append(m)
    step()
    sibs[2].wait_recv()
    to_x[0].wait_recv()
    add(2, x_buf.at[0])
    to_z = remote(my_block(2), z_buf, ssem.at[6], rsem.at[6], me.znb())
    to_z.start()
    sibs[3].wait_recv()
    step()
    to_x[1].wait_recv()
    to_z.wait_recv()
    small = 32

    def last(i):
        k = pl.ds(pl.multiple_of(i * small, small), small)
        r = pl.ds(pl.multiple_of((h * 4 + x * 2 + me.c) * rows + i * small, small), small)
        v = part[r, :].astype(F32) + sib_buf[3, k, :].astype(F32)
        v = v + x_buf[1, k, :].astype(F32) + z_buf[k, :].astype(F32)
        body(i * small, small, v)

    loop(rows // small, last)
    for m in sibs + to_x + [to_z]:
        m.wait_send()
    while fill:
        step()


def unit_rows(qk, val, ffn):
    sizes = (("q", qk), ("k", qk), ("v", val), ("s", val), ("o", val), ("g", ffn), ("u", ffn), ("d", ffn))
    out, at = {}, 0
    for name, n in sizes:
        out[name] = (at, n)
        at += n
    return out, at


def rms(v, floor):
    return lax.rsqrt(jnp.mean(v * v, -1, keepdims=True) + floor)


def forward_kernel(
    dims,
    tokens, mask, cosine, sine, attn_gain, ffn_gain, wl,
    output, x_mid, mids, wf, s_n, s_nf, s_q, s_k, s_v, s_s, s_m, s_gt, s_g, s_u, s_h, s_p,
    W, N0, N1, part, sib_buf, x_buf, z_buf, q, k, v, s, m, gt, g, u, h, p,
    zs, zr, ys, yr, lo, ld, ags, agr, rss, rsr, sv,
):
    layers, rows, lanes, units, scale = dims
    me = Place()
    names = list(units)
    groups = [(l, units[n]) for l in range(layers) for n in names]
    spot = {(l, n): l * len(names) + i for l in range(layers) for i, n in enumerate(names)}
    my_lane = pl.multiple_of(me.dp * lanes, lanes)

    def z_copy(i, d):
        l, (r0, n) = groups[i]
        tz = me.zplus(d)
        return remote(
            wl.at[l, lax.rem(tz, 2), pl.ds(r0, n)], wf.at[l, pl.ds(r0, n), pl.ds(my_lane, lanes)],
            zs.at[i, d - 1], zr.at[i, d - 1], me.at(z=tz),
        )

    def y_copy(i, d):
        l, (r0, n) = groups[i]
        lane = pl.ds(pl.multiple_of((me.zplus(-d) * 2 + me.y) * lanes, lanes), lanes)
        dst = wf.at[l, pl.ds(r0, n), lane]
        src = wl.at[l, me.half, pl.ds(r0, n)] if d == 0 else dst
        return remote(src, dst, ys.at[i, d], yr.at[i, d], me.yn())

    def local_copy(i):
        l, (r0, n) = groups[i]
        return pltpu.make_async_copy(
            wl.at[l, me.half, pl.ds(r0, n)], wf.at[l, pl.ds(r0, n), pl.ds(my_lane, lanes)], lo.at[i]
        )

    def issue(i):
        if i < len(groups):
            for d in (1, 2, 3):
                z_copy(i, d).start()
            y_copy(i, 0).start()
            local_copy(i).start()

    done = [0]

    def advance():
        i = done[0]
        if i >= len(groups):
            return
        done[0] += 1
        for d in (1, 3, 2):
            z_copy(i, d).wait_recv()
            y_copy(i, d).start()
        issue(i + LOOK)

    def take(l, *wanted):
        idx = [spot[l, n] for n in wanted]
        while done[0] <= min(idx[-1] + 1, len(groups) - 1):
            advance()
        copies = []
        for i in idx:
            for d in range(4):
                y_copy(i, d).wait_recv()
            local_copy(i).wait()
            r0, n = groups[i][1]
            c = pltpu.make_async_copy(wf.at[l, pl.ds(r0, n)], W.at[pl.ds(r0, n)], ld.at[i])
            c.start()
            copies.append(c)
        for c in copies:
            c.wait()

    saves = []

    def save(src, dst):
        c = pltpu.make_async_copy(src, dst, sv.at[len(saves)])
        c.start()
        saves.append(c)

    waited = [0]

    def settle():
        while waited[0] < len(saves):
            saves[waited[0]].wait()
            waited[0] += 1

    def weight(n):
        r0, size = units[n]
        return W[pl.ds(r0, size), :]

    def seq_rows(i):
        return pl.ds(pl.multiple_of(i * LEN, LEN), LEN)

    seqs = 2
    own = (me.half * 4 + me.tensor) * rows

    def own_rows(r0, n):
        return pl.ds(pl.multiple_of(own + r0, n), n)

    me.greet()
    for i in range(LOOK):
        issue(i)

    small = 32

    def first_norm(i):
        r = pl.ds(pl.multiple_of(i * small, small), small)
        x = tokens[r, :].astype(F32)
        N0[own_rows(i * small, small), :] = (x * rms(x, EPS) * attn_gain[0:1, :]).astype(BF16)

    loop(rows // small, first_norm)

    for l in range(layers):
        gather_acts(me, N0, rows, ags.at[2 * l], agr.at[2 * l], (advance,))
        save(N0, s_n.at[l])
        for name, dst in (("q", q), ("k", k)):
            take(l, name)

            def project(i, name=name, dst=dst):
                r = seq_rows(i)
                t = dot(N0[r, :], weight(name), NT)
                half = t.shape[1] // 2
                t1, t2 = t[:, :half], t[:, half:]
                c, sn = cosine[...], sine[...]
                dst[r, :half] = (t1 * c - t2 * sn).astype(BF16)
                dst[r, half:] = (t2 * c + t1 * sn).astype(BF16)

            loop(seqs, project)
        save(q, s_q.at[l])
        save(k, s_k.at[l])
        take(l, "v")

        def values(i):
            r = seq_rows(i)
            v[r, :] = dot(N0[r, :], weight("v"), NT).astype(BF16)

        loop(seqs, values)
        save(v, s_v.at[l])

        def retain(i):
            r = seq_rows(i)
            raw = dot(q[r, :], k[r, :], NT) * scale
            probs = (raw * mask[i]).astype(BF16)
            p[i] = probs
            m[r, :] = dot(probs, v[r, :])

        loop(seqs, retain)
        save(p, s_p.at[l])
        save(m, s_m.at[l])
        take(l, "s")

        def gate(i):
            r = seq_rows(i)
            t = dot(N0[r, :], weight("s"), NT)
            s[r, :] = t
            mix = m[r, :]
            gt[r, :] = (jax.nn.silu(t) * (mix * rms(mix, HEAD_FLOOR))).astype(BF16)

        loop(seqs, gate)
        save(s, s_s.at[l])
        save(gt, s_gt.at[l])
        take(l, "o")

        def project_out(i, src=gt, name="o"):
            r = pl.ds(pl.multiple_of(i * 256, 256), 256)
            part[r, :] = dot(src[r, :], weight(name)).astype(BF16)

        loop(seqs * LEN // 256, project_out)

        def to_mid(r0, n, total, l=l):
            r = pl.ds(pl.multiple_of(r0, n), n)
            x = (tokens[r, :].astype(F32) if l == 0 else x_mid[l - 1, r, :]) + total
            mids[l, r, :] = x
            N1[own_rows(r0, n), :] = (x * rms(x, EPS) * ffn_gain[l : l + 1, :]).astype(BF16)

        sum_acts(me, part, rows, sib_buf, x_buf, z_buf, rss.at[2 * l], rsr.at[2 * l], to_mid, (advance,))
        gather_acts(me, N1, rows, ags.at[2 * l + 1], agr.at[2 * l + 1], (advance,))
        save(N1, s_nf.at[l])
        take(l, "g")

        def gates(i):
            r = seq_rows(i)
            g[r, :] = dot(N1[r, :], weight("g"), NT)

        loop(seqs, gates)
        take(l, "u")

        def ups(i):
            r = seq_rows(i)
            t = dot(N1[r, :], weight("u"), NT)
            u[r, :] = t
            h[r, :] = (jax.nn.gelu(g[r, :], approximate=True) * t).astype(BF16)

        loop(seqs, ups)
        save(g, s_g.at[l])
        save(u, s_u.at[l])
        save(h, s_h.at[l])
        take(l, "d")
        loop(seqs * LEN // 256, functools.partial(project_out, src=h, name="d"))

        def to_next(r0, n, total, l=l):
            r = pl.ds(pl.multiple_of(r0, n), n)
            x = mids[l, r, :] + total
            if l + 1 < layers:
                x_mid[l, r, :] = x
                N0[own_rows(r0, n), :] = (x * rms(x, EPS) * attn_gain[l + 1 : l + 2, :]).astype(BF16)
            else:
                output[r, :] = x.astype(BF16)

        settle()
        sum_acts(me, part, rows, sib_buf, x_buf, z_buf, rss.at[2 * l + 1], rsr.at[2 * l + 1], to_next, (advance,))
    settle()
    for i in range(len(groups)):
        for d in (1, 2, 3):
            z_copy(i, d).wait_send()
        for d in range(4):
            y_copy(i, d).wait_send()


def run_forward(dims, tokens, mask, cosine, sine, attn_gain, ffn_gain, wl):
    layers, rows, lanes, units, scale = dims
    depth = tokens.shape[1]
    total = wl.shape[2]
    group = 8 * rows
    seqs = group // LEN
    qk, val, ffn = units["q"][1], units["v"][1], units["g"][1]
    vm = pl.BlockSpec(memory_space=pltpu.VMEM)
    hb = pl.BlockSpec(memory_space=pl.ANY)
    outs = [
        ((rows, depth), BF16), ((layers - 1, rows, depth), F32), ((layers, rows, depth), F32),
        ((layers, total, depth), BF16), ((layers, group, depth), BF16), ((layers, group, depth), BF16),
        ((layers, group, qk), BF16), ((layers, group, qk), BF16), ((layers, group, val), BF16),
        ((layers, group, val), F32), ((layers, group, val), F32), ((layers, group, val), BF16),
        ((layers, group, ffn), F32), ((layers, group, ffn), F32), ((layers, group, ffn), BF16),
        ((layers, seqs, LEN, LEN), BF16),
    ]
    n_groups = layers * len(units)
    dma = pltpu.SemaphoreType.DMA
    return pl.pallas_call(
        functools.partial(forward_kernel, dims),
        out_shape=[jax.ShapeDtypeStruct(s, d) for s, d in outs],
        in_specs=[vm] * 6 + [hb],
        out_specs=[vm] * 3 + [hb] * 13,
        scratch_shapes=[
            pltpu.VMEM((total, depth), BF16),
            pltpu.VMEM((group, depth), BF16), pltpu.VMEM((group, depth), BF16), pltpu.VMEM((group, depth), BF16),
            pltpu.VMEM((4, rows, depth), BF16), pltpu.VMEM((2, rows, depth), BF16), pltpu.VMEM((rows, depth), BF16),
            pltpu.VMEM((group, qk), BF16), pltpu.VMEM((group, qk), BF16), pltpu.VMEM((group, val), BF16),
            pltpu.VMEM((group, val), F32), pltpu.VMEM((group, val), F32), pltpu.VMEM((group, val), BF16),
            pltpu.VMEM((group, ffn), F32), pltpu.VMEM((group, ffn), F32), pltpu.VMEM((group, ffn), BF16),
            pltpu.VMEM((seqs, LEN, LEN), BF16),
            dma((n_groups, 3)), dma((n_groups, 3)), dma((n_groups, 4)), dma((n_groups, 4)),
            dma((n_groups,)), dma((n_groups,)),
            dma((2 * layers, 7)), dma((2 * layers, 7)), dma((2 * layers, 7)), dma((2 * layers, 7)),
            dma((12 * layers,)),
        ],
        compiler_params=pltpu.CompilerParams(collective_id=0, has_side_effects=True, vmem_limit_bytes=VMEM_LIMIT),
    )(tokens, mask, cosine, sine, attn_gain, ffn_gain, wl)


SLOTS = 4


def backward_kernel(
    dims,
    cot, tokens, x_mid, mids, mask, cosine, sine, attn_gain, ffn_gain,
    wf, s_n, s_nf, s_q, s_k, s_v, s_s, s_m, s_gt, s_g, s_u, s_h, s_p,
    input_grad, gains, rz,
    gr, nb, ga0, ga1, part, sib_buf, x_buf, z_buf, W, a1, a2, a3, q, k, v, p, t1, t2, tq, tk, G, ry, acc, acc_in,
    ys, yr, zs, zr, os, ags, agr, rss, rsr, ld, gns, gnr, credit,
):
    layers, rows, lanes, units, scale = dims
    me = Place()
    depth = cot.shape[1]
    wide = 512
    small = 32
    seqs = 2
    order = list(reversed(range(layers)))
    jobs = [(l, n) for l in order for n in ("d", "g", "u", "o", "q", "k", "v", "s")]
    index = {job: i for i, job in enumerate(jobs)}
    own = (me.half * 4 + me.tensor) * rows
    ffn_row = units["g"][0]
    attn_end = ffn_row
    total_rows = units["d"][0] + units["d"][1]

    def own_rows(r0, n):
        return pl.ds(pl.multiple_of(own + r0, n), n)

    def seq_rows(i):
        return pl.ds(pl.multiple_of(i * LEN, LEN), LEN)

    def lane(i):
        return pl.ds(pl.multiple_of(i * lanes, lanes), lanes)

    def y_send(i, d):
        n = units[jobs[i][1]][1]
        tz = me.zplus(d)
        return remote(
            G.at[i % SLOTS, pl.ds(0, n), lane(tz * 2 + 1 - me.y)], ry.at[i % SLOTS, pl.ds(0, n), lane(tz)],
            ys.at[i, d], yr.at[i, d], me.yn(),
        )

    def z_send(i, d):
        l, name = jobs[i]
        r0, n = units[name]
        tz = me.zplus(d)
        return remote(
            G.at[i % SLOTS, pl.ds(0, n), lane(tz * 2 + me.y)], rz.at[l, me.half, d // 2, pl.ds(r0, n)],
            zs.at[i, d - 1], zr.at[i, d - 1], me.at(z=tz),
        )

    def own_copy(i):
        l, name = jobs[i]
        r0, n = units[name]
        return pltpu.make_async_copy(
            G.at[i % SLOTS, pl.ds(0, n), lane(me.dp)], rz.at[l, me.half, 0, pl.ds(r0, n)], os.at[i]
        )

    def retire(i):
        for d in range(4):
            y_send(i, d).wait_send()
        for d in (1, 2, 3):
            z_send(i, d).wait_send()
        own_copy(i).wait()

    def make(l, name, left, right):
        i = index[l, name]
        n = units[name][1]
        if i >= SLOTS:
            retire(i - SLOTS)

        def go(j):
            cols = pl.ds(pl.multiple_of(j * wide, wide), wide)
            G[i % SLOTS, :n, cols] = dot(left[...], right[:, cols], TN).astype(BF16)

        loop(depth // wide, go)
        if i >= SLOTS:
            pl.semaphore_wait(credit.at[i % SLOTS], 1)
        for d in (2, 1, 3, 0):
            y_send(i, d).start()

    def combine(l, name):
        i = index[l, name]
        n = units[name][1]
        for d in (2, 1, 3, 0):
            y_send(i, d).wait_recv()
            tz = me.zplus(d)

            def add(j, tz=tz):
                r = pl.ds(pl.multiple_of(j * 16, 16), 16)
                c = lane(tz * 2 + me.y)
                both = G[i % SLOTS, r, c].astype(F32) + ry[i % SLOTS, r, lane(tz)].astype(F32)
                G[i % SLOTS, r, c] = both.astype(BF16)

            loop(n // 16, add)
            if d:
                z_send(i, d).start()
            else:
                own_copy(i).start()
        if i + SLOTS < len(jobs):
            pl.semaphore_signal(credit.at[i % SLOTS], inc=1, device_id=me.yn(), device_id_type=MESH)

    spots = {}

    def load(key, src, dst):
        c = pltpu.make_async_copy(src, dst, ld.at[len(spots)])
        c.start()
        spots[key] = c

    def ready(*keys):
        for key in keys:
            spots[key].wait()

    def load_ffn(l):
        load(("wf", l), wf.at[l, pl.ds(ffn_row, total_rows - ffn_row)], W.at[pl.ds(0, total_rows - ffn_row)])
        load(("g", l), s_g.at[l], a1)
        load(("u", l), s_u.at[l], a2)

    def load_attn(l):
        load(("wa", l), wf.at[l, pl.ds(0, attn_end)], W.at[pl.ds(0, attn_end)])
        load(("s", l), s_s.at[l], a1)
        load(("m", l), s_m.at[l], a2)
        load(("q", l), s_q.at[l], q)
        load(("k", l), s_k.at[l], k)
        load(("v", l), s_v.at[l], v)
        load(("p", l), s_p.at[l], p)

    def load_h(l):
        load(("h", l), s_h.at[l], a3)

    def load_nf(l):
        load(("nf", l), s_nf.at[l], nb)

    def load_gt(l):
        load(("gt", l), s_gt.at[l], a3)

    def load_n(l):
        load(("n", l), s_n.at[l], nb)

    def weight(name, base):
        r0, n = units[name]
        return W[pl.ds(r0 - base, n), :]

    def norm_back(x, gain, dn, gain_row):
        e = rms(x, EPS)
        gx = dn * gain
        inner = jnp.sum(gx * x, -1, keepdims=True)
        acc[0, gain_row : gain_row + 1, :] += jnp.sum(dn * x * e, 0, keepdims=True)
        return e * gx - (e * e * e) * x * (inner / depth)

    me.greet()
    load_ffn(order[0])
    load_h(order[0])
    load_nf(order[0])
    acc[0] = jnp.zeros(acc.shape[1:], F32)

    def begin(i):
        r = pl.ds(pl.multiple_of(i * small, small), small)
        gr[r, :] = cot[r, :].astype(F32)
        ga0[own_rows(i * small, small), :] = cot[r, :]

    loop(rows // small, begin)
    later = []
    for at, l in enumerate(order):
        last = at == layers - 1
        gather_acts(me, ga0, rows, ags.at[2 * at], agr.at[2 * at], later)
        ready(("wf", l), ("g", l), ("u", l))

        def ffn_back(i):
            r = seq_rows(i)
            gh = dot(ga0[r, :], weight("d", ffn_row), NT)
            g, u = a1[r, :], a2[r, :]
            th = jnp.tanh(0.7978845608028654 * (g + 0.044715 * g * g * g))
            val = 0.5 * g * (1.0 + th)
            slope = 0.5 * (1.0 + th) + 0.5 * g * (1.0 - th * th) * (0.7978845608028654 * (1.0 + 0.134145 * g * g))
            t1[r, :] = (gh * u * slope).astype(BF16)
            t2[r, :] = (gh * val).astype(BF16)

        loop(seqs, ffn_back)

        def ffn_sum(i):
            r = pl.ds(pl.multiple_of(i * 256, 256), 256)
            part[r, :] = (dot(t1[r, :], weight("g", ffn_row)) + dot(t2[r, :], weight("u", ffn_row))).astype(BF16)

        loop(seqs * LEN // 256, ffn_sum)
        load_attn(l)
        ready(("h", l), ("nf", l))

        def fill_d(l=l):
            make(l, "d", a3, ga0)
            load_gt(l)

        def fill_gu(l=l):
            make(l, "g", t1, nb)
            make(l, "u", t2, nb)
            load_n(l)

        def to_mid(r0, n, tot, l=l):
            r = pl.ds(pl.multiple_of(r0, n), n)
            new = gr[r, :] + norm_back(mids[l, r, :], ffn_gain[l : l + 1, :], tot, layers + l)
            gr[r, :] = new
            ga1[own_rows(r0, n), :] = new.astype(BF16)

        sum_acts(me, part, rows, sib_buf, x_buf, z_buf, rss.at[2 * at], rsr.at[2 * at], to_mid, (fill_d, fill_gu))
        mids_of = functools.partial
        gather_acts(
            me, ga1, rows, ags.at[2 * at + 1], agr.at[2 * at + 1],
            (mids_of(combine, l, "d"), mids_of(combine, l, "g")),
        )
        ready(("wa", l), ("s", l), ("m", l), ("q", l), ("k", l), ("v", l), ("p", l))

        def attn_back(i):
            r = seq_rows(i)
            gg = dot(ga1[r, :], weight("o", 0), NT)
            s, mix = a1[r, :], a2[r, :]
            sig = 1.0 / (1.0 + jnp.exp(-s))
            rr = rms(mix, HEAD_FLOOR)
            t2[r, :] = (gg * (mix * rr) * (sig * (1.0 + s * (1.0 - sig)))).astype(BF16)
            gz = gg * (s * sig)
            inner = jnp.sum(gz * mix, -1, keepdims=True) / mix.shape[1]
            gm = (rr * gz - (rr * rr * rr) * mix * inner).astype(BF16)
            raw = (dot(gm, v[r, :], NT) * mask[i]).astype(BF16)
            t1[r, :] = dot(p[i], gm, TN).astype(BF16)
            c, sn = cosine[...], sine[...]
            for dst, grad in ((tq, dot(raw, k[r, :]) * scale), (tk, dot(raw, q[r, :], TN) * scale)):
                half = grad.shape[1] // 2
                g1, g2 = grad[:, :half], grad[:, half:]
                dst[r, :half] = (g1 * c + g2 * sn).astype(BF16)
                dst[r, half:] = (g2 * c - g1 * sn).astype(BF16)

        loop(seqs, attn_back)

        def attn_sum(i):
            r = pl.ds(pl.multiple_of(i * 256, 256), 256)
            tot = dot(tq[r, :], weight("q", 0)) + dot(tk[r, :], weight("k", 0))
            tot = tot + dot(t1[r, :], weight("v", 0)) + dot(t2[r, :], weight("s", 0))
            part[r, :] = tot.astype(BF16)

        loop(seqs * LEN // 256, attn_sum)
        if not last:
            load_ffn(order[at + 1])
        ready(("gt", l), ("n", l))

        def fill_o(l=l):
            combine(l, "u")
            make(l, "o", a3, ga1)
            make(l, "q", tq, nb)

        def fill_kv(l=l, last=last):
            combine(l, "o")
            make(l, "k", tk, nb)
            combine(l, "q")
            make(l, "v", t1, nb)
            make(l, "s", t2, nb)
            if not last:
                load_nf(l - 1)
                load_h(l - 1)

        def to_prev(r0, n, tot, l=l, last=last):
            r = pl.ds(pl.multiple_of(r0, n), n)
            x = tokens[r, :].astype(F32) if l == 0 else x_mid[l - 1, r, :]
            new = gr[r, :] + norm_back(x, attn_gain[l : l + 1, :], tot, l)
            if last:
                input_grad[r, :] = new
            else:
                gr[r, :] = new
                ga0[own_rows(r0, n), :] = new.astype(BF16)

        sum_acts(me, part, rows, sib_buf, x_buf, z_buf, rss.at[2 * at + 1], rsr.at[2 * at + 1], to_prev, (fill_o, fill_kv))
        later = [mids_of(combine, l, "k"), mids_of(combine, l, "v"), mids_of(combine, l, "s")]

    for go in later:
        go()
    partners = [me.sib(), me.xn(), me.yn(), me.znb(), me.at(z=me.zplus(2))]
    for j, dev in enumerate(partners):
        m = remote(acc.at[j], acc_in.at[j], gns.at[j], gnr.at[j], dev)
        m.start()
        m.wait()
        acc[j + 1] = acc[j] + acc_in[j]
    gains[...] = acc[len(partners)]
    for i in range(len(jobs) - SLOTS, len(jobs)):
        retire(i)
    for i in range(len(jobs)):
        for d in (1, 2, 3):
            z_send(i, d).wait_recv()


def run_backward(dims, cot, tokens, x_mid, mids, mask, cosine, sine, attn_gain, ffn_gain, kept):
    layers, rows, lanes, units, scale = dims
    depth = tokens.shape[1]
    total = kept[0].shape[1]
    group = 8 * rows
    seqs = group // LEN
    qk, val, ffn = units["q"][1], units["v"][1], units["g"][1]
    vm = pl.BlockSpec(memory_space=pltpu.VMEM)
    hb = pl.BlockSpec(memory_space=pl.ANY)
    outs = [((rows, depth), F32), ((8, depth), F32), ((layers, 2, 2, total, lanes), BF16)]
    jobs = layers * len(units)
    most = max(n for _, n in units.values())
    attn_rows = units["g"][0]
    dma = pltpu.SemaphoreType.DMA
    big = pltpu.VMEM((group, depth), BF16)
    return pl.pallas_call(
        functools.partial(backward_kernel, dims),
        out_shape=[jax.ShapeDtypeStruct(s, d) for s, d in outs],
        in_specs=[vm] * 9 + [hb] * 13,
        out_specs=[vm] * 2 + [hb],
        scratch_shapes=[
            pltpu.VMEM((rows, depth), F32), big, big, big, big,
            pltpu.VMEM((4, rows, depth), BF16), pltpu.VMEM((2, rows, depth), BF16), pltpu.VMEM((rows, depth), BF16),
            pltpu.VMEM((max(attn_rows, total - attn_rows), depth), BF16),
            pltpu.VMEM((group, val), F32), pltpu.VMEM((group, val), F32), pltpu.VMEM((group, val), BF16),
            pltpu.VMEM((group, qk), BF16), pltpu.VMEM((group, qk), BF16), pltpu.VMEM((group, val), BF16),
            pltpu.VMEM((seqs, LEN, LEN), BF16),
            pltpu.VMEM((group, val), BF16), pltpu.VMEM((group, val), BF16),
            pltpu.VMEM((group, qk), BF16), pltpu.VMEM((group, qk), BF16),
            pltpu.VMEM((SLOTS, most, depth), BF16), pltpu.VMEM((SLOTS, most, depth // 2), BF16),
            pltpu.VMEM((6, 8, depth), F32), pltpu.VMEM((5, 8, depth), F32),
            dma((jobs, 4)), dma((jobs, 4)), dma((jobs, 3)), dma((jobs, 3)), dma((jobs,)),
            dma((2 * layers, 7)), dma((2 * layers, 7)), dma((2 * layers, 7)), dma((2 * layers, 7)),
            dma((16 * layers,)), dma((5,)), dma((5,)), pltpu.SemaphoreType.REGULAR((SLOTS,)),
        ],
        compiler_params=pltpu.CompilerParams(collective_id=1, has_side_effects=True, vmem_limit_bytes=VMEM_LIMIT),
    )(cot, tokens, x_mid, mids, mask, cosine, sine, attn_gain, ffn_gain, *kept)

def rotation(length, width):
    half = width // 2
    place = jnp.arange(length, dtype=F32)
    freqs = 10000.0 ** (-jnp.arange(half, dtype=F32) / half)
    angle = place[:, None] * freqs[None, :]
    return jnp.cos(angle), jnp.sin(angle)


def decay_mask(seg_rows, head, length):
    place = jnp.arange(length, dtype=jnp.int32)
    dist = place[:, None] - place[None, :]
    same = (seg_rows[:, :, None] == seg_rows[:, None, :]) & (dist >= 0)[None]
    rate = jnp.log1p(-(2.0 ** (-5.0 - head)))
    decay = jnp.exp(jnp.maximum(dist, 0).astype(F32) * rate)
    return jnp.where(same, decay[None], 0.0)


def stack_weights(w_query, w_key, w_value, w_swish, w_output, w_gelu, w_up, w_down):
    def cut(w):
        return w.reshape(w.shape[0], 2, w.shape[1] // 2, w.shape[2])

    def turn(w):
        return cut(jnp.swapaxes(w, 1, 2))

    parts = [turn(w_query), turn(w_key), turn(w_value), turn(w_swish), cut(w_output), turn(w_gelu), turn(w_up), cut(w_down)]
    return jnp.concatenate(parts, axis=2)


def setup(segments, w_query, w_value, w_gelu):
    dp, tensor = lax.axis_index("dp"), lax.axis_index("tensor")
    half = (dp // 2) % 2
    other = lax.ppermute(segments, "dp", [(i, i ^ 2) for i in range(8)])
    pair = jnp.where(half == 0, jnp.stack([segments, other]), jnp.stack([other, segments]))
    mask = decay_mask(pair, (tensor * 2 + half).astype(F32), LEN)
    cosine, sine = rotation(LEN, HEAD_QK)
    units, total = unit_rows(w_query.shape[2] // 2, w_value.shape[2] // 2, w_gelu.shape[2] // 2)
    return mask, cosine, sine, units


CONTRACT_ROWS = (((0,), (0,)), ((), ()))
CONTRACT_COLS = (((1,), (1,)), ((), ()))


def shortened(shard):
    return jax.tree.map(lambda a: a.astype(jnp.bfloat16) if a.dtype == jnp.float32 else a, shard)


def norm_rows(values, gain):
    return values * lax.rsqrt(jnp.mean(values * values, -1, keepdims=True) + EPS) * gain


def norm_heads(values):
    return values * lax.rsqrt(jnp.mean(values * values, -1, keepdims=True) + HEAD_FLOOR)


def gelu_tanh(values):
    return jax.nn.gelu(values, approximate=True)


def plain_rotation(length, width):
    half = width // 2
    place = jnp.arange(length, dtype=jnp.float32)
    freqs = 10000.0 ** (-jnp.arange(half, dtype=jnp.float32) / half)
    angle = place[:, None] * freqs[None, :]
    return (jnp.cos(angle)[:, None, :], jnp.sin(angle)[:, None, :])


def rotate(values, cosine, sine):
    half = values.shape[-1] // 2
    first = values[..., :half]
    second = values[..., half:]
    return jnp.concatenate([first * cosine - second * sine, second * cosine + first * sine], -1)


def rotate_back(grads, cosine, sine):
    half = grads.shape[-1] // 2
    first = grads[..., :half]
    second = grads[..., half:]
    return jnp.concatenate([first * cosine + second * sine, second * cosine - first * sine], -1)


def plain_mask(seg_rows, head_ids, length):
    place = jnp.arange(length, dtype=jnp.int32)
    dist = place[:, None] - place[None, :]
    same = (seg_rows[:, :, None] == seg_rows[:, None, :]) & (dist >= 0)[None]
    rates = jnp.log1p(-(2.0 ** (-5.0 - head_ids)))
    decay = jnp.exp(jnp.maximum(dist, 0).astype(jnp.float32)[None] * rates[:, None, None])
    return jnp.where(same[:, None], decay[None], 0.0)


def weights_of(rotated_query, rotated_key, mask, score_scale):
    unnormalized_scores = (
        jnp.einsum(
            "slhd,smhd->shlm", rotated_query, rotated_key, preferred_element_type=jnp.float32
        )
        * score_scale
    )
    return (unnormalized_scores * mask).astype(jnp.bfloat16)


def gather_rows(rows):
    return lax.all_gather(rows, "tensor", axis=0, tiled=True)


def sum_rows(part):
    return lax.psum_scatter(
        part.astype(jnp.bfloat16), "tensor", scatter_dimension=0, tiled=True
    ).astype(jnp.float32)


def fold_rows(acts, weights):
    pieces = jax.tree.map(lambda a: lax.all_gather(a, "dp", axis=0, tiled=True), shortened(weights))
    return tuple((jnp.dot(acts, p, preferred_element_type=jnp.float32) for p in pieces))


def map_columns(acts, weight):
    return jnp.dot(
        acts, lax.all_gather(weight, "dp", axis=1, tiled=True), preferred_element_type=jnp.float32
    )


def back_rows(grads, weights):
    pieces = lax.all_gather(shortened(weights), "dp", axis=0, tiled=True)
    total = lax.dot_general(grads[0], pieces[0], CONTRACT_COLS, preferred_element_type=jnp.float32)
    for grad, piece in zip(grads[1:], pieces[1:]):
        total = total + lax.dot_general(
            grad, piece, CONTRACT_COLS, preferred_element_type=jnp.float32
        )
    return total


def back_columns(grad, weight):
    return lax.dot_general(
        grad,
        lax.all_gather(weight, "dp", axis=1, tiled=True),
        CONTRACT_COLS,
        preferred_element_type=jnp.float32,
    )


def plain(
    tokens,
    segments,
    attn_gain,
    w_query,
    w_key,
    w_value,
    w_swish,
    w_output,
    ffn_gain,
    w_gelu,
    w_up,
    w_down,
    cotangent,
):
    layers = w_query.shape[0]
    heads_dev = w_query.shape[2] // HEAD_QK
    seqs = segments.shape[0] // LEN
    score_scale = HEAD_QK ** (-0.5)
    head_ids = (lax.axis_index("tensor") * heads_dev + jnp.arange(heads_dev)).astype(jnp.float32)
    mask = plain_mask(segments.reshape(seqs, LEN), head_ids, LEN)
    cosine, sine = plain_rotation(LEN, HEAD_QK)
    residual = tokens.astype(jnp.float32)
    saved = []
    for layer in range(layers):
        attn_in = (w_query[layer], w_key[layer], w_value[layer], w_swish[layer])
        ffn_in = (w_gelu[layer], w_up[layer])
        whole_in = attn_in + ffn_in
        whole_out = (w_output[layer], w_down[layer])
        normed = gather_rows(norm_rows(residual, attn_gain[layer]).astype(jnp.bfloat16))
        rows_all = normed.shape[0]
        query, keys, values, swish = fold_rows(normed, attn_in)
        vals = values.astype(jnp.bfloat16).reshape(seqs, LEN, heads_dev, HEAD_V)
        rotated_query = rotate(query.reshape(seqs, LEN, heads_dev, HEAD_QK), cosine, sine).astype(
            jnp.bfloat16
        )
        rotated_key = rotate(keys.reshape(seqs, LEN, heads_dev, HEAD_QK), cosine, sine).astype(
            jnp.bfloat16
        )
        probs = weights_of(rotated_query, rotated_key, mask, score_scale)
        mixed = jnp.einsum("shlm,smhv->slhv", probs, vals, preferred_element_type=jnp.float32)
        zed = norm_heads(mixed).reshape(rows_all, -1)
        gated = (jax.nn.silu(swish) * zed).astype(jnp.bfloat16)
        branch = map_columns(gated, w_output[layer])
        mid = residual + sum_rows(branch)
        normed_ffn = gather_rows(norm_rows(mid, ffn_gain[layer]).astype(jnp.bfloat16))
        gate_pre, up_pre = fold_rows(normed_ffn, ffn_in)
        hidden = (gelu_tanh(gate_pre) * up_pre).astype(jnp.bfloat16)
        branch_ffn = map_columns(hidden, w_down[layer])
        saved.append(
            (
                residual,
                normed,
                rotated_query,
                rotated_key,
                vals,
                swish,
                mixed,
                zed,
                gated,
                mid,
                normed_ffn,
                gate_pre,
                up_pre,
                hidden,
                whole_in,
                whole_out,
            )
        )
        residual = mid + sum_rows(branch_ffn)
    output = residual.astype(jnp.bfloat16)
    grad_res = cotangent.astype(jnp.float32)
    weight_parts = [None] * layers
    attn_gain_parts = [None] * layers
    ffn_gain_parts = [None] * layers
    for layer in reversed(range(layers)):
        (
            x_in,
            normed,
            rotated_query,
            rotated_key,
            vals,
            swish,
            mixed,
            zed,
            gated,
            mid,
            normed_ffn,
            gate_pre,
            up_pre,
            hidden,
            whole_in,
            whole_out,
        ) = saved[layer]
        attn_in = (w_query[layer], w_key[layer], w_value[layer], w_swish[layer])
        ffn_in = (w_gelu[layer], w_up[layer])
        rows_all = normed.shape[0]
        grad_c = gather_rows(grad_res.astype(jnp.bfloat16))
        down_grad = lax.dot_general(
            grad_c, hidden, CONTRACT_ROWS, preferred_element_type=jnp.float32
        )
        grad_hidden = back_columns(grad_c, w_down[layer])
        gelu_val, gelu_activation = jax.vjp(gelu_tanh, gate_pre)
        grad_gate = gelu_activation(grad_hidden * up_pre)[0].astype(jnp.bfloat16)
        grad_upv = (grad_hidden * gelu_val).astype(jnp.bfloat16)
        gelu_grad = lax.dot_general(
            normed_ffn, grad_gate, CONTRACT_ROWS, preferred_element_type=jnp.float32
        )
        up_grad = lax.dot_general(
            normed_ffn, grad_upv, CONTRACT_ROWS, preferred_element_type=jnp.float32
        )
        grad_nf = back_rows((grad_gate, grad_upv), ffn_in)
        _, ffn_norm_fn = jax.vjp(norm_rows, mid, ffn_gain[layer])
        grad_mid_norm, ffn_gain_parts[layer] = ffn_norm_fn(sum_rows(grad_nf))
        grad_mid = grad_res + grad_mid_norm
        grad_b = gather_rows(grad_mid.astype(jnp.bfloat16))
        output_grad_t = lax.dot_general(
            grad_b, gated, CONTRACT_ROWS, preferred_element_type=jnp.float32
        )
        grad_gated = back_columns(grad_b, w_output[layer])
        swish_output, swish_fn = jax.vjp(jax.nn.silu, swish)
        grad_sw = swish_fn(grad_gated * zed)[0].astype(jnp.bfloat16)
        grad_zed = grad_gated * swish_output
        _, head_fn = jax.vjp(norm_heads, mixed)
        grad_mixed = head_fn(grad_zed.reshape(mixed.shape))[0].astype(jnp.bfloat16)
        probs = weights_of(rotated_query, rotated_key, mask, score_scale)
        grad_probs = jnp.einsum(
            "slhv,smhv->shlm", grad_mixed, vals, preferred_element_type=jnp.float32
        )
        grad_raw = (grad_probs * mask).astype(jnp.bfloat16)
        grad_vals = jnp.einsum(
            "shlm,slhv->smhv", probs, grad_mixed, preferred_element_type=jnp.float32
        )
        grad_vals = grad_vals.astype(jnp.bfloat16).reshape(rows_all, -1)
        grad_qrot = (
            jnp.einsum("shlm,smhd->slhd", grad_raw, rotated_key, preferred_element_type=jnp.float32)
            * score_scale
        )
        grad_krot = (
            jnp.einsum(
                "shlm,slhd->smhd", grad_raw, rotated_query, preferred_element_type=jnp.float32
            )
            * score_scale
        )
        grad_q = rotate_back(grad_qrot, cosine, sine).astype(jnp.bfloat16).reshape(rows_all, -1)
        grad_k = rotate_back(grad_krot, cosine, sine).astype(jnp.bfloat16).reshape(rows_all, -1)
        attn_grads = tuple(
            (
                lax.dot_general(normed, g, CONTRACT_ROWS, preferred_element_type=jnp.float32)
                for g in (grad_q, grad_k, grad_vals, grad_sw)
            )
        )
        grad_n = back_rows((grad_q, grad_k, grad_vals, grad_sw), attn_in)
        _, attn_norm_fn = jax.vjp(norm_rows, x_in, attn_gain[layer])
        grad_x_norm, attn_gain_parts[layer] = attn_norm_fn(sum_rows(grad_n))
        grad_res = grad_mid + grad_x_norm
        weight_parts[layer] = jax.tree.map(
            lambda part: part.astype(jnp.float32),
            lax.psum_scatter(
                shortened(attn_grads + (output_grad_t, gelu_grad, up_grad, down_grad)),
                "dp",
                scatter_dimension=0,
                tiled=True,
            ),
        )
    attn_gain_grad, ffn_gain_grad = lax.psum(
        (jnp.stack(attn_gain_parts), jnp.stack(ffn_gain_parts)), ("dp", "tensor")
    )
    grad_query = jnp.stack([p[0] for p in weight_parts])
    grad_key = jnp.stack([p[1] for p in weight_parts])
    grad_value = jnp.stack([p[2] for p in weight_parts])
    grad_swish = jnp.stack([p[3] for p in weight_parts])
    grad_output = jnp.stack([p[4].T for p in weight_parts])
    grad_gelu = jnp.stack([p[5] for p in weight_parts])
    grad_up = jnp.stack([p[6] for p in weight_parts])
    grad_down = jnp.stack([p[7].T for p in weight_parts])
    return (
        output,
        grad_res,
        attn_gain_grad,
        grad_query,
        grad_key,
        grad_value,
        grad_swish,
        grad_output,
        ffn_gain_grad,
        grad_gelu,
        grad_up,
        grad_down,
    )


def grouped(
    tokens, segments, attn_gain, w_query, w_key, w_value, w_swish, w_output, ffn_gain, w_gelu, w_up, w_down, cotangent
):
    layers = w_query.shape[0]
    mask, cosine, sine, units = setup(segments, w_query, w_value, w_gelu)
    wl = stack_weights(w_query, w_key, w_value, w_swish, w_output, w_gelu, w_up, w_down)
    dims = (layers, tokens.shape[0], w_query.shape[1], units, HEAD_QK ** (-0.5))
    output, x_mid, mids, *kept = run_forward(dims, tokens, mask, cosine, sine, attn_gain, ffn_gain, wl)
    input_grad, gains, rz = run_backward(
        dims, cotangent, tokens, x_mid, mids, mask, cosine, sine, attn_gain, ffn_gain, kept
    )
    sums = rz[:, :, 0].astype(F32) + rz[:, :, 1].astype(F32)

    def piece(name):
        r0, n = units[name]
        part = sums[:, :, r0 : r0 + n]
        return part.reshape(layers, 2 * n, part.shape[3])

    def turned(name):
        return jnp.swapaxes(piece(name), 1, 2)

    return (
        output, input_grad, gains[:layers], turned("q"), turned("k"), turned("v"), turned("s"), piece("o"),
        gains[layers : 2 * layers], turned("g"), turned("u"), piece("d"),
    )


def solution(mesh):
    rows = P(("dp", "tensor"), None)
    up, down = P(None, "dp", "tensor"), P(None, "tensor", "dp")
    in_specs = (rows, P("dp"), P(), up, up, up, up, down, P(), up, up, down, rows)
    out_specs = (rows, rows, P(), up, up, up, up, down, P(), up, up, down)
    step = grouped if (mesh.shape["dp"], mesh.shape["tensor"]) == (8, 4) else plain
    return jax.shard_map(step, mesh=mesh, in_specs=in_specs, out_specs=out_specs, check_vma=False)
```

```python
import functools

import jax
import jax.numpy as jnp
from jax import lax
from jax.experimental import pallas as pl
from jax.experimental.pallas import tpu as pltpu
from jax.sharding import PartitionSpec as P

HEAD_QK = 256
HEAD_V = 432
LEN = 512

EPS = 1e-06
HEAD_FLOOR = 1.0
NN = (((1,), (0,)), ((), ()))
NT = (((1,), (1,)), ((), ()))
TN = (((0,), (0,)), ((), ()))
MESH = pl.DeviceIdType.MESH
BF16 = jnp.bfloat16
F32 = jnp.float32
LOOK = 2
SCHED = (
    ("IIPI", "PI", "", "PI", "PI", ""),
    ("PI", "PI", "", "PI", "PI", ""),
    ("PI", "PI", "", "PI", "PI", ""),
    ("PI", "PI", "", "PI", "PI", ""),
)
VMEM_LIMIT = 60 * 1024 * 1024


def dot(a, b, dims=NN):
    return lax.dot_general(a, b, dims, preferred_element_type=F32)


def loop(steps, body):
    lax.fori_loop(0, steps, lambda i, c: (body(i), c)[1], 0)


class Place:
    def __init__(self):
        dp, tensor = lax.axis_index("dp"), lax.axis_index("tensor")
        self.dp, self.tensor = dp, tensor
        self.z, self.y = lax.div(dp, 2), lax.rem(dp, 2)
        self.x, self.c = lax.div(tensor, 2), lax.rem(tensor, 2)
        self.half = lax.rem(self.z, 2)
        self.zn = self.z + 1 - 2 * self.half

    def at(self, z=None, y=None, x=None, c=None):
        z = self.z if z is None else z
        y = self.y if y is None else y
        x = self.x if x is None else x
        c = self.c if c is None else c
        return (z * 2 + y, x * 2 + c)

    def zplus(self, d):
        return lax.rem(self.z + d + 4, 4)

    def sib(self):
        return self.at(c=1 - self.c)

    def xn(self):
        return self.at(x=1 - self.x)

    def yn(self):
        return self.at(y=1 - self.y)

    def znb(self):
        return self.at(z=self.zn)

    def peers(self):
        return [self.sib(), self.xn(), self.yn()] + [self.at(z=self.zplus(d)) for d in (1, 2, 3)]

    def greet(self):
        bar = pltpu.get_barrier_semaphore()
        peers = self.peers()
        for p in peers:
            pl.semaphore_signal(bar, inc=1, device_id=p, device_id_type=MESH)
        pl.semaphore_wait(bar, len(peers))


def remote(src, dst, ssem, rsem, dev):
    return pltpu.make_async_remote_copy(
        src_ref=src, dst_ref=dst, send_sem=ssem, recv_sem=rsem, device_id=dev, device_id_type=MESH
    )


def block(half, tensor, rows):
    return pl.ds(pl.multiple_of((half * 4 + tensor) * rows, rows), rows)


def gather_acts(me, buf, rows, ssem, rsem, first, second, fill=()):
    fill = list(fill)

    def step():
        if fill:
            fill.pop(0)()

    def move(k, half, x, dev):
        r = block(half, x * 2 + me.c, rows)
        return remote(buf.at[r], buf.at[r], ssem.at[k], rsem.at[k], dev)

    h, x = me.half, me.x
    own_z = move(1, h, x, me.znb())
    own_x = move(0, h, x, me.xn())
    own_s = move(2, h, x, me.sib())
    own_z.start()
    own_x.start()
    own_s.start()
    step()
    own_x.wait_recv()
    x_s = move(5, h, 1 - x, me.sib())
    x_s.start()
    own_z.wait_recv()
    z_x = move(3, 1 - h, x, me.xn())
    z_s = move(4, 1 - h, x, me.sib())
    z_x.start()
    z_s.start()
    step()
    own_s.wait_recv()
    x_s.wait_recv()
    first(h)
    z_x.wait_recv()
    g_s = move(6, 1 - h, 1 - x, me.sib())
    g_s.start()
    step()
    z_s.wait_recv()
    g_s.wait_recv()
    second(1 - h)
    for m in (own_x, own_z, own_s, z_x, z_s, x_s, g_s):
        m.wait_send()
    while fill:
        step()


def sum_acts(me, part, rows, sib_buf, x_buf, z_buf, ssem, rsem, body, fill=()):
    fill = list(fill)

    def step():
        if fill:
            fill.pop(0)()

    h, x = me.half, me.x
    order = [(1 - h, 1 - x), (h, 1 - x), (1 - h, x), (h, x)]
    sibs = []
    for j, (hh, xx) in enumerate(order):
        m = remote(part.at[block(hh, xx * 2 + 1 - me.c, rows)], sib_buf.at[j], ssem.at[j], rsem.at[j], me.sib())
        m.start()
        sibs.append(m)
    step()
    chunk = 64

    def mine(j, i):
        hh, xx = order[j]
        return pl.ds(pl.multiple_of((hh * 4 + xx * 2 + me.c) * rows + i * chunk, chunk), chunk)

    def add(j, extra=None):
        def go(i):
            r = mine(j, i)
            k = pl.ds(pl.multiple_of(i * chunk, chunk), chunk)
            v = part[r, :].astype(F32) + sib_buf[j, k, :].astype(F32)
            if extra is not None:
                v = v + extra[k, :].astype(F32)
            part[r, :] = v.astype(BF16)

        loop(rows // chunk, go)

    def my_block(j):
        hh, xx = order[j]
        return part.at[block(hh, xx * 2 + me.c, rows)]

    to_x = []
    for j in (0, 1):
        sibs[j].wait_recv()
        add(j)
        m = remote(my_block(j), x_buf.at[j], ssem.at[4 + j], rsem.at[4 + j], me.xn())
        m.start()
        to_x.append(m)
    step()
    sibs[2].wait_recv()
    to_x[0].wait_recv()
    add(2, x_buf.at[0])
    to_z = remote(my_block(2), z_buf, ssem.at[6], rsem.at[6], me.znb())
    to_z.start()
    sibs[3].wait_recv()
    step()
    to_x[1].wait_recv()
    to_z.wait_recv()
    small = 32

    def last(i):
        k = pl.ds(pl.multiple_of(i * small, small), small)
        r = pl.ds(pl.multiple_of((h * 4 + x * 2 + me.c) * rows + i * small, small), small)
        v = part[r, :].astype(F32) + sib_buf[3, k, :].astype(F32)
        v = v + x_buf[1, k, :].astype(F32) + z_buf[k, :].astype(F32)
        body(i * small, small, v)

    loop(rows // small, last)
    for m in sibs + to_x + [to_z]:
        m.wait_send()
    while fill:
        step()


def unit_rows(qk, val, ffn):
    sizes = (("q", qk), ("k", qk), ("v", val), ("s", val), ("o", val), ("g", ffn), ("u", ffn), ("d", ffn))
    out, at = {}, 0
    for name, n in sizes:
        out[name] = (at, n)
        at += n
    return out, at


def rms(v, floor):
    return lax.rsqrt(jnp.mean(v * v, -1, keepdims=True) + floor)


def forward_kernel(
    dims,
    tokens, mask, cosine, sine, attn_gain, ffn_gain, w_q, w_k, w_v, w_s, w_o, w_g, w_u, w_d,
    output, x_mid, mids, wf, s_n, s_nf, s_q, s_k, s_v, s_s, s_m, s_gt, s_g, s_u, s_h, s_p,
    W, N0, N1, part, sib_buf, x_buf, z_buf, q, k, v, s, m, gt, g, u, h, p,
    zs, zr, ys, yr, lo, ld, ags, agr, rss, rsr, sv,
):
    layers, rows, lanes, units, scale = dims
    me = Place()
    names = list(units)
    shards = dict(q=w_q, k=w_k, v=w_v, s=w_s, o=w_o, g=w_g, u=w_u, d=w_d)
    groups = [(l, units[n]) for l in range(layers) for n in names]
    spot = {(l, n): l * len(names) + i for l in range(layers) for i, n in enumerate(names)}
    my_lane = pl.multiple_of(me.dp * lanes, lanes)

    def shard(i, half):
        n = groups[i][1][1]
        return shards[names[i % len(names)]].at[groups[i][0], pl.ds(pl.multiple_of(half * n, 16), n)]

    def z_copy(i, d):
        l, (r0, n) = groups[i]
        tz = me.zplus(d)
        return remote(
            shard(i, lax.rem(tz, 2)), wf.at[l, pl.ds(r0, n), pl.ds(my_lane, lanes)],
            zs.at[i, d - 1], zr.at[i, d - 1], me.at(z=tz),
        )

    def y_copy(i, d):
        l, (r0, n) = groups[i]
        lane = pl.ds(pl.multiple_of((me.zplus(-d) * 2 + me.y) * lanes, lanes), lanes)
        dst = wf.at[l, pl.ds(r0, n), lane]
        src = shard(i, me.half) if d == 0 else dst
        return remote(src, dst, ys.at[i, d], yr.at[i, d], me.yn())

    def local_copy(i):
        l, (r0, n) = groups[i]
        return pltpu.make_async_copy(
            shard(i, me.half), wf.at[l, pl.ds(r0, n), pl.ds(my_lane, lanes)], lo.at[i]
        )

    def issue(i):
        if i < len(groups):
            for d in (1, 2, 3):
                z_copy(i, d).start()
            y_copy(i, 0).start()
            local_copy(i).start()

    issued, pumped = [0], [0]

    def send_next():
        if issued[0] < len(groups):
            issue(issued[0])
            issued[0] += 1

    def pass_on():
        i = pumped[0]
        if i >= len(groups):
            return
        while issued[0] <= i:
            send_next()
        pumped[0] += 1
        for d in (1, 3, 2):
            z_copy(i, d).wait_recv()
            y_copy(i, d).start()

    plan = SCHED

    def act(pair, point):
        def go():
            for ch in plan[pair][point]:
                if ch == "I":
                    send_next()
                if ch == "P":
                    pass_on()
        return go

    def gfill(pair):
        return [act(pair, 0), act(pair, 1), act(pair, 5)]

    def sfill(pair):
        return [act(pair, 2), act(pair, 3), act(pair, 4)]

    def take(l, *wanted):
        idx = [spot[l, n] for n in wanted]
        while pumped[0] <= idx[-1]:
            pass_on()
            while issued[0] - pumped[0] < LOOK:
                if issued[0] >= len(groups):
                    break
                send_next()
        copies = []
        for i in idx:
            for d in range(4):
                y_copy(i, d).wait_recv()
            local_copy(i).wait()
            r0, n = groups[i][1]
            c = pltpu.make_async_copy(wf.at[l, pl.ds(r0, n)], W.at[pl.ds(r0, n)], ld.at[i])
            c.start()
            copies.append(c)
        for c in copies:
            c.wait()

    saves = []

    def save(src, dst):
        c = pltpu.make_async_copy(src, dst, sv.at[len(saves)])
        c.start()
        saves.append(c)

    waited = [0]

    def settle():
        while waited[0] < len(saves):
            saves[waited[0]].wait()
            waited[0] += 1

    def weight(n):
        r0, size = units[n]
        return W[pl.ds(r0, size), :]

    def seq_rows(i):
        return pl.ds(pl.multiple_of(i * LEN, LEN), LEN)

    seqs = 2
    own = (me.half * 4 + me.tensor) * rows

    def own_rows(r0, n):
        return pl.ds(pl.multiple_of(own + r0, n), n)

    me.greet()
    small = 32

    def first_norm(i):
        r = pl.ds(pl.multiple_of(i * small, small), small)
        x = tokens[r, :].astype(F32)
        N0[own_rows(i * small, small), :] = (x * rms(x, EPS) * attn_gain[0:1, :]).astype(BF16)

    loop(rows // small, first_norm)

    def out_rows(i, src, name):
        def go(j):
            r = pl.ds(pl.multiple_of(i * LEN + j * 256, 256), 256)
            part[r, :] = dot(src[r, :], weight(name)).astype(BF16)

        loop(LEN // 256, go)

    def attn_seq(i, l, fetch):
        def get(name):
            if fetch:
                take(l, name)

        r = seq_rows(i)
        for name, dst in (("q", q), ("k", k)):
            get(name)
            t = dot(N0[r, :], weight(name), NT)
            half = t.shape[1] // 2
            t1, t2 = t[:, :half], t[:, half:]
            c, sn = cosine[...], sine[...]
            dst[r, :half] = (t1 * c - t2 * sn).astype(BF16)
            dst[r, half:] = (t2 * c + t1 * sn).astype(BF16)
        get("v")
        v[r, :] = dot(N0[r, :], weight("v"), NT).astype(BF16)
        raw = dot(q[r, :], k[r, :], NT) * scale
        probs = (raw * mask[i]).astype(BF16)
        p[i] = probs
        m[r, :] = dot(probs, v[r, :])
        get("s")
        t = dot(N0[r, :], weight("s"), NT)
        s[r, :] = t
        mix = m[r, :]
        gt[r, :] = (jax.nn.silu(t) * (mix * rms(mix, HEAD_FLOOR))).astype(BF16)
        get("o")
        out_rows(i, gt, "o")

    def ffn_seq(i, l, fetch):
        r = seq_rows(i)
        if fetch:
            take(l, "g")
        g[r, :] = dot(N1[r, :], weight("g"), NT)
        if fetch:
            take(l, "u")
        t = dot(N1[r, :], weight("u"), NT)
        u[r, :] = t
        h[r, :] = (jax.nn.gelu(g[r, :], approximate=True) * t).astype(BF16)
        if fetch:
            take(l, "d")
        out_rows(i, h, "d")

    both = lambda body, l: (functools.partial(body, l=l, fetch=True), functools.partial(body, l=l, fetch=False))

    for l in range(layers):
        gather_acts(me, N0, rows, ags.at[2 * l], agr.at[2 * l], *both(attn_seq, l), gfill(2 * l))
        for src, dst in ((N0, s_n), (q, s_q), (k, s_k), (v, s_v), (p, s_p), (m, s_m), (s, s_s), (gt, s_gt)):
            save(src, dst.at[l])

        def to_mid(r0, n, total, l=l):
            r = pl.ds(pl.multiple_of(r0, n), n)
            x = (tokens[r, :].astype(F32) if l == 0 else x_mid[l - 1, r, :]) + total
            mids[l, r, :] = x
            N1[own_rows(r0, n), :] = (x * rms(x, EPS) * ffn_gain[l : l + 1, :]).astype(BF16)

        sum_acts(me, part, rows, sib_buf, x_buf, z_buf, rss.at[2 * l], rsr.at[2 * l], to_mid, sfill(2 * l))
        gather_acts(me, N1, rows, ags.at[2 * l + 1], agr.at[2 * l + 1], *both(ffn_seq, l), gfill(2 * l + 1))
        for src, dst in ((N1, s_nf), (g, s_g), (u, s_u), (h, s_h)):
            save(src, dst.at[l])

        def to_next(r0, n, total, l=l):
            r = pl.ds(pl.multiple_of(r0, n), n)
            x = mids[l, r, :] + total
            if l + 1 < layers:
                x_mid[l, r, :] = x
                N0[own_rows(r0, n), :] = (x * rms(x, EPS) * attn_gain[l + 1 : l + 2, :]).astype(BF16)
            else:
                output[r, :] = x.astype(BF16)

        settle()
        sum_acts(me, part, rows, sib_buf, x_buf, z_buf, rss.at[2 * l + 1], rsr.at[2 * l + 1], to_next, sfill(2 * l + 1))
    settle()
    for i in range(len(groups)):
        for d in (1, 2, 3):
            z_copy(i, d).wait_send()
        for d in range(4):
            y_copy(i, d).wait_send()


def run_forward(dims, total, tokens, mask, cosine, sine, attn_gain, ffn_gain, weights):
    layers, rows, lanes, units, scale = dims
    depth = tokens.shape[1]
    group = 8 * rows
    seqs = group // LEN
    qk, val, ffn = units["q"][1], units["v"][1], units["g"][1]
    vm = pl.BlockSpec(memory_space=pltpu.VMEM)
    hb = pl.BlockSpec(memory_space=pl.ANY)
    outs = [
        ((rows, depth), BF16), ((layers - 1, rows, depth), F32), ((layers, rows, depth), F32),
        ((layers, total, depth), BF16), ((layers, group, depth), BF16), ((layers, group, depth), BF16),
        ((layers, group, qk), BF16), ((layers, group, qk), BF16), ((layers, group, val), BF16),
        ((layers, group, val), F32), ((layers, group, val), F32), ((layers, group, val), BF16),
        ((layers, group, ffn), F32), ((layers, group, ffn), F32), ((layers, group, ffn), BF16),
        ((layers, seqs, LEN, LEN), BF16),
    ]
    n_groups = layers * len(units)
    dma = pltpu.SemaphoreType.DMA
    return pl.pallas_call(
        functools.partial(forward_kernel, dims),
        out_shape=[jax.ShapeDtypeStruct(s, d) for s, d in outs],
        in_specs=[vm] * 6 + [hb] * 8,
        out_specs=[vm] * 3 + [hb] * 13,
        scratch_shapes=[
            pltpu.VMEM((total, depth), BF16),
            pltpu.VMEM((group, depth), BF16), pltpu.VMEM((group, depth), BF16), pltpu.VMEM((group, depth), BF16),
            pltpu.VMEM((4, rows, depth), BF16), pltpu.VMEM((2, rows, depth), BF16), pltpu.VMEM((rows, depth), BF16),
            pltpu.VMEM((group, qk), BF16), pltpu.VMEM((group, qk), BF16), pltpu.VMEM((group, val), BF16),
            pltpu.VMEM((group, val), F32), pltpu.VMEM((group, val), F32), pltpu.VMEM((group, val), BF16),
            pltpu.VMEM((group, ffn), F32), pltpu.VMEM((group, ffn), F32), pltpu.VMEM((group, ffn), BF16),
            pltpu.VMEM((seqs, LEN, LEN), BF16),
            dma((n_groups, 3)), dma((n_groups, 3)), dma((n_groups, 4)), dma((n_groups, 4)),
            dma((n_groups,)), dma((n_groups,)),
            dma((2 * layers, 7)), dma((2 * layers, 7)), dma((2 * layers, 7)), dma((2 * layers, 7)),
            dma((12 * layers,)),
        ],
        compiler_params=pltpu.CompilerParams(collective_id=0, has_side_effects=True, vmem_limit_bytes=VMEM_LIMIT),
    )(tokens, mask, cosine, sine, attn_gain, ffn_gain, *weights)


SLOTS = 4
BSCHED = (
    ("", "", "", "", "M", "MM", ""),
    ("C", "C", "", "", "CMM", "CMCMM", ""),
    ("C", "C", "C", "", "M", "MM", ""),
    ("C", "C", "", "", "CMM", "CMCMM", ""),
)


def backward_kernel(
    dims,
    cot, tokens, x_mid, mids, mask, cosine, sine, attn_gain, ffn_gain,
    wf, s_n, s_nf, s_q, s_k, s_v, s_s, s_m, s_gt, s_g, s_u, s_h, s_p,
    input_grad, gains, rz,
    gr, xb, nb, ga0, ga1, part, sib_buf, x_buf, z_buf, W, a1, a2, a3, q, k, v, p, t1, t2, tq, tk, G, ry, acc, acc_in,
    ys, yr, zs, zr, os, ags, agr, rss, rsr, ld, gns, gnr, credit,
):
    layers, rows, lanes, units, scale = dims
    me = Place()
    depth = cot.shape[1]
    wide = 512
    small = 32
    seqs = 2
    order = list(reversed(range(layers)))
    jobs = [(l, n) for l in order for n in ("d", "g", "u", "o", "q", "k", "v", "s")]
    index = {job: i for i, job in enumerate(jobs)}
    own = (me.half * 4 + me.tensor) * rows
    ffn_row = units["g"][0]
    attn_end = ffn_row
    total_rows = units["d"][0] + units["d"][1]

    def own_rows(r0, n):
        return pl.ds(pl.multiple_of(own + r0, n), n)

    def seq_rows(i):
        return pl.ds(pl.multiple_of(i * LEN, LEN), LEN)

    def lane(i):
        return pl.ds(pl.multiple_of(i * lanes, lanes), lanes)

    def y_send(i, d):
        n = units[jobs[i][1]][1]
        tz = me.zplus(d)
        return remote(
            G.at[i % SLOTS, pl.ds(0, n), lane(tz * 2 + 1 - me.y)], ry.at[i % SLOTS, pl.ds(0, n), lane(tz)],
            ys.at[i, d], yr.at[i, d], me.yn(),
        )

    def z_send(i, d):
        l, name = jobs[i]
        r0, n = units[name]
        tz = me.zplus(d)
        return remote(
            G.at[i % SLOTS, pl.ds(0, n), lane(tz * 2 + me.y)], rz.at[l, me.half, d // 2, pl.ds(r0, n)],
            zs.at[i, d - 1], zr.at[i, d - 1], me.at(z=tz),
        )

    def own_copy(i):
        l, name = jobs[i]
        r0, n = units[name]
        return pltpu.make_async_copy(
            G.at[i % SLOTS, pl.ds(0, n), lane(me.dp)], rz.at[l, me.half, 0, pl.ds(r0, n)], os.at[i]
        )

    def retire(i):
        for d in range(4):
            y_send(i, d).wait_send()
        for d in (1, 2, 3):
            z_send(i, d).wait_send()
        own_copy(i).wait()

    def make(l, name, left, right):
        i = index[l, name]
        n = units[name][1]
        if i >= SLOTS:
            retire(i - SLOTS)

        def go(j):
            cols = pl.ds(pl.multiple_of(j * wide, wide), wide)
            G[i % SLOTS, :n, cols] = dot(left[...], right[:, cols], TN).astype(BF16)

        loop(depth // wide, go)
        if i >= SLOTS:
            pl.semaphore_wait(credit.at[i % SLOTS], 1)
        for d in (2, 1, 3, 0):
            y_send(i, d).start()

    def combine(l, name):
        i = index[l, name]
        n = units[name][1]
        for d in (2, 1, 3, 0):
            y_send(i, d).wait_recv()
            tz = me.zplus(d)

            def add(j, tz=tz):
                r = pl.ds(pl.multiple_of(j * 16, 16), 16)
                c = lane(tz * 2 + me.y)
                both = G[i % SLOTS, r, c].astype(F32) + ry[i % SLOTS, r, lane(tz)].astype(F32)
                G[i % SLOTS, r, c] = both.astype(BF16)

            loop(n // 16, add)
            if d:
                z_send(i, d).start()
            else:
                own_copy(i).start()
        if i + SLOTS < len(jobs):
            pl.semaphore_signal(credit.at[i % SLOTS], inc=1, device_id=me.yn(), device_id_type=MESH)

    spots = {}

    def load(key, src, dst):
        c = pltpu.make_async_copy(src, dst, ld.at[len(spots)])
        c.start()
        spots[key] = c

    def ready(*keys):
        for key in keys:
            spots[key].wait()

    def load_ffn(l):
        load(("wf", l), wf.at[l, pl.ds(ffn_row, total_rows - ffn_row)], W.at[pl.ds(0, total_rows - ffn_row)])
        load(("g", l), s_g.at[l], a1)
        load(("u", l), s_u.at[l], a2)

    def load_attn(l):
        load(("wa", l), wf.at[l, pl.ds(0, attn_end)], W.at[pl.ds(0, attn_end)])
        load(("s", l), s_s.at[l], a1)
        load(("m", l), s_m.at[l], a2)
        load(("q", l), s_q.at[l], q)
        load(("k", l), s_k.at[l], k)
        load(("v", l), s_v.at[l], v)
        load(("p", l), s_p.at[l], p)

    def load_mid(l):
        load(("mid", l), mids.at[l], xb)

    def load_h(l):
        load(("h", l), s_h.at[l], a3)

    def load_nf(l):
        load(("nf", l), s_nf.at[l], nb)

    def load_gt(l):
        load(("gt", l), s_gt.at[l], a3)

    def load_n(l):
        load(("n", l), s_n.at[l], nb)

    def weight(name, base):
        r0, n = units[name]
        return W[pl.ds(r0 - base, n), :]

    def norm_back(x, gain, dn, gain_row):
        e = rms(x, EPS)
        gx = dn * gain
        inner = jnp.sum(gx * x, -1, keepdims=True)
        acc[0, gain_row : gain_row + 1, :] += jnp.sum(dn * x * e, 0, keepdims=True)
        return e * gx - (e * e * e) * x * (inner / depth)

    me.greet()
    load_ffn(order[0])
    load_mid(order[0])
    load_h(order[0])
    load_nf(order[0])
    acc[0] = jnp.zeros(acc.shape[1:], F32)

    def begin(i):
        r = pl.ds(pl.multiple_of(i * small, small), small)
        gr[r, :] = cot[r, :].astype(F32)
        ga0[own_rows(i * small, small), :] = cot[r, :]

    loop(rows // small, begin)

    jobs_of = {
        "d": (a3, ga0, ("h",), lambda l: load_gt(l)),
        "g": (t1, nb, ("nf",), None),
        "u": (t2, nb, (), lambda l: load_n(l)),
        "o": (a3, ga1, ("gt",), None),
        "q": (tq, nb, ("n",), None),
        "k": (tk, nb, (), None),
        "v": (t1, nb, (), None),
        "s": (t2, nb, (), lambda l: (load_nf(l - 1), load_h(l - 1)) if l else None),
    }
    open_to, made, added = [0], [0], [0]

    def add_next():
        if added[0] < made[0]:
            combine(*jobs[added[0]])
            added[0] += 1

    def make_next():
        if made[0] < open_to[0]:
            i = made[0]
            while added[0] <= i - SLOTS:
                add_next()
            l, name = jobs[i]
            left, right, needs, then = jobs_of[name]
            ready(*((key, l) for key in needs))
            make(l, name, left, right)
            made[0] += 1
            if then:
                then(l)

    def make_all():
        while made[0] < open_to[0]:
            make_next()

    plan = BSCHED

    def act(pair, point):
        def go():
            for ch in plan[pair][point]:
                if ch == "M":
                    make_next()
                if ch == "C":
                    add_next()

        return go

    def gfill(pair):
        return [act(pair, i) for i in (0, 1, 2)]

    def sfill(pair):
        return [act(pair, i) for i in (3, 4, 5, 6)]

    def tile_rows(i, j):
        return pl.ds(pl.multiple_of(i * LEN + j * 256, 256), 256)

    def ffn_seq(i):
        def go(j):
            r = tile_rows(i, j)
            gh = dot(ga0[r, :], weight("d", ffn_row), NT)
            g, u = a1[r, :], a2[r, :]
            th = jnp.tanh(0.7978845608028654 * (g + 0.044715 * g * g * g))
            val = 0.5 * g * (1.0 + th)
            slope = 0.5 * (1.0 + th) + 0.5 * g * (1.0 - th * th) * (0.7978845608028654 * (1.0 + 0.134145 * g * g))
            t1[r, :] = (gh * u * slope).astype(BF16)
            t2[r, :] = (gh * val).astype(BF16)
            part[r, :] = (dot(t1[r, :], weight("g", ffn_row)) + dot(t2[r, :], weight("u", ffn_row))).astype(BF16)

        loop(LEN // 256, go)

    def attn_head(i):
        def go(j):
            r = tile_rows(i, j)
            gg = dot(ga1[r, :], weight("o", 0), NT)
            s, mix = a1[r, :], a2[r, :]
            sig = 1.0 / (1.0 + jnp.exp(-s))
            rr = rms(mix, HEAD_FLOOR)
            t2[r, :] = (gg * (mix * rr) * (sig * (1.0 + s * (1.0 - sig)))).astype(BF16)
            gz = gg * (s * sig)
            inner = jnp.sum(gz * mix, -1, keepdims=True) / mix.shape[1]
            t1[r, :] = (rr * gz - (rr * rr * rr) * mix * inner).astype(BF16)

        loop(LEN // 256, go)

    def attn_tail(i):
        r = seq_rows(i)
        gm = t1[r, :]
        raw = (dot(gm, v[r, :], NT) * mask[i]).astype(BF16)
        t1[r, :] = dot(p[i], gm, TN).astype(BF16)
        c, sn = cosine[...], sine[...]
        for dst, grad in ((tq, dot(raw, k[r, :]) * scale), (tk, dot(raw, q[r, :], TN) * scale)):
            half = grad.shape[1] // 2
            g1, g2 = grad[:, :half], grad[:, half:]
            dst[r, :half] = (g1 * c + g2 * sn).astype(BF16)
            dst[r, half:] = (g2 * c - g1 * sn).astype(BF16)

        def go(j):
            r = pl.ds(pl.multiple_of(i * LEN + j * 256, 256), 256)
            tot = dot(tq[r, :], weight("q", 0)) + dot(tk[r, :], weight("k", 0))
            tot = tot + dot(t1[r, :], weight("v", 0)) + dot(t2[r, :], weight("s", 0))
            part[r, :] = tot.astype(BF16)

        loop(LEN // 256, go)

    def attn_seq(i):
        attn_head(i)
        attn_tail(i)

    def after(keys, body):
        def go(i):
            make_all()
            ready(*keys)
            body(i)

        return go

    for at, l in enumerate(order):
        last = at == layers - 1
        first = after([("wf", l), ("g", l), ("u", l), ("mid", l)], ffn_seq)
        gather_acts(me, ga0, rows, ags.at[2 * at], agr.at[2 * at], first, ffn_seq, gfill(2 * at))
        load_attn(l)
        open_to[0] = 8 * at + 3

        def to_mid(r0, n, tot, l=l):
            r = pl.ds(pl.multiple_of(r0, n), n)
            new = gr[r, :] + norm_back(xb[r, :], ffn_gain[l : l + 1, :], tot, layers + l)
            gr[r, :] = new
            ga1[own_rows(r0, n), :] = new.astype(BF16)

        sum_acts(me, part, rows, sib_buf, x_buf, z_buf, rss.at[2 * at], rsr.at[2 * at], to_mid, sfill(2 * at))
        if l:
            load(("x", l), x_mid.at[l - 1], xb)
        first = after([(key, l) for key in ("wa", "s", "m", "q", "k", "v", "p") + (("x",) if l else ())], attn_seq)
        gather_acts(me, ga1, rows, ags.at[2 * at + 1], agr.at[2 * at + 1], first, attn_seq, gfill(2 * at + 1))
        if not last:
            load_ffn(order[at + 1])
        open_to[0] = 8 * at + 8

        def to_prev(r0, n, tot, l=l, last=last):
            r = pl.ds(pl.multiple_of(r0, n), n)
            x = tokens[r, :].astype(F32) if l == 0 else xb[r, :]
            new = gr[r, :] + norm_back(x, attn_gain[l : l + 1, :], tot, l)
            if last:
                input_grad[r, :] = new
            else:
                gr[r, :] = new
                ga0[own_rows(r0, n), :] = new.astype(BF16)

        sum_acts(
            me, part, rows, sib_buf, x_buf, z_buf, rss.at[2 * at + 1], rsr.at[2 * at + 1], to_prev, sfill(2 * at + 1)
        )
        if not last:
            load_mid(order[at + 1])

    make_all()
    while added[0] < made[0]:
        add_next()
    partners = [me.sib(), me.xn(), me.yn(), me.znb(), me.at(z=me.zplus(2))]
    for j, dev in enumerate(partners):
        m = remote(acc.at[j], acc_in.at[j], gns.at[j], gnr.at[j], dev)
        m.start()
        m.wait()
        acc[j + 1] = acc[j] + acc_in[j]
    gains[...] = acc[len(partners)]
    for i in range(len(jobs) - SLOTS, len(jobs)):
        retire(i)
    for i in range(len(jobs)):
        for d in (1, 2, 3):
            z_send(i, d).wait_recv()


def run_backward(dims, cot, tokens, x_mid, mids, mask, cosine, sine, attn_gain, ffn_gain, kept):
    layers, rows, lanes, units, scale = dims
    depth = tokens.shape[1]
    total = kept[0].shape[1]
    group = 8 * rows
    seqs = group // LEN
    qk, val, ffn = units["q"][1], units["v"][1], units["g"][1]
    vm = pl.BlockSpec(memory_space=pltpu.VMEM)
    hb = pl.BlockSpec(memory_space=pl.ANY)
    outs = [((rows, depth), F32), ((8, depth), F32), ((layers, 2, 2, total, lanes), BF16)]
    jobs = layers * len(units)
    most = max(n for _, n in units.values())
    attn_rows = units["g"][0]
    dma = pltpu.SemaphoreType.DMA
    big = pltpu.VMEM((group, depth), BF16)
    return pl.pallas_call(
        functools.partial(backward_kernel, dims),
        out_shape=[jax.ShapeDtypeStruct(s, d) for s, d in outs],
        in_specs=[vm, vm, hb, hb] + [vm] * 5 + [hb] * 13,
        out_specs=[vm] * 2 + [hb],
        scratch_shapes=[
            pltpu.VMEM((rows, depth), F32), pltpu.VMEM((rows, depth), F32), big, big, big, big,
            pltpu.VMEM((4, rows, depth), BF16), pltpu.VMEM((2, rows, depth), BF16), pltpu.VMEM((rows, depth), BF16),
            pltpu.VMEM((max(attn_rows, total - attn_rows), depth), BF16),
            pltpu.VMEM((group, val), F32), pltpu.VMEM((group, val), F32), pltpu.VMEM((group, val), BF16),
            pltpu.VMEM((group, qk), BF16), pltpu.VMEM((group, qk), BF16), pltpu.VMEM((group, val), BF16),
            pltpu.VMEM((seqs, LEN, LEN), BF16),
            pltpu.VMEM((group, val), BF16), pltpu.VMEM((group, val), BF16),
            pltpu.VMEM((group, qk), BF16), pltpu.VMEM((group, qk), BF16),
            pltpu.VMEM((SLOTS, most, depth), BF16), pltpu.VMEM((SLOTS, most, depth // 2), BF16),
            pltpu.VMEM((6, 8, depth), F32), pltpu.VMEM((5, 8, depth), F32),
            dma((jobs, 4)), dma((jobs, 4)), dma((jobs, 3)), dma((jobs, 3)), dma((jobs,)),
            dma((2 * layers, 7)), dma((2 * layers, 7)), dma((2 * layers, 7)), dma((2 * layers, 7)),
            dma((16 * layers,)), dma((5,)), dma((5,)), pltpu.SemaphoreType.REGULAR((SLOTS,)),
        ],
        compiler_params=pltpu.CompilerParams(collective_id=1, has_side_effects=True, vmem_limit_bytes=VMEM_LIMIT),
    )(cot, tokens, x_mid, mids, mask, cosine, sine, attn_gain, ffn_gain, *kept)


NAMES = ("q", "k", "v", "s", "o", "g", "u", "d")
TILE = 128


def unstack_kernel(units, parts, *outs):
    for name, out in zip(NAMES, outs):
        r0, n = units[name]
        both = [parts[0, h, 0, r0 : r0 + n].astype(F32) + parts[0, h, 1, r0 : r0 + n].astype(F32) for h in range(2)]
        if name in ("q", "k"):
            out[0] = jnp.concatenate(both, 0).T
        else:
            for h in range(2):
                out[0, h * n : (h + 1) * n] = both[h]


def unstack_grads(units, parts):
    layers, _, _, total, lanes = parts.shape
    shapes, specs = [], []
    for name in NAMES:
        n = 2 * units[name][1]
        if name in ("q", "k"):
            shapes.append((layers, lanes, n))
            specs.append(pl.BlockSpec((1, TILE, n), lambda l, j: (l, j, 0)))
        else:
            shapes.append((layers, n, lanes))
            specs.append(pl.BlockSpec((1, n, TILE), lambda l, j: (l, 0, j)))
    return pl.pallas_call(
        functools.partial(unstack_kernel, units),
        grid=(layers, lanes // TILE),
        in_specs=[pl.BlockSpec((1, 2, 2, total, TILE), lambda l, j: (l, 0, 0, 0, j))],
        out_specs=specs,
        out_shape=[jax.ShapeDtypeStruct(s, F32) for s in shapes],
        compiler_params=pltpu.CompilerParams(vmem_limit_bytes=VMEM_LIMIT),
    )(parts)

def rotation(length, width):
    half = width // 2
    place = jnp.arange(length, dtype=F32)
    freqs = 10000.0 ** (-jnp.arange(half, dtype=F32) / half)
    angle = place[:, None] * freqs[None, :]
    return jnp.cos(angle), jnp.sin(angle)


def decay_mask(seg_rows, head, length):
    place = jnp.arange(length, dtype=jnp.int32)
    dist = place[:, None] - place[None, :]
    same = (seg_rows[:, :, None] == seg_rows[:, None, :]) & (dist >= 0)[None]
    rate = jnp.log1p(-(2.0 ** (-5.0 - head)))
    decay = jnp.exp(jnp.maximum(dist, 0).astype(F32) * rate)
    return jnp.where(same, decay[None], 0.0)


def setup(segments, w_query, w_value, w_gelu):
    dp, tensor = lax.axis_index("dp"), lax.axis_index("tensor")
    half = (dp // 2) % 2
    other = lax.ppermute(segments, "dp", [(i, i ^ 2) for i in range(8)])
    pair = jnp.where(half == 0, jnp.stack([segments, other]), jnp.stack([other, segments]))
    mask = decay_mask(pair, (tensor * 2 + half).astype(F32), LEN)
    cosine, sine = rotation(LEN, HEAD_QK)
    units, total = unit_rows(w_query.shape[2] // 2, w_value.shape[2] // 2, w_gelu.shape[2] // 2)
    return mask, cosine, sine, units, total


CONTRACT_ROWS = (((0,), (0,)), ((), ()))
CONTRACT_COLS = (((1,), (1,)), ((), ()))


def shortened(shard):
    return jax.tree.map(lambda a: a.astype(jnp.bfloat16) if a.dtype == jnp.float32 else a, shard)


def norm_rows(values, gain):
    return values * lax.rsqrt(jnp.mean(values * values, -1, keepdims=True) + EPS) * gain


def norm_heads(values):
    return values * lax.rsqrt(jnp.mean(values * values, -1, keepdims=True) + HEAD_FLOOR)


def gelu_tanh(values):
    return jax.nn.gelu(values, approximate=True)


def plain_rotation(length, width):
    half = width // 2
    place = jnp.arange(length, dtype=jnp.float32)
    freqs = 10000.0 ** (-jnp.arange(half, dtype=jnp.float32) / half)
    angle = place[:, None] * freqs[None, :]
    return (jnp.cos(angle)[:, None, :], jnp.sin(angle)[:, None, :])


def rotate(values, cosine, sine):
    half = values.shape[-1] // 2
    first = values[..., :half]
    second = values[..., half:]
    return jnp.concatenate([first * cosine - second * sine, second * cosine + first * sine], -1)


def rotate_back(grads, cosine, sine):
    half = grads.shape[-1] // 2
    first = grads[..., :half]
    second = grads[..., half:]
    return jnp.concatenate([first * cosine + second * sine, second * cosine - first * sine], -1)


def plain_mask(seg_rows, head_ids, length):
    place = jnp.arange(length, dtype=jnp.int32)
    dist = place[:, None] - place[None, :]
    same = (seg_rows[:, :, None] == seg_rows[:, None, :]) & (dist >= 0)[None]
    rates = jnp.log1p(-(2.0 ** (-5.0 - head_ids)))
    decay = jnp.exp(jnp.maximum(dist, 0).astype(jnp.float32)[None] * rates[:, None, None])
    return jnp.where(same[:, None], decay[None], 0.0)


def weights_of(rotated_query, rotated_key, mask, score_scale):
    unnormalized_scores = (
        jnp.einsum(
            "slhd,smhd->shlm", rotated_query, rotated_key, preferred_element_type=jnp.float32
        )
        * score_scale
    )
    return (unnormalized_scores * mask).astype(jnp.bfloat16)


def gather_rows(rows):
    return lax.all_gather(rows, "tensor", axis=0, tiled=True)


def sum_rows(part):
    return lax.psum_scatter(
        part.astype(jnp.bfloat16), "tensor", scatter_dimension=0, tiled=True
    ).astype(jnp.float32)


def fold_rows(acts, weights):
    pieces = jax.tree.map(lambda a: lax.all_gather(a, "dp", axis=0, tiled=True), shortened(weights))
    return tuple((jnp.dot(acts, p, preferred_element_type=jnp.float32) for p in pieces))


def map_columns(acts, weight):
    return jnp.dot(
        acts, lax.all_gather(weight, "dp", axis=1, tiled=True), preferred_element_type=jnp.float32
    )


def back_rows(grads, weights):
    pieces = lax.all_gather(shortened(weights), "dp", axis=0, tiled=True)
    total = lax.dot_general(grads[0], pieces[0], CONTRACT_COLS, preferred_element_type=jnp.float32)
    for grad, piece in zip(grads[1:], pieces[1:]):
        total = total + lax.dot_general(
            grad, piece, CONTRACT_COLS, preferred_element_type=jnp.float32
        )
    return total


def back_columns(grad, weight):
    return lax.dot_general(
        grad,
        lax.all_gather(weight, "dp", axis=1, tiled=True),
        CONTRACT_COLS,
        preferred_element_type=jnp.float32,
    )


def plain(
    tokens,
    segments,
    attn_gain,
    w_query,
    w_key,
    w_value,
    w_swish,
    w_output,
    ffn_gain,
    w_gelu,
    w_up,
    w_down,
    cotangent,
):
    layers = w_query.shape[0]
    heads_dev = w_query.shape[2] // HEAD_QK
    seqs = segments.shape[0] // LEN
    score_scale = HEAD_QK ** (-0.5)
    head_ids = (lax.axis_index("tensor") * heads_dev + jnp.arange(heads_dev)).astype(jnp.float32)
    mask = plain_mask(segments.reshape(seqs, LEN), head_ids, LEN)
    cosine, sine = plain_rotation(LEN, HEAD_QK)
    residual = tokens.astype(jnp.float32)
    saved = []
    for layer in range(layers):
        attn_in = (w_query[layer], w_key[layer], w_value[layer], w_swish[layer])
        ffn_in = (w_gelu[layer], w_up[layer])
        whole_in = attn_in + ffn_in
        whole_out = (w_output[layer], w_down[layer])
        normed = gather_rows(norm_rows(residual, attn_gain[layer]).astype(jnp.bfloat16))
        rows_all = normed.shape[0]
        query, keys, values, swish = fold_rows(normed, attn_in)
        vals = values.astype(jnp.bfloat16).reshape(seqs, LEN, heads_dev, HEAD_V)
        rotated_query = rotate(query.reshape(seqs, LEN, heads_dev, HEAD_QK), cosine, sine).astype(
            jnp.bfloat16
        )
        rotated_key = rotate(keys.reshape(seqs, LEN, heads_dev, HEAD_QK), cosine, sine).astype(
            jnp.bfloat16
        )
        probs = weights_of(rotated_query, rotated_key, mask, score_scale)
        mixed = jnp.einsum("shlm,smhv->slhv", probs, vals, preferred_element_type=jnp.float32)
        zed = norm_heads(mixed).reshape(rows_all, -1)
        gated = (jax.nn.silu(swish) * zed).astype(jnp.bfloat16)
        branch = map_columns(gated, w_output[layer])
        mid = residual + sum_rows(branch)
        normed_ffn = gather_rows(norm_rows(mid, ffn_gain[layer]).astype(jnp.bfloat16))
        gate_pre, up_pre = fold_rows(normed_ffn, ffn_in)
        hidden = (gelu_tanh(gate_pre) * up_pre).astype(jnp.bfloat16)
        branch_ffn = map_columns(hidden, w_down[layer])
        saved.append(
            (
                residual,
                normed,
                rotated_query,
                rotated_key,
                vals,
                swish,
                mixed,
                zed,
                gated,
                mid,
                normed_ffn,
                gate_pre,
                up_pre,
                hidden,
                whole_in,
                whole_out,
            )
        )
        residual = mid + sum_rows(branch_ffn)
    output = residual.astype(jnp.bfloat16)
    grad_res = cotangent.astype(jnp.float32)
    weight_parts = [None] * layers
    attn_gain_parts = [None] * layers
    ffn_gain_parts = [None] * layers
    for layer in reversed(range(layers)):
        (
            x_in,
            normed,
            rotated_query,
            rotated_key,
            vals,
            swish,
            mixed,
            zed,
            gated,
            mid,
            normed_ffn,
            gate_pre,
            up_pre,
            hidden,
            whole_in,
            whole_out,
        ) = saved[layer]
        attn_in = (w_query[layer], w_key[layer], w_value[layer], w_swish[layer])
        ffn_in = (w_gelu[layer], w_up[layer])
        rows_all = normed.shape[0]
        grad_c = gather_rows(grad_res.astype(jnp.bfloat16))
        down_grad = lax.dot_general(
            grad_c, hidden, CONTRACT_ROWS, preferred_element_type=jnp.float32
        )
        grad_hidden = back_columns(grad_c, w_down[layer])
        gelu_val, gelu_activation = jax.vjp(gelu_tanh, gate_pre)
        grad_gate = gelu_activation(grad_hidden * up_pre)[0].astype(jnp.bfloat16)
        grad_upv = (grad_hidden * gelu_val).astype(jnp.bfloat16)
        gelu_grad = lax.dot_general(
            normed_ffn, grad_gate, CONTRACT_ROWS, preferred_element_type=jnp.float32
        )
        up_grad = lax.dot_general(
            normed_ffn, grad_upv, CONTRACT_ROWS, preferred_element_type=jnp.float32
        )
        grad_nf = back_rows((grad_gate, grad_upv), ffn_in)
        _, ffn_norm_fn = jax.vjp(norm_rows, mid, ffn_gain[layer])
        grad_mid_norm, ffn_gain_parts[layer] = ffn_norm_fn(sum_rows(grad_nf))
        grad_mid = grad_res + grad_mid_norm
        grad_b = gather_rows(grad_mid.astype(jnp.bfloat16))
        output_grad_t = lax.dot_general(
            grad_b, gated, CONTRACT_ROWS, preferred_element_type=jnp.float32
        )
        grad_gated = back_columns(grad_b, w_output[layer])
        swish_output, swish_fn = jax.vjp(jax.nn.silu, swish)
        grad_sw = swish_fn(grad_gated * zed)[0].astype(jnp.bfloat16)
        grad_zed = grad_gated * swish_output
        _, head_fn = jax.vjp(norm_heads, mixed)
        grad_mixed = head_fn(grad_zed.reshape(mixed.shape))[0].astype(jnp.bfloat16)
        probs = weights_of(rotated_query, rotated_key, mask, score_scale)
        grad_probs = jnp.einsum(
            "slhv,smhv->shlm", grad_mixed, vals, preferred_element_type=jnp.float32
        )
        grad_raw = (grad_probs * mask).astype(jnp.bfloat16)
        grad_vals = jnp.einsum(
            "shlm,slhv->smhv", probs, grad_mixed, preferred_element_type=jnp.float32
        )
        grad_vals = grad_vals.astype(jnp.bfloat16).reshape(rows_all, -1)
        grad_qrot = (
            jnp.einsum("shlm,smhd->slhd", grad_raw, rotated_key, preferred_element_type=jnp.float32)
            * score_scale
        )
        grad_krot = (
            jnp.einsum(
                "shlm,slhd->smhd", grad_raw, rotated_query, preferred_element_type=jnp.float32
            )
            * score_scale
        )
        grad_q = rotate_back(grad_qrot, cosine, sine).astype(jnp.bfloat16).reshape(rows_all, -1)
        grad_k = rotate_back(grad_krot, cosine, sine).astype(jnp.bfloat16).reshape(rows_all, -1)
        attn_grads = tuple(
            (
                lax.dot_general(normed, g, CONTRACT_ROWS, preferred_element_type=jnp.float32)
                for g in (grad_q, grad_k, grad_vals, grad_sw)
            )
        )
        grad_n = back_rows((grad_q, grad_k, grad_vals, grad_sw), attn_in)
        _, attn_norm_fn = jax.vjp(norm_rows, x_in, attn_gain[layer])
        grad_x_norm, attn_gain_parts[layer] = attn_norm_fn(sum_rows(grad_n))
        grad_res = grad_mid + grad_x_norm
        weight_parts[layer] = jax.tree.map(
            lambda part: part.astype(jnp.float32),
            lax.psum_scatter(
                shortened(attn_grads + (output_grad_t, gelu_grad, up_grad, down_grad)),
                "dp",
                scatter_dimension=0,
                tiled=True,
            ),
        )
    attn_gain_grad, ffn_gain_grad = lax.psum(
        (jnp.stack(attn_gain_parts), jnp.stack(ffn_gain_parts)), ("dp", "tensor")
    )
    grad_query = jnp.stack([p[0] for p in weight_parts])
    grad_key = jnp.stack([p[1] for p in weight_parts])
    grad_value = jnp.stack([p[2] for p in weight_parts])
    grad_swish = jnp.stack([p[3] for p in weight_parts])
    grad_output = jnp.stack([p[4].T for p in weight_parts])
    grad_gelu = jnp.stack([p[5] for p in weight_parts])
    grad_up = jnp.stack([p[6] for p in weight_parts])
    grad_down = jnp.stack([p[7].T for p in weight_parts])
    return (
        output,
        grad_res,
        attn_gain_grad,
        grad_query,
        grad_key,
        grad_value,
        grad_swish,
        grad_output,
        ffn_gain_grad,
        grad_gelu,
        grad_up,
        grad_down,
    )


def grouped(
    tokens, segments, attn_gain, w_query, w_key, w_value, w_swish, w_output, ffn_gain, w_gelu, w_up, w_down, cotangent
):
    layers = w_query.shape[0]
    mask, cosine, sine, units, total = setup(segments, w_query, w_value, w_gelu)
    turn = lambda w: jnp.swapaxes(w, 1, 2)
    weights = (
        turn(w_query), turn(w_key), turn(w_value), turn(w_swish), w_output, turn(w_gelu), turn(w_up), w_down,
    )
    dims = (layers, tokens.shape[0], w_query.shape[1], units, HEAD_QK ** (-0.5))
    output, x_mid, mids, *kept = run_forward(
        dims, total, tokens, mask, cosine, sine, attn_gain, ffn_gain, weights
    )
    input_grad, gains, parts = run_backward(
        dims, cotangent, tokens, x_mid, mids, mask, cosine, sine, attn_gain, ffn_gain, kept
    )
    q, k, v, s, o, g, u, d = unstack_grads(units, parts)
    return (
        output, input_grad, gains[:layers], q, k, turn(v), turn(s), o, gains[layers : 2 * layers], turn(g), turn(u), d,
    )


def solution(mesh):
    rows = P(("dp", "tensor"), None)
    up, down = P(None, "dp", "tensor"), P(None, "tensor", "dp")
    in_specs = (rows, P("dp"), P(), up, up, up, up, down, P(), up, up, down, rows)
    out_specs = (rows, rows, P(), up, up, up, up, down, P(), up, up, down)
    step = grouped if (mesh.shape["dp"], mesh.shape["tensor"]) == (8, 4) else plain
    return jax.shard_map(step, mesh=mesh, in_specs=in_specs, out_specs=out_specs, check_vma=False)
```

```python
import functools

import jax
import jax.numpy as jnp
from jax import lax
from jax.experimental import pallas as pl
from jax.experimental.pallas import tpu as pltpu
from jax.sharding import PartitionSpec as P

HEAD_QK = 256
HEAD_V = 432
LEN = 512

EPS = 1e-06
HEAD_FLOOR = 1.0
NN = (((1,), (0,)), ((), ()))
NT = (((1,), (1,)), ((), ()))
TN = (((0,), (0,)), ((), ()))
MESH = pl.DeviceIdType.MESH
BF16 = jnp.bfloat16
F32 = jnp.float32
LOOK = 2
SCHED = (
    ("III", "P", "", "PI", "PI", "PI"),
    ("PI", "PI", "", "PI", "PI", ""),
    ("PI", "PI", "", "PI", "PI", ""),
    ("PI", "PI", "", "PI", "PI", ""),
    ("PI", "PI", "", "", ""),
)
COT_AFTER = "v"
CHUNKS = 2
VMEM_LIMIT = 60 * 1024 * 1024


def dot(a, b, dims=NN):
    return lax.dot_general(a, b, dims, preferred_element_type=F32)


def loop(steps, body):
    lax.fori_loop(0, steps, lambda i, c: (body(i), c)[1], 0)


class Place:
    def __init__(self):
        dp, tensor = lax.axis_index("dp"), lax.axis_index("tensor")
        self.dp, self.tensor = dp, tensor
        self.z, self.y = lax.div(dp, 2), lax.rem(dp, 2)
        self.x, self.c = lax.div(tensor, 2), lax.rem(tensor, 2)
        self.half = lax.rem(self.z, 2)
        self.zn = self.z + 1 - 2 * self.half

    def at(self, z=None, y=None, x=None, c=None):
        z = self.z if z is None else z
        y = self.y if y is None else y
        x = self.x if x is None else x
        c = self.c if c is None else c
        return (z * 2 + y, x * 2 + c)

    def zplus(self, d):
        return lax.rem(self.z + d + 4, 4)

    def sib(self):
        return self.at(c=1 - self.c)

    def xn(self):
        return self.at(x=1 - self.x)

    def yn(self):
        return self.at(y=1 - self.y)

    def znb(self):
        return self.at(z=self.zn)

    def peers(self):
        return [self.sib(), self.xn(), self.yn()] + [self.at(z=self.zplus(d)) for d in (1, 2, 3)]

    def greet(self):
        bar = pltpu.get_barrier_semaphore()
        peers = self.peers()
        for p in peers:
            pl.semaphore_signal(bar, inc=1, device_id=p, device_id_type=MESH)
        pl.semaphore_wait(bar, len(peers))


def remote(src, dst, ssem, rsem, dev):
    return pltpu.make_async_remote_copy(
        src_ref=src, dst_ref=dst, send_sem=ssem, recv_sem=rsem, device_id=dev, device_id_type=MESH
    )


def block(half, tensor, rows):
    return pl.ds(pl.multiple_of((half * 4 + tensor) * rows, rows), rows)


def part_of(r, at, n):
    return pl.ds(pl.multiple_of(r.start + at, n), n)


class Gather:
    def __init__(self, me, buf, rows, ssem, rsem):
        def move(k, half, x, dev, at=0, size=rows):
            r = part_of(block(half, x * 2 + me.c, rows), at, size)
            return remote(buf.at[r], buf.at[r], ssem.at[k], rsem.at[k], dev)

        n = rows // CHUNKS
        h, x = me.half, me.x
        self.me = me
        self.own_x = move(0, h, x, me.xn())
        self.own_s = move(1, h, x, me.sib())
        self.x_s = move(2, h, 1 - x, me.sib())
        self.z_s = move(3, 1 - h, x, me.sib())
        self.g_s = move(4, 1 - h, 1 - x, me.sib())
        self.own_z = [move(5 + i, h, x, me.znb(), i * n, n) for i in range(CHUNKS)]
        self.z_x = [move(5 + CHUNKS + i, 1 - h, x, me.xn(), i * n, n) for i in range(CHUNKS)]

    def begin(self):
        for m in self.own_z + [self.own_x, self.own_s]:
            m.start()

    def finish(self, first, second, fill=()):
        fill = list(fill)

        def step():
            if fill:
                fill.pop(0)()

        step()
        self.own_x.wait_recv()
        self.x_s.start()
        for a, b in zip(self.own_z, self.z_x):
            a.wait_recv()
            b.start()
        self.z_s.start()
        step()
        self.own_s.wait_recv()
        self.x_s.wait_recv()
        first(self.me.half)
        for m in self.z_x:
            m.wait_recv()
        self.g_s.start()
        step()
        self.z_s.wait_recv()
        self.g_s.wait_recv()
        second(1 - self.me.half)
        for m in self.own_z + self.z_x + [self.own_x, self.own_s, self.z_s, self.x_s, self.g_s]:
            m.wait_send()


def gather_acts(me, buf, rows, ssem, rsem, first, second, fill=()):
    g = Gather(me, buf, rows, ssem, rsem)
    g.begin()
    g.finish(first, second, fill)


def sum_acts(me, part, rows, sib_buf, x_buf, z_buf, ssem, rsem, body, fill=()):
    fill = list(fill)
    n = rows // CHUNKS

    def step():
        if fill:
            fill.pop(0)()

    h, x = me.half, me.x
    order = [(1 - h, 1 - x), (h, 1 - x), (1 - h, x), (h, x)]
    sibs = []
    for j, (hh, xx) in enumerate(order):
        m = remote(part.at[block(hh, xx * 2 + 1 - me.c, rows)], sib_buf.at[j], ssem.at[j], rsem.at[j], me.sib())
        m.start()
        sibs.append(m)
    step()
    small = 32

    def mine(j, at, size):
        hh, xx = order[j]
        return part_of(block(hh, xx * 2 + me.c, rows), at, size)

    def add(j, at, size, extra=None):
        def go(i):
            r = mine(j, at + i * small, small)
            k = pl.ds(pl.multiple_of(at + i * small, small), small)
            v = part[r, :].astype(F32) + sib_buf[j, k, :].astype(F32)
            if extra is not None:
                v = v + extra[k, :].astype(F32)
            part[r, :] = v.astype(BF16)

        loop(size // small, go)

    def cut(i):
        return pl.ds(i * n, n)

    g_x = [
        remote(part.at[mine(0, i * n, n)], x_buf.at[0, cut(i)], ssem.at[5 + i], rsem.at[5 + i], me.xn())
        for i in range(CHUNKS)
    ]
    x_x = remote(part.at[mine(1, 0, rows)], x_buf.at[1], ssem.at[4], rsem.at[4], me.xn())
    to_z = [
        remote(
            part.at[mine(2, i * n, n)], z_buf.at[cut(i)], ssem.at[5 + CHUNKS + i], rsem.at[5 + CHUNKS + i], me.znb()
        )
        for i in range(CHUNKS)
    ]
    sibs[0].wait_recv()
    for i in range(CHUNKS):
        add(0, i * n, n)
        g_x[i].start()
    sibs[1].wait_recv()
    add(1, 0, rows)
    x_x.start()
    step()
    sibs[2].wait_recv()
    for i in range(CHUNKS):
        g_x[i].wait_recv()
        add(2, i * n, n, x_buf.at[0])
        to_z[i].start()
    sibs[3].wait_recv()
    step()
    x_x.wait_recv()
    for m in to_z:
        m.wait_recv()

    def last(i):
        k = pl.ds(pl.multiple_of(i * small, small), small)
        v = part[mine(3, i * small, small), :].astype(F32) + sib_buf[3, k, :].astype(F32)
        v = v + x_buf[1, k, :].astype(F32) + z_buf[k, :].astype(F32)
        body(i * small, small, v)

    loop(rows // small, last)
    for m in sibs + g_x + to_z + [x_x]:
        m.wait_send()
    while fill:
        step()


def unit_rows(qk, val, ffn):
    sizes = (("q", qk), ("k", qk), ("v", val), ("s", val), ("o", val), ("g", ffn), ("u", ffn), ("d", ffn))
    out, at = {}, 0
    for name, n in sizes:
        out[name] = (at, n)
        at += n
    return out, at


def rms(v, floor):
    return lax.rsqrt(jnp.mean(v * v, -1, keepdims=True) + floor)


def forward_kernel(
    dims,
    tokens, cot, mask, cosine, sine, attn_gain, ffn_gain, w_q, w_k, w_v, w_s, w_o, w_g, w_u, w_d,
    output, x_mid, mids, wf, s_gc, s_n, s_nf, s_q, s_k, s_v, s_s, s_m, s_gt, s_g, s_u, s_h, s_p,
    W, N0, N1, part, sib_buf, x_buf, z_buf, q, k, v, s, m, gt, g, u, h, p,
    zs, zr, ys, yr, lo, ld, ags, agr, rss, rsr, sv,
):
    layers, rows, lanes, units, scale = dims
    me = Place()
    names = list(units)
    shards = dict(q=w_q, k=w_k, v=w_v, s=w_s, o=w_o, g=w_g, u=w_u, d=w_d)
    groups = [(l, units[n]) for l in range(layers) for n in names]
    spot = {(l, n): l * len(names) + i for l in range(layers) for i, n in enumerate(names)}
    my_lane = pl.multiple_of(me.dp * lanes, lanes)

    def shard(i, half):
        n = groups[i][1][1]
        return shards[names[i % len(names)]].at[groups[i][0], pl.ds(pl.multiple_of(half * n, 16), n)]

    def z_copy(i, d):
        l, (r0, n) = groups[i]
        tz = me.zplus(d)
        return remote(
            shard(i, lax.rem(tz, 2)), wf.at[l, pl.ds(r0, n), pl.ds(my_lane, lanes)],
            zs.at[i, d - 1], zr.at[i, d - 1], me.at(z=tz),
        )

    def y_copy(i, d):
        l, (r0, n) = groups[i]
        lane = pl.ds(pl.multiple_of((me.zplus(-d) * 2 + me.y) * lanes, lanes), lanes)
        dst = wf.at[l, pl.ds(r0, n), lane]
        src = shard(i, me.half) if d == 0 else dst
        return remote(src, dst, ys.at[i, d], yr.at[i, d], me.yn())

    def local_copy(i):
        l, (r0, n) = groups[i]
        return pltpu.make_async_copy(
            shard(i, me.half), wf.at[l, pl.ds(r0, n), pl.ds(my_lane, lanes)], lo.at[i]
        )

    def issue(i):
        if i < len(groups):
            for d in (1, 2, 3):
                z_copy(i, d).start()
            y_copy(i, 0).start()
            local_copy(i).start()

    issued, pumped = [0], [0]

    def send_next():
        if issued[0] < len(groups):
            issue(issued[0])
            issued[0] += 1

    def pass_on():
        i = pumped[0]
        if i >= len(groups):
            return
        while issued[0] <= i:
            send_next()
        pumped[0] += 1
        for d in (1, 3, 2):
            z_copy(i, d).wait_recv()
            y_copy(i, d).start()

    plan = SCHED

    def act(pair, point):
        def go():
            for ch in plan[pair][point]:
                if ch == "I":
                    send_next()
                if ch == "P":
                    pass_on()
        return go

    def gfill(pair):
        return [act(pair, 0), act(pair, 1), act(pair, 5)]

    def sfill(pair):
        return [act(pair, 2), act(pair, 3), act(pair, 4)]

    def take(l, *wanted):
        idx = [spot[l, n] for n in wanted]
        while pumped[0] <= idx[-1]:
            pass_on()
            while issued[0] - pumped[0] < LOOK:
                if issued[0] >= len(groups):
                    break
                send_next()
        copies = []
        for i in idx:
            for d in range(4):
                y_copy(i, d).wait_recv()
            local_copy(i).wait()
            r0, n = groups[i][1]
            c = pltpu.make_async_copy(wf.at[l, pl.ds(r0, n)], W.at[pl.ds(r0, n)], ld.at[i])
            c.start()
            copies.append(c)
        for c in copies:
            c.wait()

    saves = []

    def save(src, dst):
        c = pltpu.make_async_copy(src, dst, sv.at[len(saves)])
        c.start()
        saves.append(c)

    waited = [0]

    def settle():
        while waited[0] < len(saves):
            saves[waited[0]].wait()
            waited[0] += 1

    def weight(n):
        r0, size = units[n]
        return W[pl.ds(r0, size), :]

    def seq_rows(i):
        return pl.ds(pl.multiple_of(i * LEN, LEN), LEN)

    seqs = 2
    own = (me.half * 4 + me.tensor) * rows

    def own_rows(r0, n):
        return pl.ds(pl.multiple_of(own + r0, n), n)

    me.greet()
    small = 32

    def first_norm(i):
        r = pl.ds(pl.multiple_of(i * small, small), small)
        x = tokens[r, :].astype(F32)
        N0[own_rows(i * small, small), :] = (x * rms(x, EPS) * attn_gain[0:1, :]).astype(BF16)
        N1[own_rows(i * small, small), :] = cot[r, :]

    loop(rows // small, first_norm)
    def out_rows(i, src, name):
        def go(j):
            r = pl.ds(pl.multiple_of(i * LEN + j * 256, 256), 256)
            part[r, :] = dot(src[r, :], weight(name)).astype(BF16)

        loop(LEN // 256, go)

    def turned(name, dst, i):
        r = seq_rows(i)
        t = dot(N0[r, :], weight(name), NT)
        half = t.shape[1] // 2
        t1, t2 = t[:, :half], t[:, half:]
        c, sn = cosine[...], sine[...]
        dst[r, :half] = (t1 * c - t2 * sn).astype(BF16)
        dst[r, half:] = (t2 * c + t1 * sn).astype(BF16)

    def retain(i):
        r = seq_rows(i)
        v[r, :] = dot(N0[r, :], weight("v"), NT).astype(BF16)
        raw = dot(q[r, :], k[r, :], NT) * scale
        probs = (raw * mask[i]).astype(BF16)
        p[i] = probs
        m[r, :] = dot(probs, v[r, :])

    def gate(i):
        r = seq_rows(i)
        t = dot(N0[r, :], weight("s"), NT)
        s[r, :] = t
        mix = m[r, :]
        gt[r, :] = (jax.nn.silu(t) * (mix * rms(mix, HEAD_FLOOR))).astype(BF16)

    stages = (
        ("q", functools.partial(turned, "q", q)), ("k", functools.partial(turned, "k", k)), ("v", retain),
        ("s", gate), ("o", lambda i: out_rows(i, gt, "o")),
    )

    def attn_seq(i, l, fetch):
        for name, stage in stages:
            if fetch:
                take(l, name)
            stage(i)

    def ffn_seq(i, l, fetch):
        r = seq_rows(i)
        if fetch:
            take(l, "g")
        g[r, :] = dot(N1[r, :], weight("g"), NT)
        if fetch:
            take(l, "u")
        t = dot(N1[r, :], weight("u"), NT)
        u[r, :] = t
        h[r, :] = (jax.nn.gelu(g[r, :], approximate=True) * t).astype(BF16)
        if fetch:
            take(l, "d")
        out_rows(i, h, "d")

    both = lambda body, l: (functools.partial(body, l=l, fetch=True), functools.partial(body, l=l, fetch=False))

    for l in range(layers):
        if l:
            gather_acts(me, N0, rows, ags.at[2 * l], agr.at[2 * l], *both(attn_seq, l), gfill(2 * l))
        else:
            own_rows_of = Gather(me, N0, rows, ags.at[0], agr.at[0])
            grads_of = Gather(me, N1, rows, ags.at[2 * layers], agr.at[2 * layers])
            own_rows_of.begin()
            act(0, 0)()
            grads_of.begin()
            idle = lambda i: None
            own_rows_of.finish(idle, idle, [act(0, 1), act(0, 5), act(2 * layers, 3)])
            for name, stage in stages:
                take(0, name)
                loop(seqs, stage)
                if name == COT_AFTER:
                    grads_of.finish(idle, idle, [act(2 * layers, i) for i in (0, 1, 2)])
                    save(N1, s_gc)
        for src, dst in ((N0, s_n), (q, s_q), (k, s_k), (v, s_v), (p, s_p), (m, s_m), (s, s_s), (gt, s_gt)):
            save(src, dst.at[l])

        if l == 0:
            saves[0].wait()
            waited[0] = 1

        def to_mid(r0, n, total, l=l):
            r = pl.ds(pl.multiple_of(r0, n), n)
            x = (tokens[r, :].astype(F32) if l == 0 else x_mid[l - 1, r, :]) + total
            mids[l, r, :] = x
            N1[own_rows(r0, n), :] = (x * rms(x, EPS) * ffn_gain[l : l + 1, :]).astype(BF16)

        sum_acts(me, part, rows, sib_buf, x_buf, z_buf, rss.at[2 * l], rsr.at[2 * l], to_mid, sfill(2 * l))
        gather_acts(me, N1, rows, ags.at[2 * l + 1], agr.at[2 * l + 1], *both(ffn_seq, l), gfill(2 * l + 1))
        for src, dst in ((N1, s_nf), (g, s_g), (u, s_u), (h, s_h)):
            save(src, dst.at[l])

        def to_next(r0, n, total, l=l):
            r = pl.ds(pl.multiple_of(r0, n), n)
            x = mids[l, r, :] + total
            if l + 1 < layers:
                x_mid[l, r, :] = x
                N0[own_rows(r0, n), :] = (x * rms(x, EPS) * attn_gain[l + 1 : l + 2, :]).astype(BF16)
            else:
                output[r, :] = x.astype(BF16)

        settle()
        sum_acts(me, part, rows, sib_buf, x_buf, z_buf, rss.at[2 * l + 1], rsr.at[2 * l + 1], to_next, sfill(2 * l + 1))
    settle()
    for i in range(len(groups)):
        for d in (1, 2, 3):
            z_copy(i, d).wait_send()
        for d in range(4):
            y_copy(i, d).wait_send()


def run_forward(dims, total, tokens, cot, mask, cosine, sine, attn_gain, ffn_gain, weights):
    layers, rows, lanes, units, scale = dims
    depth = tokens.shape[1]
    group = 8 * rows
    seqs = group // LEN
    qk, val, ffn = units["q"][1], units["v"][1], units["g"][1]
    vm = pl.BlockSpec(memory_space=pltpu.VMEM)
    hb = pl.BlockSpec(memory_space=pl.ANY)
    outs = [
        ((rows, depth), BF16), ((layers - 1, rows, depth), F32), ((layers, rows, depth), F32),
        ((layers, total, depth), BF16), ((group, depth), BF16),
        ((layers, group, depth), BF16), ((layers, group, depth), BF16),
        ((layers, group, qk), BF16), ((layers, group, qk), BF16), ((layers, group, val), BF16),
        ((layers, group, val), F32), ((layers, group, val), F32), ((layers, group, val), BF16),
        ((layers, group, ffn), F32), ((layers, group, ffn), F32), ((layers, group, ffn), BF16),
        ((layers, seqs, LEN, LEN), BF16),
    ]
    n_groups = layers * len(units)
    dma = pltpu.SemaphoreType.DMA
    return pl.pallas_call(
        functools.partial(forward_kernel, dims),
        out_shape=[jax.ShapeDtypeStruct(s, d) for s, d in outs],
        in_specs=[vm] * 7 + [hb] * 8,
        out_specs=[vm] * 3 + [hb] * 14,
        scratch_shapes=[
            pltpu.VMEM((total, depth), BF16),
            pltpu.VMEM((group, depth), BF16), pltpu.VMEM((group, depth), BF16), pltpu.VMEM((group, depth), BF16),
            pltpu.VMEM((4, rows, depth), BF16), pltpu.VMEM((2, rows, depth), BF16), pltpu.VMEM((rows, depth), BF16),
            pltpu.VMEM((group, qk), BF16), pltpu.VMEM((group, qk), BF16), pltpu.VMEM((group, val), BF16),
            pltpu.VMEM((group, val), F32), pltpu.VMEM((group, val), F32), pltpu.VMEM((group, val), BF16),
            pltpu.VMEM((group, ffn), F32), pltpu.VMEM((group, ffn), F32), pltpu.VMEM((group, ffn), BF16),
            pltpu.VMEM((seqs, LEN, LEN), BF16),
            dma((n_groups, 3)), dma((n_groups, 3)), dma((n_groups, 4)), dma((n_groups, 4)),
            dma((n_groups,)), dma((n_groups,)),
            *[dma((2 * layers + 1, 5 + 2 * CHUNKS)) for _ in range(4)],
            dma((12 * layers + 1,)),
        ],
        compiler_params=pltpu.CompilerParams(collective_id=0, has_side_effects=True, vmem_limit_bytes=VMEM_LIMIT),
    )(tokens, cot, mask, cosine, sine, attn_gain, ffn_gain, *weights)


SLOTS = 4
BSCHED = (
    ("", "", "", "", "M", "MM", ""),
    ("C", "C", "", "", "CMM", "CMCMM", ""),
    ("C", "C", "C", "", "M", "MM", ""),
    ("C", "C", "", "", "CMM", "CMCMM", ""),
)


def backward_kernel(
    dims,
    cot, tokens, x_mid, mids, mask, cosine, sine, attn_gain, ffn_gain,
    wf, s_gc, s_n, s_nf, s_q, s_k, s_v, s_s, s_m, s_gt, s_g, s_u, s_h, s_p,
    input_grad, gains, rz,
    gr, xb, nb, ga0, ga1, part, sib_buf, x_buf, z_buf, W, a1, a2, a3, q, k, v, p, t1, t2, tq, tk, G, ry, acc, acc_in,
    ys, yr, zs, zr, os, ags, agr, rss, rsr, ld, gns, gnr, credit,
):
    layers, rows, lanes, units, scale = dims
    me = Place()
    depth = cot.shape[1]
    wide = 512
    small = 32
    seqs = 2
    order = list(reversed(range(layers)))
    jobs = [(l, n) for l in order for n in ("d", "g", "u", "o", "q", "k", "v", "s")]
    index = {job: i for i, job in enumerate(jobs)}
    own = (me.half * 4 + me.tensor) * rows
    ffn_row = units["g"][0]
    attn_end = ffn_row
    total_rows = units["d"][0] + units["d"][1]

    def own_rows(r0, n):
        return pl.ds(pl.multiple_of(own + r0, n), n)

    def seq_rows(i):
        return pl.ds(pl.multiple_of(i * LEN, LEN), LEN)

    def lane(i):
        return pl.ds(pl.multiple_of(i * lanes, lanes), lanes)

    def y_send(i, d):
        n = units[jobs[i][1]][1]
        tz = me.zplus(d)
        return remote(
            G.at[i % SLOTS, pl.ds(0, n), lane(tz * 2 + 1 - me.y)], ry.at[i % SLOTS, pl.ds(0, n), lane(tz)],
            ys.at[i, d], yr.at[i, d], me.yn(),
        )

    def z_send(i, d):
        l, name = jobs[i]
        r0, n = units[name]
        tz = me.zplus(d)
        return remote(
            G.at[i % SLOTS, pl.ds(0, n), lane(tz * 2 + me.y)], rz.at[l, me.half, d // 2, pl.ds(r0, n)],
            zs.at[i, d - 1], zr.at[i, d - 1], me.at(z=tz),
        )

    def own_copy(i):
        l, name = jobs[i]
        r0, n = units[name]
        return pltpu.make_async_copy(
            G.at[i % SLOTS, pl.ds(0, n), lane(me.dp)], rz.at[l, me.half, 0, pl.ds(r0, n)], os.at[i]
        )

    def retire(i):
        for d in range(4):
            y_send(i, d).wait_send()
        for d in (1, 2, 3):
            z_send(i, d).wait_send()
        own_copy(i).wait()

    def make(l, name, left, right):
        i = index[l, name]
        n = units[name][1]
        if i >= SLOTS:
            retire(i - SLOTS)

        def go(j):
            cols = pl.ds(pl.multiple_of(j * wide, wide), wide)
            G[i % SLOTS, :n, cols] = dot(left[...], right[:, cols], TN).astype(BF16)

        loop(depth // wide, go)
        if i >= SLOTS:
            pl.semaphore_wait(credit.at[i % SLOTS], 1)
        for d in (2, 1, 3, 0):
            y_send(i, d).start()

    def combine(l, name):
        i = index[l, name]
        n = units[name][1]
        for d in (2, 1, 3, 0):
            y_send(i, d).wait_recv()
            tz = me.zplus(d)

            def add(j, tz=tz):
                r = pl.ds(pl.multiple_of(j * 16, 16), 16)
                c = lane(tz * 2 + me.y)
                both = G[i % SLOTS, r, c].astype(F32) + ry[i % SLOTS, r, lane(tz)].astype(F32)
                G[i % SLOTS, r, c] = both.astype(BF16)

            loop(n // 16, add)
            if d:
                z_send(i, d).start()
            else:
                own_copy(i).start()
        if i + SLOTS < len(jobs):
            pl.semaphore_signal(credit.at[i % SLOTS], inc=1, device_id=me.yn(), device_id_type=MESH)

    spots = {}

    def load(key, src, dst):
        c = pltpu.make_async_copy(src, dst, ld.at[len(spots)])
        c.start()
        spots[key] = c

    def ready(*keys):
        for key in keys:
            spots[key].wait()

    def load_ffn(l):
        load(("wf", l), wf.at[l, pl.ds(ffn_row, total_rows - ffn_row)], W.at[pl.ds(0, total_rows - ffn_row)])
        load(("g", l), s_g.at[l], a1)
        load(("u", l), s_u.at[l], a2)

    def load_attn(l):
        load(("wa", l), wf.at[l, pl.ds(0, attn_end)], W.at[pl.ds(0, attn_end)])
        load(("s", l), s_s.at[l], a1)
        load(("m", l), s_m.at[l], a2)
        load(("q", l), s_q.at[l], q)
        load(("k", l), s_k.at[l], k)
        load(("v", l), s_v.at[l], v)
        load(("p", l), s_p.at[l], p)

    def load_mid(l):
        load(("mid", l), mids.at[l], xb)

    def load_h(l):
        load(("h", l), s_h.at[l], a3)

    def load_nf(l):
        load(("nf", l), s_nf.at[l], nb)

    def load_gt(l):
        load(("gt", l), s_gt.at[l], a3)

    def load_n(l):
        load(("n", l), s_n.at[l], nb)

    def weight(name, base):
        r0, n = units[name]
        return W[pl.ds(r0 - base, n), :]

    def norm_back(x, gain, dn, gain_row):
        e = rms(x, EPS)
        gx = dn * gain
        inner = jnp.sum(gx * x, -1, keepdims=True)
        acc[0, gain_row : gain_row + 1, :] += jnp.sum(dn * x * e, 0, keepdims=True)
        return e * gx - (e * e * e) * x * (inner / depth)

    me.greet()
    load("gc", s_gc, ga0)
    load_ffn(order[0])
    load_mid(order[0])
    load_h(order[0])
    load_nf(order[0])
    acc[0] = jnp.zeros(acc.shape[1:], F32)

    def begin(i):
        r = pl.ds(pl.multiple_of(i * small, small), small)
        gr[r, :] = cot[r, :].astype(F32)

    loop(rows // small, begin)

    jobs_of = {
        "d": (a3, ga0, ("h",), lambda l: load_gt(l)),
        "g": (t1, nb, ("nf",), None),
        "u": (t2, nb, (), lambda l: load_n(l)),
        "o": (a3, ga1, ("gt",), None),
        "q": (tq, nb, ("n",), None),
        "k": (tk, nb, (), None),
        "v": (t1, nb, (), None),
        "s": (t2, nb, (), lambda l: (load_nf(l - 1), load_h(l - 1)) if l else None),
    }
    open_to, made, added = [0], [0], [0]

    def add_next():
        if added[0] < made[0]:
            combine(*jobs[added[0]])
            added[0] += 1

    def make_next():
        if made[0] < open_to[0]:
            i = made[0]
            while added[0] <= i - SLOTS:
                add_next()
            l, name = jobs[i]
            left, right, needs, then = jobs_of[name]
            ready(*((key, l) for key in needs))
            make(l, name, left, right)
            made[0] += 1
            if then:
                then(l)

    def make_all():
        while made[0] < open_to[0]:
            make_next()

    plan = BSCHED

    def act(pair, point):
        def go():
            for ch in plan[pair][point]:
                if ch == "M":
                    make_next()
                if ch == "C":
                    add_next()

        return go

    def gfill(pair):
        return [act(pair, i) for i in (0, 1, 2)]

    def sfill(pair):
        return [act(pair, i) for i in (3, 4, 5, 6)]

    def tile_rows(i, j):
        return pl.ds(pl.multiple_of(i * LEN + j * 256, 256), 256)

    def ffn_seq(i):
        def go(j):
            r = tile_rows(i, j)
            gh = dot(ga0[r, :], weight("d", ffn_row), NT)
            g, u = a1[r, :], a2[r, :]
            th = jnp.tanh(0.7978845608028654 * (g + 0.044715 * g * g * g))
            val = 0.5 * g * (1.0 + th)
            slope = 0.5 * (1.0 + th) + 0.5 * g * (1.0 - th * th) * (0.7978845608028654 * (1.0 + 0.134145 * g * g))
            t1[r, :] = (gh * u * slope).astype(BF16)
            t2[r, :] = (gh * val).astype(BF16)
            part[r, :] = (dot(t1[r, :], weight("g", ffn_row)) + dot(t2[r, :], weight("u", ffn_row))).astype(BF16)

        loop(LEN // 256, go)

    def attn_head(i):
        def go(j):
            r = tile_rows(i, j)
            gg = dot(ga1[r, :], weight("o", 0), NT)
            s, mix = a1[r, :], a2[r, :]
            sig = 1.0 / (1.0 + jnp.exp(-s))
            rr = rms(mix, HEAD_FLOOR)
            t2[r, :] = (gg * (mix * rr) * (sig * (1.0 + s * (1.0 - sig)))).astype(BF16)
            gz = gg * (s * sig)
            inner = jnp.sum(gz * mix, -1, keepdims=True) / mix.shape[1]
            t1[r, :] = (rr * gz - (rr * rr * rr) * mix * inner).astype(BF16)

        loop(LEN // 256, go)

    def attn_tail(i):
        r = seq_rows(i)
        gm = t1[r, :]
        raw = (dot(gm, v[r, :], NT) * mask[i]).astype(BF16)
        t1[r, :] = dot(p[i], gm, TN).astype(BF16)
        c, sn = cosine[...], sine[...]
        for dst, grad in ((tq, dot(raw, k[r, :]) * scale), (tk, dot(raw, q[r, :], TN) * scale)):
            half = grad.shape[1] // 2
            g1, g2 = grad[:, :half], grad[:, half:]
            dst[r, :half] = (g1 * c + g2 * sn).astype(BF16)
            dst[r, half:] = (g2 * c - g1 * sn).astype(BF16)

        def go(j):
            r = pl.ds(pl.multiple_of(i * LEN + j * 256, 256), 256)
            tot = dot(tq[r, :], weight("q", 0)) + dot(tk[r, :], weight("k", 0))
            tot = tot + dot(t1[r, :], weight("v", 0)) + dot(t2[r, :], weight("s", 0))
            part[r, :] = tot.astype(BF16)

        loop(LEN // 256, go)

    def attn_seq(i):
        attn_head(i)
        attn_tail(i)

    def after(keys, body):
        def go(i):
            make_all()
            ready(*keys)
            body(i)

        return go

    for at, l in enumerate(order):
        last = at == layers - 1
        first = after([("wf", l), ("g", l), ("u", l), ("mid", l)], ffn_seq)
        if at == 0:
            ready("gc")
            first(0)
            ffn_seq(1)
        else:
            gather_acts(me, ga0, rows, ags.at[2 * at], agr.at[2 * at], first, ffn_seq, gfill(2 * at))
        load_attn(l)
        open_to[0] = 8 * at + 3

        def to_mid(r0, n, tot, l=l):
            r = pl.ds(pl.multiple_of(r0, n), n)
            new = gr[r, :] + norm_back(xb[r, :], ffn_gain[l : l + 1, :], tot, layers + l)
            gr[r, :] = new
            ga1[own_rows(r0, n), :] = new.astype(BF16)

        sum_acts(me, part, rows, sib_buf, x_buf, z_buf, rss.at[2 * at], rsr.at[2 * at], to_mid, sfill(2 * at))
        if l:
            load(("x", l), x_mid.at[l - 1], xb)
        first = after([(key, l) for key in ("wa", "s", "m", "q", "k", "v", "p") + (("x",) if l else ())], attn_seq)
        gather_acts(me, ga1, rows, ags.at[2 * at + 1], agr.at[2 * at + 1], first, attn_seq, gfill(2 * at + 1))
        if not last:
            load_ffn(order[at + 1])
        open_to[0] = 8 * at + 8

        def to_prev(r0, n, tot, l=l, last=last):
            r = pl.ds(pl.multiple_of(r0, n), n)
            x = tokens[r, :].astype(F32) if l == 0 else xb[r, :]
            new = gr[r, :] + norm_back(x, attn_gain[l : l + 1, :], tot, l)
            if last:
                input_grad[r, :] = new
            else:
                gr[r, :] = new
                ga0[own_rows(r0, n), :] = new.astype(BF16)

        sum_acts(
            me, part, rows, sib_buf, x_buf, z_buf, rss.at[2 * at + 1], rsr.at[2 * at + 1], to_prev, sfill(2 * at + 1)
        )
        if not last:
            load_mid(order[at + 1])

    make_all()
    while added[0] < made[0]:
        add_next()
    partners = [me.sib(), me.xn(), me.yn(), me.znb(), me.at(z=me.zplus(2))]
    for j, dev in enumerate(partners):
        m = remote(acc.at[j], acc_in.at[j], gns.at[j], gnr.at[j], dev)
        m.start()
        m.wait()
        acc[j + 1] = acc[j] + acc_in[j]
    gains[...] = acc[len(partners)]
    for i in range(len(jobs) - SLOTS, len(jobs)):
        retire(i)
    for i in range(len(jobs)):
        for d in (1, 2, 3):
            z_send(i, d).wait_recv()


def run_backward(dims, cot, tokens, x_mid, mids, mask, cosine, sine, attn_gain, ffn_gain, kept):
    layers, rows, lanes, units, scale = dims
    depth = tokens.shape[1]
    total = kept[0].shape[1]
    group = 8 * rows
    seqs = group // LEN
    qk, val, ffn = units["q"][1], units["v"][1], units["g"][1]
    vm = pl.BlockSpec(memory_space=pltpu.VMEM)
    hb = pl.BlockSpec(memory_space=pl.ANY)
    outs = [((rows, depth), F32), ((8, depth), F32), ((layers, 2, 2, total, lanes), BF16)]
    jobs = layers * len(units)
    most = max(n for _, n in units.values())
    attn_rows = units["g"][0]
    dma = pltpu.SemaphoreType.DMA
    big = pltpu.VMEM((group, depth), BF16)
    return pl.pallas_call(
        functools.partial(backward_kernel, dims),
        out_shape=[jax.ShapeDtypeStruct(s, d) for s, d in outs],
        in_specs=[vm, vm, hb, hb] + [vm] * 5 + [hb] * 14,
        out_specs=[vm] * 2 + [hb],
        scratch_shapes=[
            pltpu.VMEM((rows, depth), F32), pltpu.VMEM((rows, depth), F32), big, big, big, big,
            pltpu.VMEM((4, rows, depth), BF16), pltpu.VMEM((2, rows, depth), BF16), pltpu.VMEM((rows, depth), BF16),
            pltpu.VMEM((max(attn_rows, total - attn_rows), depth), BF16),
            pltpu.VMEM((group, val), F32), pltpu.VMEM((group, val), F32), pltpu.VMEM((group, val), BF16),
            pltpu.VMEM((group, qk), BF16), pltpu.VMEM((group, qk), BF16), pltpu.VMEM((group, val), BF16),
            pltpu.VMEM((seqs, LEN, LEN), BF16),
            pltpu.VMEM((group, val), BF16), pltpu.VMEM((group, val), BF16),
            pltpu.VMEM((group, qk), BF16), pltpu.VMEM((group, qk), BF16),
            pltpu.VMEM((SLOTS, most, depth), BF16), pltpu.VMEM((SLOTS, most, depth // 2), BF16),
            pltpu.VMEM((6, 8, depth), F32), pltpu.VMEM((5, 8, depth), F32),
            dma((jobs, 4)), dma((jobs, 4)), dma((jobs, 3)), dma((jobs, 3)), dma((jobs,)),
            *[dma((2 * layers, 5 + 2 * CHUNKS)) for _ in range(4)],
            dma((16 * layers + 1,)), dma((5,)), dma((5,)), pltpu.SemaphoreType.REGULAR((SLOTS,)),
        ],
        compiler_params=pltpu.CompilerParams(collective_id=1, has_side_effects=True, vmem_limit_bytes=VMEM_LIMIT),
    )(cot, tokens, x_mid, mids, mask, cosine, sine, attn_gain, ffn_gain, *kept)


NAMES = ("q", "k", "v", "s", "o", "g", "u", "d")
TILE = 128


def unstack_kernel(units, parts, *outs):
    for name, out in zip(NAMES, outs):
        r0, n = units[name]
        both = [parts[0, h, 0, r0 : r0 + n].astype(F32) + parts[0, h, 1, r0 : r0 + n].astype(F32) for h in range(2)]
        if name in ("q", "k"):
            out[0] = jnp.concatenate(both, 0).T
        else:
            for h in range(2):
                out[0, h * n : (h + 1) * n] = both[h]


def unstack_grads(units, parts):
    layers, _, _, total, lanes = parts.shape
    shapes, specs = [], []
    for name in NAMES:
        n = 2 * units[name][1]
        if name in ("q", "k"):
            shapes.append((layers, lanes, n))
            specs.append(pl.BlockSpec((1, TILE, n), lambda l, j: (l, j, 0)))
        else:
            shapes.append((layers, n, lanes))
            specs.append(pl.BlockSpec((1, n, TILE), lambda l, j: (l, 0, j)))
    return pl.pallas_call(
        functools.partial(unstack_kernel, units),
        grid=(layers, lanes // TILE),
        in_specs=[pl.BlockSpec((1, 2, 2, total, TILE), lambda l, j: (l, 0, 0, 0, j))],
        out_specs=specs,
        out_shape=[jax.ShapeDtypeStruct(s, F32) for s in shapes],
        compiler_params=pltpu.CompilerParams(vmem_limit_bytes=VMEM_LIMIT),
    )(parts)

def rotation(length, width):
    half = width // 2
    place = jnp.arange(length, dtype=F32)
    freqs = 10000.0 ** (-jnp.arange(half, dtype=F32) / half)
    angle = place[:, None] * freqs[None, :]
    return jnp.cos(angle), jnp.sin(angle)


def decay_mask(seg_rows, head, length):
    place = jnp.arange(length, dtype=jnp.int32)
    dist = place[:, None] - place[None, :]
    same = (seg_rows[:, :, None] == seg_rows[:, None, :]) & (dist >= 0)[None]
    rate = jnp.log1p(-(2.0 ** (-5.0 - head)))
    decay = jnp.exp(jnp.maximum(dist, 0).astype(F32) * rate)
    return jnp.where(same, decay[None], 0.0)


def setup(segments, w_query, w_value, w_gelu):
    dp, tensor = lax.axis_index("dp"), lax.axis_index("tensor")
    half = (dp // 2) % 2
    other = lax.ppermute(segments, "dp", [(i, i ^ 2) for i in range(8)])
    pair = jnp.where(half == 0, jnp.stack([segments, other]), jnp.stack([other, segments]))
    mask = decay_mask(pair, (tensor * 2 + half).astype(F32), LEN)
    cosine, sine = rotation(LEN, HEAD_QK)
    units, total = unit_rows(w_query.shape[2] // 2, w_value.shape[2] // 2, w_gelu.shape[2] // 2)
    return mask, cosine, sine, units, total


CONTRACT_ROWS = (((0,), (0,)), ((), ()))
CONTRACT_COLS = (((1,), (1,)), ((), ()))


def shortened(shard):
    return jax.tree.map(lambda a: a.astype(jnp.bfloat16) if a.dtype == jnp.float32 else a, shard)


def norm_rows(values, gain):
    return values * lax.rsqrt(jnp.mean(values * values, -1, keepdims=True) + EPS) * gain


def norm_heads(values):
    return values * lax.rsqrt(jnp.mean(values * values, -1, keepdims=True) + HEAD_FLOOR)


def gelu_tanh(values):
    return jax.nn.gelu(values, approximate=True)


def plain_rotation(length, width):
    half = width // 2
    place = jnp.arange(length, dtype=jnp.float32)
    freqs = 10000.0 ** (-jnp.arange(half, dtype=jnp.float32) / half)
    angle = place[:, None] * freqs[None, :]
    return (jnp.cos(angle)[:, None, :], jnp.sin(angle)[:, None, :])


def rotate(values, cosine, sine):
    half = values.shape[-1] // 2
    first = values[..., :half]
    second = values[..., half:]
    return jnp.concatenate([first * cosine - second * sine, second * cosine + first * sine], -1)


def rotate_back(grads, cosine, sine):
    half = grads.shape[-1] // 2
    first = grads[..., :half]
    second = grads[..., half:]
    return jnp.concatenate([first * cosine + second * sine, second * cosine - first * sine], -1)


def plain_mask(seg_rows, head_ids, length):
    place = jnp.arange(length, dtype=jnp.int32)
    dist = place[:, None] - place[None, :]
    same = (seg_rows[:, :, None] == seg_rows[:, None, :]) & (dist >= 0)[None]
    rates = jnp.log1p(-(2.0 ** (-5.0 - head_ids)))
    decay = jnp.exp(jnp.maximum(dist, 0).astype(jnp.float32)[None] * rates[:, None, None])
    return jnp.where(same[:, None], decay[None], 0.0)


def weights_of(rotated_query, rotated_key, mask, score_scale):
    unnormalized_scores = (
        jnp.einsum(
            "slhd,smhd->shlm", rotated_query, rotated_key, preferred_element_type=jnp.float32
        )
        * score_scale
    )
    return (unnormalized_scores * mask).astype(jnp.bfloat16)


def gather_rows(rows):
    return lax.all_gather(rows, "tensor", axis=0, tiled=True)


def sum_rows(part):
    return lax.psum_scatter(
        part.astype(jnp.bfloat16), "tensor", scatter_dimension=0, tiled=True
    ).astype(jnp.float32)


def fold_rows(acts, weights):
    pieces = jax.tree.map(lambda a: lax.all_gather(a, "dp", axis=0, tiled=True), shortened(weights))
    return tuple((jnp.dot(acts, p, preferred_element_type=jnp.float32) for p in pieces))


def map_columns(acts, weight):
    return jnp.dot(
        acts, lax.all_gather(weight, "dp", axis=1, tiled=True), preferred_element_type=jnp.float32
    )


def back_rows(grads, weights):
    pieces = lax.all_gather(shortened(weights), "dp", axis=0, tiled=True)
    total = lax.dot_general(grads[0], pieces[0], CONTRACT_COLS, preferred_element_type=jnp.float32)
    for grad, piece in zip(grads[1:], pieces[1:]):
        total = total + lax.dot_general(
            grad, piece, CONTRACT_COLS, preferred_element_type=jnp.float32
        )
    return total


def back_columns(grad, weight):
    return lax.dot_general(
        grad,
        lax.all_gather(weight, "dp", axis=1, tiled=True),
        CONTRACT_COLS,
        preferred_element_type=jnp.float32,
    )


def plain(
    tokens,
    segments,
    attn_gain,
    w_query,
    w_key,
    w_value,
    w_swish,
    w_output,
    ffn_gain,
    w_gelu,
    w_up,
    w_down,
    cotangent,
):
    layers = w_query.shape[0]
    heads_dev = w_query.shape[2] // HEAD_QK
    seqs = segments.shape[0] // LEN
    score_scale = HEAD_QK ** (-0.5)
    head_ids = (lax.axis_index("tensor") * heads_dev + jnp.arange(heads_dev)).astype(jnp.float32)
    mask = plain_mask(segments.reshape(seqs, LEN), head_ids, LEN)
    cosine, sine = plain_rotation(LEN, HEAD_QK)
    residual = tokens.astype(jnp.float32)
    saved = []
    for layer in range(layers):
        attn_in = (w_query[layer], w_key[layer], w_value[layer], w_swish[layer])
        ffn_in = (w_gelu[layer], w_up[layer])
        whole_in = attn_in + ffn_in
        whole_out = (w_output[layer], w_down[layer])
        normed = gather_rows(norm_rows(residual, attn_gain[layer]).astype(jnp.bfloat16))
        rows_all = normed.shape[0]
        query, keys, values, swish = fold_rows(normed, attn_in)
        vals = values.astype(jnp.bfloat16).reshape(seqs, LEN, heads_dev, HEAD_V)
        rotated_query = rotate(query.reshape(seqs, LEN, heads_dev, HEAD_QK), cosine, sine).astype(
            jnp.bfloat16
        )
        rotated_key = rotate(keys.reshape(seqs, LEN, heads_dev, HEAD_QK), cosine, sine).astype(
            jnp.bfloat16
        )
        probs = weights_of(rotated_query, rotated_key, mask, score_scale)
        mixed = jnp.einsum("shlm,smhv->slhv", probs, vals, preferred_element_type=jnp.float32)
        zed = norm_heads(mixed).reshape(rows_all, -1)
        gated = (jax.nn.silu(swish) * zed).astype(jnp.bfloat16)
        branch = map_columns(gated, w_output[layer])
        mid = residual + sum_rows(branch)
        normed_ffn = gather_rows(norm_rows(mid, ffn_gain[layer]).astype(jnp.bfloat16))
        gate_pre, up_pre = fold_rows(normed_ffn, ffn_in)
        hidden = (gelu_tanh(gate_pre) * up_pre).astype(jnp.bfloat16)
        branch_ffn = map_columns(hidden, w_down[layer])
        saved.append(
            (
                residual,
                normed,
                rotated_query,
                rotated_key,
                vals,
                swish,
                mixed,
                zed,
                gated,
                mid,
                normed_ffn,
                gate_pre,
                up_pre,
                hidden,
                whole_in,
                whole_out,
            )
        )
        residual = mid + sum_rows(branch_ffn)
    output = residual.astype(jnp.bfloat16)
    grad_res = cotangent.astype(jnp.float32)
    weight_parts = [None] * layers
    attn_gain_parts = [None] * layers
    ffn_gain_parts = [None] * layers
    for layer in reversed(range(layers)):
        (
            x_in,
            normed,
            rotated_query,
            rotated_key,
            vals,
            swish,
            mixed,
            zed,
            gated,
            mid,
            normed_ffn,
            gate_pre,
            up_pre,
            hidden,
            whole_in,
            whole_out,
        ) = saved[layer]
        attn_in = (w_query[layer], w_key[layer], w_value[layer], w_swish[layer])
        ffn_in = (w_gelu[layer], w_up[layer])
        rows_all = normed.shape[0]
        grad_c = gather_rows(grad_res.astype(jnp.bfloat16))
        down_grad = lax.dot_general(
            grad_c, hidden, CONTRACT_ROWS, preferred_element_type=jnp.float32
        )
        grad_hidden = back_columns(grad_c, w_down[layer])
        gelu_val, gelu_activation = jax.vjp(gelu_tanh, gate_pre)
        grad_gate = gelu_activation(grad_hidden * up_pre)[0].astype(jnp.bfloat16)
        grad_upv = (grad_hidden * gelu_val).astype(jnp.bfloat16)
        gelu_grad = lax.dot_general(
            normed_ffn, grad_gate, CONTRACT_ROWS, preferred_element_type=jnp.float32
        )
        up_grad = lax.dot_general(
            normed_ffn, grad_upv, CONTRACT_ROWS, preferred_element_type=jnp.float32
        )
        grad_nf = back_rows((grad_gate, grad_upv), ffn_in)
        _, ffn_norm_fn = jax.vjp(norm_rows, mid, ffn_gain[layer])
        grad_mid_norm, ffn_gain_parts[layer] = ffn_norm_fn(sum_rows(grad_nf))
        grad_mid = grad_res + grad_mid_norm
        grad_b = gather_rows(grad_mid.astype(jnp.bfloat16))
        output_grad_t = lax.dot_general(
            grad_b, gated, CONTRACT_ROWS, preferred_element_type=jnp.float32
        )
        grad_gated = back_columns(grad_b, w_output[layer])
        swish_output, swish_fn = jax.vjp(jax.nn.silu, swish)
        grad_sw = swish_fn(grad_gated * zed)[0].astype(jnp.bfloat16)
        grad_zed = grad_gated * swish_output
        _, head_fn = jax.vjp(norm_heads, mixed)
        grad_mixed = head_fn(grad_zed.reshape(mixed.shape))[0].astype(jnp.bfloat16)
        probs = weights_of(rotated_query, rotated_key, mask, score_scale)
        grad_probs = jnp.einsum(
            "slhv,smhv->shlm", grad_mixed, vals, preferred_element_type=jnp.float32
        )
        grad_raw = (grad_probs * mask).astype(jnp.bfloat16)
        grad_vals = jnp.einsum(
            "shlm,slhv->smhv", probs, grad_mixed, preferred_element_type=jnp.float32
        )
        grad_vals = grad_vals.astype(jnp.bfloat16).reshape(rows_all, -1)
        grad_qrot = (
            jnp.einsum("shlm,smhd->slhd", grad_raw, rotated_key, preferred_element_type=jnp.float32)
            * score_scale
        )
        grad_krot = (
            jnp.einsum(
                "shlm,slhd->smhd", grad_raw, rotated_query, preferred_element_type=jnp.float32
            )
            * score_scale
        )
        grad_q = rotate_back(grad_qrot, cosine, sine).astype(jnp.bfloat16).reshape(rows_all, -1)
        grad_k = rotate_back(grad_krot, cosine, sine).astype(jnp.bfloat16).reshape(rows_all, -1)
        attn_grads = tuple(
            (
                lax.dot_general(normed, g, CONTRACT_ROWS, preferred_element_type=jnp.float32)
                for g in (grad_q, grad_k, grad_vals, grad_sw)
            )
        )
        grad_n = back_rows((grad_q, grad_k, grad_vals, grad_sw), attn_in)
        _, attn_norm_fn = jax.vjp(norm_rows, x_in, attn_gain[layer])
        grad_x_norm, attn_gain_parts[layer] = attn_norm_fn(sum_rows(grad_n))
        grad_res = grad_mid + grad_x_norm
        weight_parts[layer] = jax.tree.map(
            lambda part: part.astype(jnp.float32),
            lax.psum_scatter(
                shortened(attn_grads + (output_grad_t, gelu_grad, up_grad, down_grad)),
                "dp",
                scatter_dimension=0,
                tiled=True,
            ),
        )
    attn_gain_grad, ffn_gain_grad = lax.psum(
        (jnp.stack(attn_gain_parts), jnp.stack(ffn_gain_parts)), ("dp", "tensor")
    )
    grad_query = jnp.stack([p[0] for p in weight_parts])
    grad_key = jnp.stack([p[1] for p in weight_parts])
    grad_value = jnp.stack([p[2] for p in weight_parts])
    grad_swish = jnp.stack([p[3] for p in weight_parts])
    grad_output = jnp.stack([p[4].T for p in weight_parts])
    grad_gelu = jnp.stack([p[5] for p in weight_parts])
    grad_up = jnp.stack([p[6] for p in weight_parts])
    grad_down = jnp.stack([p[7].T for p in weight_parts])
    return (
        output,
        grad_res,
        attn_gain_grad,
        grad_query,
        grad_key,
        grad_value,
        grad_swish,
        grad_output,
        ffn_gain_grad,
        grad_gelu,
        grad_up,
        grad_down,
    )


def grouped(
    tokens, segments, attn_gain, w_query, w_key, w_value, w_swish, w_output, ffn_gain, w_gelu, w_up, w_down, cotangent
):
    layers = w_query.shape[0]
    mask, cosine, sine, units, total = setup(segments, w_query, w_value, w_gelu)
    turn = lambda w: jnp.swapaxes(w, 1, 2)
    weights = (
        turn(w_query), turn(w_key), turn(w_value), turn(w_swish), w_output, turn(w_gelu), turn(w_up), w_down,
    )
    dims = (layers, tokens.shape[0], w_query.shape[1], units, HEAD_QK ** (-0.5))
    output, x_mid, mids, *kept = run_forward(
        dims, total, tokens, cotangent, mask, cosine, sine, attn_gain, ffn_gain, weights
    )
    input_grad, gains, parts = run_backward(
        dims, cotangent, tokens, x_mid, mids, mask, cosine, sine, attn_gain, ffn_gain, kept
    )
    q, k, v, s, o, g, u, d = unstack_grads(units, parts)
    return (
        output, input_grad, gains[:layers], q, k, turn(v), turn(s), o, gains[layers : 2 * layers], turn(g), turn(u), d,
    )


def solution(mesh):
    rows = P(("dp", "tensor"), None)
    up, down = P(None, "dp", "tensor"), P(None, "tensor", "dp")
    in_specs = (rows, P("dp"), P(), up, up, up, up, down, P(), up, up, down, rows)
    out_specs = (rows, rows, P(), up, up, up, up, down, P(), up, up, down)
    step = grouped if (mesh.shape["dp"], mesh.shape["tensor"]) == (8, 4) else plain
    return jax.shard_map(step, mesh=mesh, in_specs=in_specs, out_specs=out_specs, check_vma=False)
```

```python
import functools

import jax
import jax.numpy as jnp
from jax import lax
from jax.experimental import pallas as pl
from jax.experimental.pallas import tpu as pltpu
from jax.sharding import PartitionSpec as P

HEAD_QK = 256
HEAD_V = 432
LEN = 512

EPS = 1e-06
HEAD_FLOOR = 1.0
NN = (((1,), (0,)), ((), ()))
NT = (((1,), (1,)), ((), ()))
TN = (((0,), (0,)), ((), ()))
MESH = pl.DeviceIdType.MESH
BF16 = jnp.bfloat16
F32 = jnp.float32
LOOK = 2
SCHED = (
    ("III", "P", "", "PI", "PI", "PI"),
    ("PI", "PI", "", "PI", "PI", ""),
    ("PI", "PI", "", "PI", "PI", "PI"),
    ("PI", "PI", "", "PI", "PI", ""),
    ("PI", "PI", "", "", ""),
)
COT_AFTER = "v"
CHUNKS = 2
VMEM_LIMIT = 60 * 1024 * 1024


def dot(a, b, dims=NN):
    return lax.dot_general(a, b, dims, preferred_element_type=F32)


def loop(steps, body):
    lax.fori_loop(0, steps, lambda i, c: (body(i), c)[1], 0)


class Place:
    def __init__(self):
        dp, tensor = lax.axis_index("dp"), lax.axis_index("tensor")
        self.dp, self.tensor = dp, tensor
        self.z, self.y = lax.div(dp, 2), lax.rem(dp, 2)
        self.x, self.c = lax.div(tensor, 2), lax.rem(tensor, 2)
        self.half = lax.rem(self.z, 2)
        self.zn = self.z + 1 - 2 * self.half

    def at(self, z=None, y=None, x=None, c=None):
        z = self.z if z is None else z
        y = self.y if y is None else y
        x = self.x if x is None else x
        c = self.c if c is None else c
        return (z * 2 + y, x * 2 + c)

    def zplus(self, d):
        return lax.rem(self.z + d + 4, 4)

    def sib(self):
        return self.at(c=1 - self.c)

    def xn(self):
        return self.at(x=1 - self.x)

    def yn(self):
        return self.at(y=1 - self.y)

    def znb(self):
        return self.at(z=self.zn)

    def peers(self):
        return [self.sib(), self.xn(), self.yn()] + [self.at(z=self.zplus(d)) for d in (1, 2, 3)]

    def greet(self):
        bar = pltpu.get_barrier_semaphore()
        peers = self.peers()
        for p in peers:
            pl.semaphore_signal(bar, inc=1, device_id=p, device_id_type=MESH)
        pl.semaphore_wait(bar, len(peers))


def remote(src, dst, ssem, rsem, dev):
    return pltpu.make_async_remote_copy(
        src_ref=src, dst_ref=dst, send_sem=ssem, recv_sem=rsem, device_id=dev, device_id_type=MESH
    )


def block(half, tensor, rows):
    return pl.ds(pl.multiple_of((half * 4 + tensor) * rows, rows), rows)


def part_of(r, at, n):
    return pl.ds(pl.multiple_of(r.start + at, n), n)


class Gather:
    def __init__(self, me, buf, rows, ssem, rsem):
        def move(k, half, x, dev, at=0, size=rows):
            r = part_of(block(half, x * 2 + me.c, rows), at, size)
            return remote(buf.at[r], buf.at[r], ssem.at[k], rsem.at[k], dev)

        n = rows // CHUNKS
        h, x = me.half, me.x
        self.me = me
        self.own_x = move(0, h, x, me.xn())
        self.own_s = move(1, h, x, me.sib())
        self.x_s = move(2, h, 1 - x, me.sib())
        self.z_s = move(3, 1 - h, x, me.sib())
        self.g_s = move(4, 1 - h, 1 - x, me.sib())
        self.own_z = [move(5 + i, h, x, me.znb(), i * n, n) for i in range(CHUNKS)]
        self.z_x = [move(5 + CHUNKS + i, 1 - h, x, me.xn(), i * n, n) for i in range(CHUNKS)]

    def begin(self):
        for m in self.own_z + [self.own_x, self.own_s]:
            m.start()

    def finish(self, first, second, fill=()):
        fill = list(fill)

        def step():
            if fill:
                fill.pop(0)()

        step()
        self.own_x.wait_recv()
        self.x_s.start()
        for a, b in zip(self.own_z, self.z_x):
            a.wait_recv()
            b.start()
        self.z_s.start()
        step()
        self.own_s.wait_recv()
        self.x_s.wait_recv()
        first(self.me.half)
        for m in self.z_x:
            m.wait_recv()
        self.g_s.start()
        step()
        self.z_s.wait_recv()
        self.g_s.wait_recv()
        second(1 - self.me.half)
        for m in self.own_z + self.z_x + [self.own_x, self.own_s, self.z_s, self.x_s, self.g_s]:
            m.wait_send()


def gather_acts(me, buf, rows, ssem, rsem, first, second, fill=()):
    g = Gather(me, buf, rows, ssem, rsem)
    g.begin()
    g.finish(first, second, fill)


def sum_acts(me, part, rows, sib_buf, x_buf, z_buf, ssem, rsem, body, fill=()):
    fill = list(fill)
    n = rows // CHUNKS

    def step():
        if fill:
            fill.pop(0)()

    h, x = me.half, me.x
    order = [(1 - h, 1 - x), (h, 1 - x), (1 - h, x), (h, x)]
    sibs = []
    for j, (hh, xx) in enumerate(order):
        m = remote(part.at[block(hh, xx * 2 + 1 - me.c, rows)], sib_buf.at[j], ssem.at[j], rsem.at[j], me.sib())
        m.start()
        sibs.append(m)
    step()
    small = 32

    def mine(j, at, size):
        hh, xx = order[j]
        return part_of(block(hh, xx * 2 + me.c, rows), at, size)

    def add(j, at, size, extra=None):
        def go(i):
            r = mine(j, at + i * small, small)
            k = pl.ds(pl.multiple_of(at + i * small, small), small)
            v = part[r, :].astype(F32) + sib_buf[j, k, :].astype(F32)
            if extra is not None:
                v = v + extra[k, :].astype(F32)
            part[r, :] = v.astype(BF16)

        loop(size // small, go)

    def cut(i):
        return pl.ds(i * n, n)

    g_x = [
        remote(part.at[mine(0, i * n, n)], x_buf.at[0, cut(i)], ssem.at[5 + i], rsem.at[5 + i], me.xn())
        for i in range(CHUNKS)
    ]
    x_x = remote(part.at[mine(1, 0, rows)], x_buf.at[1], ssem.at[4], rsem.at[4], me.xn())
    to_z = [
        remote(
            part.at[mine(2, i * n, n)], z_buf.at[cut(i)], ssem.at[5 + CHUNKS + i], rsem.at[5 + CHUNKS + i], me.znb()
        )
        for i in range(CHUNKS)
    ]
    sibs[0].wait_recv()
    for i in range(CHUNKS):
        add(0, i * n, n)
        g_x[i].start()
    sibs[1].wait_recv()
    add(1, 0, rows)
    x_x.start()
    step()
    sibs[2].wait_recv()
    for i in range(CHUNKS):
        g_x[i].wait_recv()
        add(2, i * n, n, x_buf.at[0])
        to_z[i].start()
    sibs[3].wait_recv()
    step()
    x_x.wait_recv()
    for m in to_z:
        m.wait_recv()

    def last(i):
        k = pl.ds(pl.multiple_of(i * small, small), small)
        v = part[mine(3, i * small, small), :].astype(F32) + sib_buf[3, k, :].astype(F32)
        v = v + x_buf[1, k, :].astype(F32) + z_buf[k, :].astype(F32)
        body(i * small, small, v)

    loop(rows // small, last)
    for m in sibs + g_x + to_z + [x_x]:
        m.wait_send()
    while fill:
        step()


def unit_rows(qk, val, ffn):
    sizes = (("q", qk), ("k", qk), ("v", val), ("s", val), ("o", val), ("g", ffn), ("u", ffn), ("d", ffn))
    out, at = {}, 0
    for name, n in sizes:
        out[name] = (at, n)
        at += n
    return out, at


def rms(v, floor):
    return lax.rsqrt(jnp.mean(v * v, -1, keepdims=True) + floor)


def forward_kernel(
    dims,
    tokens, cot, mask, cosine, sine, attn_gain, ffn_gain, w_q, w_k, w_v, w_s, w_o, w_g, w_u, w_d,
    output, x_mid, mids, wf, s_gc, s_n, s_nf, s_q, s_k, s_v, s_s, s_m, s_gt, s_g, s_u, s_h, s_p,
    W, N0, N1, part, sib_buf, x_buf, z_buf, q, k, v, s, m, gt, g, u, h, p,
    zs, zr, ys, yr, lo, ld, ags, agr, rss, rsr, sv,
):
    layers, rows, lanes, units, scale = dims
    me = Place()
    names = list(units)
    shards = dict(q=w_q, k=w_k, v=w_v, s=w_s, o=w_o, g=w_g, u=w_u, d=w_d)
    groups = [(l, units[n]) for l in range(layers) for n in names]
    spot = {(l, n): l * len(names) + i for l in range(layers) for i, n in enumerate(names)}
    my_lane = pl.multiple_of(me.dp * lanes, lanes)

    def shard(i, half):
        n = groups[i][1][1]
        return shards[names[i % len(names)]].at[groups[i][0], pl.ds(pl.multiple_of(half * n, 16), n)]

    def z_copy(i, d):
        l, (r0, n) = groups[i]
        tz = me.zplus(d)
        return remote(
            shard(i, lax.rem(tz, 2)), wf.at[l, pl.ds(r0, n), pl.ds(my_lane, lanes)],
            zs.at[i, d - 1], zr.at[i, d - 1], me.at(z=tz),
        )

    def y_copy(i, d):
        l, (r0, n) = groups[i]
        lane = pl.ds(pl.multiple_of((me.zplus(-d) * 2 + me.y) * lanes, lanes), lanes)
        dst = wf.at[l, pl.ds(r0, n), lane]
        src = shard(i, me.half) if d == 0 else dst
        return remote(src, dst, ys.at[i, d], yr.at[i, d], me.yn())

    def local_copy(i):
        l, (r0, n) = groups[i]
        return pltpu.make_async_copy(
            shard(i, me.half), wf.at[l, pl.ds(r0, n), pl.ds(my_lane, lanes)], lo.at[i]
        )

    def issue(i):
        if i < len(groups):
            for d in (1, 2, 3):
                z_copy(i, d).start()
            y_copy(i, 0).start()
            local_copy(i).start()

    issued, pumped = [0], [0]

    def send_next():
        if issued[0] < len(groups):
            issue(issued[0])
            issued[0] += 1

    def pass_on():
        i = pumped[0]
        if i >= len(groups):
            return
        while issued[0] <= i:
            send_next()
        pumped[0] += 1
        for d in (1, 3, 2):
            z_copy(i, d).wait_recv()
            y_copy(i, d).start()

    plan = SCHED

    def act(pair, point):
        def go():
            for ch in plan[pair][point]:
                if ch == "I":
                    send_next()
                if ch == "P":
                    pass_on()
        return go

    def gfill(pair):
        return [act(pair, 0), act(pair, 1), act(pair, 5)]

    def sfill(pair):
        return [act(pair, 2), act(pair, 3), act(pair, 4)]

    def take(l, *wanted):
        idx = [spot[l, n] for n in wanted]
        while pumped[0] <= idx[-1]:
            pass_on()
            while issued[0] - pumped[0] < LOOK:
                if issued[0] >= len(groups):
                    break
                send_next()
        copies = []
        for i in idx:
            for d in range(4):
                y_copy(i, d).wait_recv()
            local_copy(i).wait()
            r0, n = groups[i][1]
            c = pltpu.make_async_copy(wf.at[l, pl.ds(r0, n)], W.at[pl.ds(r0, n)], ld.at[i])
            c.start()
            copies.append(c)
        for c in copies:
            c.wait()

    saves = []

    def save(src, dst):
        c = pltpu.make_async_copy(src, dst, sv.at[len(saves)])
        c.start()
        saves.append(c)

    waited = [0]

    def settle():
        while waited[0] < len(saves):
            saves[waited[0]].wait()
            waited[0] += 1

    def weight(n):
        r0, size = units[n]
        return W[pl.ds(r0, size), :]

    def seq_rows(i):
        return pl.ds(pl.multiple_of(i * LEN, LEN), LEN)

    seqs = 2
    own = (me.half * 4 + me.tensor) * rows

    def own_rows(r0, n):
        return pl.ds(pl.multiple_of(own + r0, n), n)

    me.greet()
    small = 32

    def first_norm(i):
        r = pl.ds(pl.multiple_of(i * small, small), small)
        x = tokens[r, :].astype(F32)
        N0[own_rows(i * small, small), :] = (x * rms(x, EPS) * attn_gain[0:1, :]).astype(BF16)
        N1[own_rows(i * small, small), :] = cot[r, :]

    loop(rows // small, first_norm)
    def out_rows(i, src, name):
        def go(j):
            r = pl.ds(pl.multiple_of(i * LEN + j * 256, 256), 256)
            part[r, :] = dot(src[r, :], weight(name)).astype(BF16)

        loop(LEN // 256, go)

    def turned(name, dst, i):
        r = seq_rows(i)
        t = dot(N0[r, :], weight(name), NT)
        half = t.shape[1] // 2
        t1, t2 = t[:, :half], t[:, half:]
        c, sn = cosine[...], sine[...]
        dst[r, :half] = (t1 * c - t2 * sn).astype(BF16)
        dst[r, half:] = (t2 * c + t1 * sn).astype(BF16)

    def retain(i):
        r = seq_rows(i)
        v[r, :] = dot(N0[r, :], weight("v"), NT).astype(BF16)
        raw = dot(q[r, :], k[r, :], NT) * scale
        probs = (raw * mask[i]).astype(BF16)
        p[i] = probs
        m[r, :] = dot(probs, v[r, :])

    def gate(i):
        r = seq_rows(i)
        t = dot(N0[r, :], weight("s"), NT)
        s[r, :] = t
        mix = m[r, :]
        gt[r, :] = (jax.nn.silu(t) * (mix * rms(mix, HEAD_FLOOR))).astype(BF16)

    stages = (
        ("q", functools.partial(turned, "q", q)), ("k", functools.partial(turned, "k", k)), ("v", retain),
        ("s", gate), ("o", lambda i: out_rows(i, gt, "o")),
    )

    def attn_seq(i, l, fetch):
        for name, stage in stages:
            if fetch:
                take(l, name)
            stage(i)

    def ffn_seq(i, l, fetch):
        r = seq_rows(i)
        if fetch:
            take(l, "g")
        g[r, :] = dot(N1[r, :], weight("g"), NT)
        if fetch:
            take(l, "u")
        t = dot(N1[r, :], weight("u"), NT)
        u[r, :] = t
        h[r, :] = (jax.nn.gelu(g[r, :], approximate=True) * t).astype(BF16)
        if fetch:
            take(l, "d")
        out_rows(i, h, "d")

    both = lambda body, l: (functools.partial(body, l=l, fetch=True), functools.partial(body, l=l, fetch=False))

    for l in range(layers):
        if l:
            gather_acts(me, N0, rows, ags.at[2 * l], agr.at[2 * l], *both(attn_seq, l), gfill(2 * l))
        else:
            own_rows_of = Gather(me, N0, rows, ags.at[0], agr.at[0])
            grads_of = Gather(me, N1, rows, ags.at[2 * layers], agr.at[2 * layers])
            own_rows_of.begin()
            act(0, 0)()
            grads_of.begin()
            idle = lambda i: None
            own_rows_of.finish(idle, idle, [act(0, 1), act(0, 5), act(2 * layers, 3)])
            for name, stage in stages:
                take(0, name)
                loop(seqs, stage)
                if name == COT_AFTER:
                    grads_of.finish(idle, idle, [act(2 * layers, i) for i in (0, 1, 2)])
                    save(N1, s_gc)
        for src, dst in ((N0, s_n), (q, s_q), (k, s_k), (v, s_v), (p, s_p), (m, s_m), (s, s_s), (gt, s_gt)):
            save(src, dst.at[l])

        if l == 0:
            saves[0].wait()
            waited[0] = 1

        def to_mid(r0, n, total, l=l):
            r = pl.ds(pl.multiple_of(r0, n), n)
            x = (tokens[r, :].astype(F32) if l == 0 else x_mid[l - 1, r, :]) + total
            mids[l, r, :] = x
            N1[own_rows(r0, n), :] = (x * rms(x, EPS) * ffn_gain[l : l + 1, :]).astype(BF16)

        sum_acts(me, part, rows, sib_buf, x_buf, z_buf, rss.at[2 * l], rsr.at[2 * l], to_mid, sfill(2 * l))
        gather_acts(me, N1, rows, ags.at[2 * l + 1], agr.at[2 * l + 1], *both(ffn_seq, l), gfill(2 * l + 1))
        for src, dst in ((N1, s_nf), (g, s_g), (u, s_u), (h, s_h)):
            save(src, dst.at[l])

        def to_next(r0, n, total, l=l):
            r = pl.ds(pl.multiple_of(r0, n), n)
            x = mids[l, r, :] + total
            if l + 1 < layers:
                x_mid[l, r, :] = x
                N0[own_rows(r0, n), :] = (x * rms(x, EPS) * attn_gain[l + 1 : l + 2, :]).astype(BF16)
            else:
                output[r, :] = x.astype(BF16)

        settle()
        sum_acts(me, part, rows, sib_buf, x_buf, z_buf, rss.at[2 * l + 1], rsr.at[2 * l + 1], to_next, sfill(2 * l + 1))
    settle()
    for i in range(len(groups)):
        for d in (1, 2, 3):
            z_copy(i, d).wait_send()
        for d in range(4):
            y_copy(i, d).wait_send()


def run_forward(dims, total, tokens, cot, mask, cosine, sine, attn_gain, ffn_gain, weights):
    layers, rows, lanes, units, scale = dims
    depth = tokens.shape[1]
    group = 8 * rows
    seqs = group // LEN
    qk, val, ffn = units["q"][1], units["v"][1], units["g"][1]
    vm = pl.BlockSpec(memory_space=pltpu.VMEM)
    hb = pl.BlockSpec(memory_space=pl.ANY)
    outs = [
        ((rows, depth), BF16), ((layers - 1, rows, depth), F32), ((layers, rows, depth), F32),
        ((layers, total, depth), BF16), ((group, depth), BF16),
        ((layers, group, depth), BF16), ((layers, group, depth), BF16),
        ((layers, group, qk), BF16), ((layers, group, qk), BF16), ((layers, group, val), BF16),
        ((layers, group, val), F32), ((layers, group, val), F32), ((layers, group, val), BF16),
        ((layers, group, ffn), F32), ((layers, group, ffn), F32), ((layers, group, ffn), BF16),
        ((layers, seqs, LEN, LEN), BF16),
    ]
    n_groups = layers * len(units)
    dma = pltpu.SemaphoreType.DMA
    return pl.pallas_call(
        functools.partial(forward_kernel, dims),
        out_shape=[jax.ShapeDtypeStruct(s, d) for s, d in outs],
        in_specs=[vm] * 7 + [hb] * 8,
        out_specs=[vm] * 3 + [hb] * 14,
        scratch_shapes=[
            pltpu.VMEM((total, depth), BF16),
            pltpu.VMEM((group, depth), BF16), pltpu.VMEM((group, depth), BF16), pltpu.VMEM((group, depth), BF16),
            pltpu.VMEM((4, rows, depth), BF16), pltpu.VMEM((2, rows, depth), BF16), pltpu.VMEM((rows, depth), BF16),
            pltpu.VMEM((group, qk), BF16), pltpu.VMEM((group, qk), BF16), pltpu.VMEM((group, val), BF16),
            pltpu.VMEM((group, val), F32), pltpu.VMEM((group, val), F32), pltpu.VMEM((group, val), BF16),
            pltpu.VMEM((group, ffn), F32), pltpu.VMEM((group, ffn), F32), pltpu.VMEM((group, ffn), BF16),
            pltpu.VMEM((seqs, LEN, LEN), BF16),
            dma((n_groups, 3)), dma((n_groups, 3)), dma((n_groups, 4)), dma((n_groups, 4)),
            dma((n_groups,)), dma((n_groups,)),
            *[dma((2 * layers + 1, 5 + 2 * CHUNKS)) for _ in range(4)],
            dma((12 * layers + 1,)),
        ],
        compiler_params=pltpu.CompilerParams(collective_id=0, has_side_effects=True, vmem_limit_bytes=VMEM_LIMIT),
    )(tokens, cot, mask, cosine, sine, attn_gain, ffn_gain, *weights)


SLOTS = 4
EARLY = 1
BSCHED = (
    ("", "", "", "", "M", "MM", ""),
    ("C", "C", "", "", "CMM", "CMCM", ""),
    ("C", "C", "C", "", "M", "MM", ""),
    ("C", "C", "", "", "CMM", "CMCM", ""),
)


def backward_kernel(
    dims,
    cot, tokens, x_mid, mids, mask, cosine, sine, attn_gain, ffn_gain,
    wf, s_gc, s_n, s_nf, s_q, s_k, s_v, s_s, s_m, s_gt, s_g, s_u, s_h, s_p,
    input_grad, gains, rz,
    gr, xb, nb, ga0, ga1, part, sib_buf, x_buf, z_buf, W, a1, a2, a3, q, k, v, p, t1, t2, tq, tk, G, ry, acc, acc_in,
    ys, yr, zs, zr, os, ags, agr, rss, rsr, ld, gns, gnr, credit,
):
    layers, rows, lanes, units, scale = dims
    me = Place()
    depth = cot.shape[1]
    wide = 512
    small = 32
    seqs = 2
    order = list(reversed(range(layers)))
    jobs = [(l, n) for l in order for n in ("d", "g", "u", "o", "s", "q", "k", "v")]
    index = {job: i for i, job in enumerate(jobs)}
    own = (me.half * 4 + me.tensor) * rows
    ffn_row = units["g"][0]
    attn_end = ffn_row
    total_rows = units["d"][0] + units["d"][1]

    def own_rows(r0, n):
        return pl.ds(pl.multiple_of(own + r0, n), n)

    def seq_rows(i):
        return pl.ds(pl.multiple_of(i * LEN, LEN), LEN)

    def lane(i):
        return pl.ds(pl.multiple_of(i * lanes, lanes), lanes)

    def y_send(i, d):
        n = units[jobs[i][1]][1]
        tz = me.zplus(d)
        return remote(
            G.at[i % SLOTS, pl.ds(0, n), lane(tz * 2 + 1 - me.y)], ry.at[i % SLOTS, pl.ds(0, n), lane(tz)],
            ys.at[i, d], yr.at[i, d], me.yn(),
        )

    def z_send(i, d):
        l, name = jobs[i]
        r0, n = units[name]
        tz = me.zplus(d)
        return remote(
            G.at[i % SLOTS, pl.ds(0, n), lane(tz * 2 + me.y)], rz.at[l, me.half, d // 2, pl.ds(r0, n)],
            zs.at[i, d - 1], zr.at[i, d - 1], me.at(z=tz),
        )

    def own_copy(i):
        l, name = jobs[i]
        r0, n = units[name]
        return pltpu.make_async_copy(
            G.at[i % SLOTS, pl.ds(0, n), lane(me.dp)], rz.at[l, me.half, 0, pl.ds(r0, n)], os.at[i]
        )

    def retire(i):
        for d in range(4):
            y_send(i, d).wait_send()
        for d in (1, 2, 3):
            z_send(i, d).wait_send()
        own_copy(i).wait()

    def make(l, name, left, right):
        i = index[l, name]
        n = units[name][1]
        if i >= SLOTS:
            retire(i - SLOTS)

        def go(j):
            cols = pl.ds(pl.multiple_of(j * wide, wide), wide)
            G[i % SLOTS, :n, cols] = dot(left[...], right[:, cols], TN).astype(BF16)

        loop(depth // wide, go)
        if i >= SLOTS:
            pl.semaphore_wait(credit.at[i % SLOTS], 1)
        for d in (2, 1, 3, 0):
            y_send(i, d).start()

    def combine(l, name):
        i = index[l, name]
        n = units[name][1]
        for d in (2, 1, 3, 0):
            y_send(i, d).wait_recv()
            tz = me.zplus(d)

            def add(j, tz=tz):
                r = pl.ds(pl.multiple_of(j * 16, 16), 16)
                c = lane(tz * 2 + me.y)
                both = G[i % SLOTS, r, c].astype(F32) + ry[i % SLOTS, r, lane(tz)].astype(F32)
                G[i % SLOTS, r, c] = both.astype(BF16)

            loop(n // 16, add)
            if d:
                z_send(i, d).start()
            else:
                own_copy(i).start()
        if i + SLOTS < len(jobs):
            pl.semaphore_signal(credit.at[i % SLOTS], inc=1, device_id=me.yn(), device_id_type=MESH)

    spots = {}

    def load(key, src, dst):
        c = pltpu.make_async_copy(src, dst, ld.at[len(spots)])
        c.start()
        spots[key] = c

    def ready(*keys):
        for key in keys:
            spots[key].wait()

    def load_ffn(l):
        load(("wf", l), wf.at[l, pl.ds(ffn_row, total_rows - ffn_row)], W.at[pl.ds(0, total_rows - ffn_row)])
        load(("g", l), s_g.at[l], a1)
        load(("u", l), s_u.at[l], a2)

    def load_attn(l):
        load(("wa", l), wf.at[l, pl.ds(0, attn_end)], W.at[pl.ds(0, attn_end)])
        load(("s", l), s_s.at[l], a1)
        load(("m", l), s_m.at[l], a2)
        load(("q", l), s_q.at[l], q)
        load(("k", l), s_k.at[l], k)
        load(("v", l), s_v.at[l], v)
        load(("p", l), s_p.at[l], p)

    def load_mid(l):
        load(("mid", l), mids.at[l], xb)

    def load_h(l):
        load(("h", l), s_h.at[l], a3)

    def load_nf(l):
        load(("nf", l), s_nf.at[l], nb)

    def load_gt(l):
        load(("gt", l), s_gt.at[l], a3)

    def load_n(l):
        load(("n", l), s_n.at[l], nb)

    def weight(name, base):
        r0, n = units[name]
        return W[pl.ds(r0 - base, n), :]

    def norm_back(x, gain, dn, gain_row):
        e = rms(x, EPS)
        gx = dn * gain
        inner = jnp.sum(gx * x, -1, keepdims=True)
        acc[0, gain_row : gain_row + 1, :] += jnp.sum(dn * x * e, 0, keepdims=True)
        return e * gx - (e * e * e) * x * (inner / depth)

    me.greet()
    load("gc", s_gc, ga0)
    load_ffn(order[0])
    load_mid(order[0])
    load_h(order[0])
    load_nf(order[0])
    acc[0] = jnp.zeros(acc.shape[1:], F32)

    def begin(i):
        r = pl.ds(pl.multiple_of(i * small, small), small)
        gr[r, :] = cot[r, :].astype(F32)

    loop(rows // small, begin)

    jobs_of = {
        "d": (a3, ga0, ("h",), lambda l: load_gt(l)),
        "g": (t1, nb, ("nf",), None),
        "u": (t2, nb, (), lambda l: load_n(l)),
        "o": (a3, ga1, ("gt",), None),
        "s": (t2, nb, ("n",), None),
        "q": (tq, nb, (), None),
        "k": (tk, nb, (), None),
        "v": (t1, nb, (), lambda l: (load_nf(l - 1), load_h(l - 1)) if l else None),
    }
    open_to, made, added = [0], [0], [0]

    def add_next():
        if added[0] < made[0]:
            combine(*jobs[added[0]])
            added[0] += 1

    def make_next():
        if made[0] < open_to[0]:
            i = made[0]
            while added[0] <= i - SLOTS:
                add_next()
            l, name = jobs[i]
            left, right, needs, then = jobs_of[name]
            ready(*((key, l) for key in needs))
            make(l, name, left, right)
            made[0] += 1
            if then:
                then(l)

    def make_all():
        while made[0] < open_to[0]:
            make_next()

    plan = BSCHED

    def act(pair, point):
        def go():
            for ch in plan[pair][point]:
                if ch == "M":
                    make_next()
                if ch == "C":
                    add_next()

        return go

    def gfill(pair):
        return [act(pair, i) for i in (0, 1, 2)]

    def sfill(pair):
        return [act(pair, i) for i in (3, 4, 5, 6)]

    def tile_rows(i, j):
        return pl.ds(pl.multiple_of(i * LEN + j * 256, 256), 256)

    def ffn_seq(i):
        def go(j):
            r = tile_rows(i, j)
            gh = dot(ga0[r, :], weight("d", ffn_row), NT)
            g, u = a1[r, :], a2[r, :]
            th = jnp.tanh(0.7978845608028654 * (g + 0.044715 * g * g * g))
            val = 0.5 * g * (1.0 + th)
            slope = 0.5 * (1.0 + th) + 0.5 * g * (1.0 - th * th) * (0.7978845608028654 * (1.0 + 0.134145 * g * g))
            t1[r, :] = (gh * u * slope).astype(BF16)
            t2[r, :] = (gh * val).astype(BF16)
            part[r, :] = (dot(t1[r, :], weight("g", ffn_row)) + dot(t2[r, :], weight("u", ffn_row))).astype(BF16)

        loop(LEN // 256, go)

    def attn_head(i):
        def go(j):
            r = tile_rows(i, j)
            gg = dot(ga1[r, :], weight("o", 0), NT)
            s, mix = a1[r, :], a2[r, :]
            sig = 1.0 / (1.0 + jnp.exp(-s))
            rr = rms(mix, HEAD_FLOOR)
            t2[r, :] = (gg * (mix * rr) * (sig * (1.0 + s * (1.0 - sig)))).astype(BF16)
            gz = gg * (s * sig)
            inner = jnp.sum(gz * mix, -1, keepdims=True) / mix.shape[1]
            t1[r, :] = (rr * gz - (rr * rr * rr) * mix * inner).astype(BF16)

        loop(LEN // 256, go)

    def attn_tail(i):
        r = seq_rows(i)
        gm = t1[r, :]
        raw = (dot(gm, v[r, :], NT) * mask[i]).astype(BF16)
        t1[r, :] = dot(p[i], gm, TN).astype(BF16)
        c, sn = cosine[...], sine[...]
        for dst, grad in ((tq, dot(raw, k[r, :]) * scale), (tk, dot(raw, q[r, :], TN) * scale)):
            half = grad.shape[1] // 2
            g1, g2 = grad[:, :half], grad[:, half:]
            dst[r, :half] = (g1 * c + g2 * sn).astype(BF16)
            dst[r, half:] = (g2 * c - g1 * sn).astype(BF16)

        def go(j):
            r = pl.ds(pl.multiple_of(i * LEN + j * 256, 256), 256)
            tot = dot(tq[r, :], weight("q", 0)) + dot(tk[r, :], weight("k", 0))
            tot = tot + dot(t1[r, :], weight("v", 0)) + dot(t2[r, :], weight("s", 0))
            part[r, :] = tot.astype(BF16)

        loop(LEN // 256, go)

    def attn_seq(i):
        attn_head(i)
        attn_tail(i)

    def attn_second(i, at):
        attn_head(i)
        open_to[0] = 8 * at + 3 + EARLY
        make_all()
        attn_tail(i)

    def after(keys, body):
        def go(i):
            make_all()
            ready(*keys)
            body(i)

        return go

    for at, l in enumerate(order):
        last = at == layers - 1
        first = after([("wf", l), ("g", l), ("u", l), ("mid", l)], ffn_seq)
        if at == 0:
            ready("gc")
            first(0)
            ffn_seq(1)
        else:
            gather_acts(me, ga0, rows, ags.at[2 * at], agr.at[2 * at], first, ffn_seq, gfill(2 * at))
        load_attn(l)
        open_to[0] = 8 * at + 3

        def to_mid(r0, n, tot, l=l):
            r = pl.ds(pl.multiple_of(r0, n), n)
            new = gr[r, :] + norm_back(xb[r, :], ffn_gain[l : l + 1, :], tot, layers + l)
            gr[r, :] = new
            ga1[own_rows(r0, n), :] = new.astype(BF16)

        sum_acts(me, part, rows, sib_buf, x_buf, z_buf, rss.at[2 * at], rsr.at[2 * at], to_mid, sfill(2 * at))
        if l:
            load(("x", l), x_mid.at[l - 1], xb)
        first = after([(key, l) for key in ("wa", "s", "m", "q", "k", "v", "p") + (("x",) if l else ())], attn_seq)
        gather_acts(me, ga1, rows, ags.at[2 * at + 1], agr.at[2 * at + 1], first, functools.partial(attn_second, at=at), gfill(2 * at + 1))
        if not last:
            load_ffn(order[at + 1])
        open_to[0] = 8 * at + 8

        def to_prev(r0, n, tot, l=l, last=last):
            r = pl.ds(pl.multiple_of(r0, n), n)
            x = tokens[r, :].astype(F32) if l == 0 else xb[r, :]
            new = gr[r, :] + norm_back(x, attn_gain[l : l + 1, :], tot, l)
            if last:
                input_grad[r, :] = new
            else:
                gr[r, :] = new
                ga0[own_rows(r0, n), :] = new.astype(BF16)

        sum_acts(
            me, part, rows, sib_buf, x_buf, z_buf, rss.at[2 * at + 1], rsr.at[2 * at + 1], to_prev, sfill(2 * at + 1)
        )
        if not last:
            load_mid(order[at + 1])

    make_all()
    while added[0] < made[0]:
        add_next()
    partners = [me.sib(), me.xn(), me.yn(), me.znb(), me.at(z=me.zplus(2))]
    for j, dev in enumerate(partners):
        m = remote(acc.at[j], acc_in.at[j], gns.at[j], gnr.at[j], dev)
        m.start()
        m.wait()
        acc[j + 1] = acc[j] + acc_in[j]
    gains[...] = acc[len(partners)]
    for i in range(len(jobs) - SLOTS, len(jobs)):
        retire(i)
    for i in range(len(jobs)):
        for d in (1, 2, 3):
            z_send(i, d).wait_recv()


def run_backward(dims, cot, tokens, x_mid, mids, mask, cosine, sine, attn_gain, ffn_gain, kept):
    layers, rows, lanes, units, scale = dims
    depth = tokens.shape[1]
    total = kept[0].shape[1]
    group = 8 * rows
    seqs = group // LEN
    qk, val, ffn = units["q"][1], units["v"][1], units["g"][1]
    vm = pl.BlockSpec(memory_space=pltpu.VMEM)
    hb = pl.BlockSpec(memory_space=pl.ANY)
    outs = [((rows, depth), F32), ((8, depth), F32), ((layers, 2, 2, total, lanes), BF16)]
    jobs = layers * len(units)
    most = max(n for _, n in units.values())
    attn_rows = units["g"][0]
    dma = pltpu.SemaphoreType.DMA
    big = pltpu.VMEM((group, depth), BF16)
    return pl.pallas_call(
        functools.partial(backward_kernel, dims),
        out_shape=[jax.ShapeDtypeStruct(s, d) for s, d in outs],
        in_specs=[vm, vm, hb, hb] + [vm] * 5 + [hb] * 14,
        out_specs=[vm] * 2 + [hb],
        scratch_shapes=[
            pltpu.VMEM((rows, depth), F32), pltpu.VMEM((rows, depth), F32), big, big, big, big,
            pltpu.VMEM((4, rows, depth), BF16), pltpu.VMEM((2, rows, depth), BF16), pltpu.VMEM((rows, depth), BF16),
            pltpu.VMEM((max(attn_rows, total - attn_rows), depth), BF16),
            pltpu.VMEM((group, val), F32), pltpu.VMEM((group, val), F32), pltpu.VMEM((group, val), BF16),
            pltpu.VMEM((group, qk), BF16), pltpu.VMEM((group, qk), BF16), pltpu.VMEM((group, val), BF16),
            pltpu.VMEM((seqs, LEN, LEN), BF16),
            pltpu.VMEM((group, val), BF16), pltpu.VMEM((group, val), BF16),
            pltpu.VMEM((group, qk), BF16), pltpu.VMEM((group, qk), BF16),
            pltpu.VMEM((SLOTS, most, depth), BF16), pltpu.VMEM((SLOTS, most, depth // 2), BF16),
            pltpu.VMEM((6, 8, depth), F32), pltpu.VMEM((5, 8, depth), F32),
            dma((jobs, 4)), dma((jobs, 4)), dma((jobs, 3)), dma((jobs, 3)), dma((jobs,)),
            *[dma((2 * layers, 5 + 2 * CHUNKS)) for _ in range(4)],
            dma((16 * layers + 1,)), dma((5,)), dma((5,)), pltpu.SemaphoreType.REGULAR((SLOTS,)),
        ],
        compiler_params=pltpu.CompilerParams(collective_id=1, has_side_effects=True, vmem_limit_bytes=VMEM_LIMIT),
    )(cot, tokens, x_mid, mids, mask, cosine, sine, attn_gain, ffn_gain, *kept)


NAMES = ("q", "k", "v", "s", "o", "g", "u", "d")
TILE = 128


def unstack_kernel(units, parts, *outs):
    for name, out in zip(NAMES, outs):
        r0, n = units[name]
        both = [parts[0, h, 0, r0 : r0 + n].astype(F32) + parts[0, h, 1, r0 : r0 + n].astype(F32) for h in range(2)]
        if name in ("q", "k"):
            out[0] = jnp.concatenate(both, 0).T
        else:
            for h in range(2):
                out[0, h * n : (h + 1) * n] = both[h]


def unstack_grads(units, parts):
    layers, _, _, total, lanes = parts.shape
    shapes, specs = [], []
    for name in NAMES:
        n = 2 * units[name][1]
        if name in ("q", "k"):
            shapes.append((layers, lanes, n))
            specs.append(pl.BlockSpec((1, TILE, n), lambda l, j: (l, j, 0)))
        else:
            shapes.append((layers, n, lanes))
            specs.append(pl.BlockSpec((1, n, TILE), lambda l, j: (l, 0, j)))
    return pl.pallas_call(
        functools.partial(unstack_kernel, units),
        grid=(layers, lanes // TILE),
        in_specs=[pl.BlockSpec((1, 2, 2, total, TILE), lambda l, j: (l, 0, 0, 0, j))],
        out_specs=specs,
        out_shape=[jax.ShapeDtypeStruct(s, F32) for s in shapes],
        compiler_params=pltpu.CompilerParams(vmem_limit_bytes=VMEM_LIMIT),
    )(parts)

def rotation(length, width):
    half = width // 2
    place = jnp.arange(length, dtype=F32)
    freqs = 10000.0 ** (-jnp.arange(half, dtype=F32) / half)
    angle = place[:, None] * freqs[None, :]
    return jnp.cos(angle), jnp.sin(angle)


def decay_mask(seg_rows, head, length):
    place = jnp.arange(length, dtype=jnp.int32)
    dist = place[:, None] - place[None, :]
    same = (seg_rows[:, :, None] == seg_rows[:, None, :]) & (dist >= 0)[None]
    rate = jnp.log1p(-(2.0 ** (-5.0 - head)))
    decay = jnp.exp(jnp.maximum(dist, 0).astype(F32) * rate)
    return jnp.where(same, decay[None], 0.0)


def setup(segments, w_query, w_value, w_gelu):
    dp, tensor = lax.axis_index("dp"), lax.axis_index("tensor")
    half = (dp // 2) % 2
    other = lax.ppermute(segments, "dp", [(i, i ^ 2) for i in range(8)])
    pair = jnp.where(half == 0, jnp.stack([segments, other]), jnp.stack([other, segments]))
    mask = decay_mask(pair, (tensor * 2 + half).astype(F32), LEN)
    cosine, sine = rotation(LEN, HEAD_QK)
    units, total = unit_rows(w_query.shape[2] // 2, w_value.shape[2] // 2, w_gelu.shape[2] // 2)
    return mask, cosine, sine, units, total


CONTRACT_ROWS = (((0,), (0,)), ((), ()))
CONTRACT_COLS = (((1,), (1,)), ((), ()))


def shortened(shard):
    return jax.tree.map(lambda a: a.astype(jnp.bfloat16) if a.dtype == jnp.float32 else a, shard)


def norm_rows(values, gain):
    return values * lax.rsqrt(jnp.mean(values * values, -1, keepdims=True) + EPS) * gain


def norm_heads(values):
    return values * lax.rsqrt(jnp.mean(values * values, -1, keepdims=True) + HEAD_FLOOR)


def gelu_tanh(values):
    return jax.nn.gelu(values, approximate=True)


def plain_rotation(length, width):
    half = width // 2
    place = jnp.arange(length, dtype=jnp.float32)
    freqs = 10000.0 ** (-jnp.arange(half, dtype=jnp.float32) / half)
    angle = place[:, None] * freqs[None, :]
    return (jnp.cos(angle)[:, None, :], jnp.sin(angle)[:, None, :])


def rotate(values, cosine, sine):
    half = values.shape[-1] // 2
    first = values[..., :half]
    second = values[..., half:]
    return jnp.concatenate([first * cosine - second * sine, second * cosine + first * sine], -1)


def rotate_back(grads, cosine, sine):
    half = grads.shape[-1] // 2
    first = grads[..., :half]
    second = grads[..., half:]
    return jnp.concatenate([first * cosine + second * sine, second * cosine - first * sine], -1)


def plain_mask(seg_rows, head_ids, length):
    place = jnp.arange(length, dtype=jnp.int32)
    dist = place[:, None] - place[None, :]
    same = (seg_rows[:, :, None] == seg_rows[:, None, :]) & (dist >= 0)[None]
    rates = jnp.log1p(-(2.0 ** (-5.0 - head_ids)))
    decay = jnp.exp(jnp.maximum(dist, 0).astype(jnp.float32)[None] * rates[:, None, None])
    return jnp.where(same[:, None], decay[None], 0.0)


def weights_of(rotated_query, rotated_key, mask, score_scale):
    unnormalized_scores = (
        jnp.einsum(
            "slhd,smhd->shlm", rotated_query, rotated_key, preferred_element_type=jnp.float32
        )
        * score_scale
    )
    return (unnormalized_scores * mask).astype(jnp.bfloat16)


def gather_rows(rows):
    return lax.all_gather(rows, "tensor", axis=0, tiled=True)


def sum_rows(part):
    return lax.psum_scatter(
        part.astype(jnp.bfloat16), "tensor", scatter_dimension=0, tiled=True
    ).astype(jnp.float32)


def fold_rows(acts, weights):
    pieces = jax.tree.map(lambda a: lax.all_gather(a, "dp", axis=0, tiled=True), shortened(weights))
    return tuple((jnp.dot(acts, p, preferred_element_type=jnp.float32) for p in pieces))


def map_columns(acts, weight):
    return jnp.dot(
        acts, lax.all_gather(weight, "dp", axis=1, tiled=True), preferred_element_type=jnp.float32
    )


def back_rows(grads, weights):
    pieces = lax.all_gather(shortened(weights), "dp", axis=0, tiled=True)
    total = lax.dot_general(grads[0], pieces[0], CONTRACT_COLS, preferred_element_type=jnp.float32)
    for grad, piece in zip(grads[1:], pieces[1:]):
        total = total + lax.dot_general(
            grad, piece, CONTRACT_COLS, preferred_element_type=jnp.float32
        )
    return total


def back_columns(grad, weight):
    return lax.dot_general(
        grad,
        lax.all_gather(weight, "dp", axis=1, tiled=True),
        CONTRACT_COLS,
        preferred_element_type=jnp.float32,
    )


def plain(
    tokens,
    segments,
    attn_gain,
    w_query,
    w_key,
    w_value,
    w_swish,
    w_output,
    ffn_gain,
    w_gelu,
    w_up,
    w_down,
    cotangent,
):
    layers = w_query.shape[0]
    heads_dev = w_query.shape[2] // HEAD_QK
    seqs = segments.shape[0] // LEN
    score_scale = HEAD_QK ** (-0.5)
    head_ids = (lax.axis_index("tensor") * heads_dev + jnp.arange(heads_dev)).astype(jnp.float32)
    mask = plain_mask(segments.reshape(seqs, LEN), head_ids, LEN)
    cosine, sine = plain_rotation(LEN, HEAD_QK)
    residual = tokens.astype(jnp.float32)
    saved = []
    for layer in range(layers):
        attn_in = (w_query[layer], w_key[layer], w_value[layer], w_swish[layer])
        ffn_in = (w_gelu[layer], w_up[layer])
        whole_in = attn_in + ffn_in
        whole_out = (w_output[layer], w_down[layer])
        normed = gather_rows(norm_rows(residual, attn_gain[layer]).astype(jnp.bfloat16))
        rows_all = normed.shape[0]
        query, keys, values, swish = fold_rows(normed, attn_in)
        vals = values.astype(jnp.bfloat16).reshape(seqs, LEN, heads_dev, HEAD_V)
        rotated_query = rotate(query.reshape(seqs, LEN, heads_dev, HEAD_QK), cosine, sine).astype(
            jnp.bfloat16
        )
        rotated_key = rotate(keys.reshape(seqs, LEN, heads_dev, HEAD_QK), cosine, sine).astype(
            jnp.bfloat16
        )
        probs = weights_of(rotated_query, rotated_key, mask, score_scale)
        mixed = jnp.einsum("shlm,smhv->slhv", probs, vals, preferred_element_type=jnp.float32)
        zed = norm_heads(mixed).reshape(rows_all, -1)
        gated = (jax.nn.silu(swish) * zed).astype(jnp.bfloat16)
        branch = map_columns(gated, w_output[layer])
        mid = residual + sum_rows(branch)
        normed_ffn = gather_rows(norm_rows(mid, ffn_gain[layer]).astype(jnp.bfloat16))
        gate_pre, up_pre = fold_rows(normed_ffn, ffn_in)
        hidden = (gelu_tanh(gate_pre) * up_pre).astype(jnp.bfloat16)
        branch_ffn = map_columns(hidden, w_down[layer])
        saved.append(
            (
                residual,
                normed,
                rotated_query,
                rotated_key,
                vals,
                swish,
                mixed,
                zed,
                gated,
                mid,
                normed_ffn,
                gate_pre,
                up_pre,
                hidden,
                whole_in,
                whole_out,
            )
        )
        residual = mid + sum_rows(branch_ffn)
    output = residual.astype(jnp.bfloat16)
    grad_res = cotangent.astype(jnp.float32)
    weight_parts = [None] * layers
    attn_gain_parts = [None] * layers
    ffn_gain_parts = [None] * layers
    for layer in reversed(range(layers)):
        (
            x_in,
            normed,
            rotated_query,
            rotated_key,
            vals,
            swish,
            mixed,
            zed,
            gated,
            mid,
            normed_ffn,
            gate_pre,
            up_pre,
            hidden,
            whole_in,
            whole_out,
        ) = saved[layer]
        attn_in = (w_query[layer], w_key[layer], w_value[layer], w_swish[layer])
        ffn_in = (w_gelu[layer], w_up[layer])
        rows_all = normed.shape[0]
        grad_c = gather_rows(grad_res.astype(jnp.bfloat16))
        down_grad = lax.dot_general(
            grad_c, hidden, CONTRACT_ROWS, preferred_element_type=jnp.float32
        )
        grad_hidden = back_columns(grad_c, w_down[layer])
        gelu_val, gelu_activation = jax.vjp(gelu_tanh, gate_pre)
        grad_gate = gelu_activation(grad_hidden * up_pre)[0].astype(jnp.bfloat16)
        grad_upv = (grad_hidden * gelu_val).astype(jnp.bfloat16)
        gelu_grad = lax.dot_general(
            normed_ffn, grad_gate, CONTRACT_ROWS, preferred_element_type=jnp.float32
        )
        up_grad = lax.dot_general(
            normed_ffn, grad_upv, CONTRACT_ROWS, preferred_element_type=jnp.float32
        )
        grad_nf = back_rows((grad_gate, grad_upv), ffn_in)
        _, ffn_norm_fn = jax.vjp(norm_rows, mid, ffn_gain[layer])
        grad_mid_norm, ffn_gain_parts[layer] = ffn_norm_fn(sum_rows(grad_nf))
        grad_mid = grad_res + grad_mid_norm
        grad_b = gather_rows(grad_mid.astype(jnp.bfloat16))
        output_grad_t = lax.dot_general(
            grad_b, gated, CONTRACT_ROWS, preferred_element_type=jnp.float32
        )
        grad_gated = back_columns(grad_b, w_output[layer])
        swish_output, swish_fn = jax.vjp(jax.nn.silu, swish)
        grad_sw = swish_fn(grad_gated * zed)[0].astype(jnp.bfloat16)
        grad_zed = grad_gated * swish_output
        _, head_fn = jax.vjp(norm_heads, mixed)
        grad_mixed = head_fn(grad_zed.reshape(mixed.shape))[0].astype(jnp.bfloat16)
        probs = weights_of(rotated_query, rotated_key, mask, score_scale)
        grad_probs = jnp.einsum(
            "slhv,smhv->shlm", grad_mixed, vals, preferred_element_type=jnp.float32
        )
        grad_raw = (grad_probs * mask).astype(jnp.bfloat16)
        grad_vals = jnp.einsum(
            "shlm,slhv->smhv", probs, grad_mixed, preferred_element_type=jnp.float32
        )
        grad_vals = grad_vals.astype(jnp.bfloat16).reshape(rows_all, -1)
        grad_qrot = (
            jnp.einsum("shlm,smhd->slhd", grad_raw, rotated_key, preferred_element_type=jnp.float32)
            * score_scale
        )
        grad_krot = (
            jnp.einsum(
                "shlm,slhd->smhd", grad_raw, rotated_query, preferred_element_type=jnp.float32
            )
            * score_scale
        )
        grad_q = rotate_back(grad_qrot, cosine, sine).astype(jnp.bfloat16).reshape(rows_all, -1)
        grad_k = rotate_back(grad_krot, cosine, sine).astype(jnp.bfloat16).reshape(rows_all, -1)
        attn_grads = tuple(
            (
                lax.dot_general(normed, g, CONTRACT_ROWS, preferred_element_type=jnp.float32)
                for g in (grad_q, grad_k, grad_vals, grad_sw)
            )
        )
        grad_n = back_rows((grad_q, grad_k, grad_vals, grad_sw), attn_in)
        _, attn_norm_fn = jax.vjp(norm_rows, x_in, attn_gain[layer])
        grad_x_norm, attn_gain_parts[layer] = attn_norm_fn(sum_rows(grad_n))
        grad_res = grad_mid + grad_x_norm
        weight_parts[layer] = jax.tree.map(
            lambda part: part.astype(jnp.float32),
            lax.psum_scatter(
                shortened(attn_grads + (output_grad_t, gelu_grad, up_grad, down_grad)),
                "dp",
                scatter_dimension=0,
                tiled=True,
            ),
        )
    attn_gain_grad, ffn_gain_grad = lax.psum(
        (jnp.stack(attn_gain_parts), jnp.stack(ffn_gain_parts)), ("dp", "tensor")
    )
    grad_query = jnp.stack([p[0] for p in weight_parts])
    grad_key = jnp.stack([p[1] for p in weight_parts])
    grad_value = jnp.stack([p[2] for p in weight_parts])
    grad_swish = jnp.stack([p[3] for p in weight_parts])
    grad_output = jnp.stack([p[4].T for p in weight_parts])
    grad_gelu = jnp.stack([p[5] for p in weight_parts])
    grad_up = jnp.stack([p[6] for p in weight_parts])
    grad_down = jnp.stack([p[7].T for p in weight_parts])
    return (
        output,
        grad_res,
        attn_gain_grad,
        grad_query,
        grad_key,
        grad_value,
        grad_swish,
        grad_output,
        ffn_gain_grad,
        grad_gelu,
        grad_up,
        grad_down,
    )


def grouped(
    tokens, segments, attn_gain, w_query, w_key, w_value, w_swish, w_output, ffn_gain, w_gelu, w_up, w_down, cotangent
):
    layers = w_query.shape[0]
    mask, cosine, sine, units, total = setup(segments, w_query, w_value, w_gelu)
    turn = lambda w: jnp.swapaxes(w, 1, 2)
    weights = (
        turn(w_query), turn(w_key), turn(w_value), turn(w_swish), w_output, turn(w_gelu), turn(w_up), w_down,
    )
    dims = (layers, tokens.shape[0], w_query.shape[1], units, HEAD_QK ** (-0.5))
    output, x_mid, mids, *kept = run_forward(
        dims, total, tokens, cotangent, mask, cosine, sine, attn_gain, ffn_gain, weights
    )
    input_grad, gains, parts = run_backward(
        dims, cotangent, tokens, x_mid, mids, mask, cosine, sine, attn_gain, ffn_gain, kept
    )
    q, k, v, s, o, g, u, d = unstack_grads(units, parts)
    return (
        output, input_grad, gains[:layers], q, k, turn(v), turn(s), o, gains[layers : 2 * layers], turn(g), turn(u), d,
    )


def solution(mesh):
    rows = P(("dp", "tensor"), None)
    up, down = P(None, "dp", "tensor"), P(None, "tensor", "dp")
    in_specs = (rows, P("dp"), P(), up, up, up, up, down, P(), up, up, down, rows)
    out_specs = (rows, rows, P(), up, up, up, up, down, P(), up, up, down)
    step = grouped if (mesh.shape["dp"], mesh.shape["tensor"]) == (8, 4) else plain
    return jax.shard_map(step, mesh=mesh, in_specs=in_specs, out_specs=out_specs, check_vma=False)
```

```python
import functools

import jax
import jax.numpy as jnp
from jax import lax
from jax.experimental import pallas as pl
from jax.experimental.pallas import tpu as pltpu
from jax.sharding import PartitionSpec as P

HEAD_QK = 256
HEAD_V = 432
LEN = 512

EPS = 1e-06
HEAD_FLOOR = 1.0
NN = (((1,), (0,)), ((), ()))
NT = (((1,), (1,)), ((), ()))
TN = (((0,), (0,)), ((), ()))
MESH = pl.DeviceIdType.MESH
BF16 = jnp.bfloat16
F32 = jnp.float32
LOOK = 2
SCHED = (
    ("III", "P", "", "PI", "PI", "PI"),
    ("PI", "PI", "", "PI", "PI", ""),
    ("PI", "PI", "", "PI", "PI", "PI"),
    ("PI", "PI", "", "PI", "PI", ""),
    ("PI", "PI", "", "", ""),
)
COT_AFTER = "v"
CHUNKS = 4
VMEM_LIMIT = 60 * 1024 * 1024


def dot(a, b, dims=NN):
    return lax.dot_general(a, b, dims, preferred_element_type=F32)


def loop(steps, body):
    lax.fori_loop(0, steps, lambda i, c: (body(i), c)[1], 0)


class Place:
    def __init__(self):
        dp, tensor = lax.axis_index("dp"), lax.axis_index("tensor")
        self.dp, self.tensor = dp, tensor
        self.z, self.y = lax.div(dp, 2), lax.rem(dp, 2)
        self.x, self.c = lax.div(tensor, 2), lax.rem(tensor, 2)
        self.half = lax.rem(self.z, 2)
        self.zn = self.z + 1 - 2 * self.half

    def at(self, z=None, y=None, x=None, c=None):
        z = self.z if z is None else z
        y = self.y if y is None else y
        x = self.x if x is None else x
        c = self.c if c is None else c
        return (z * 2 + y, x * 2 + c)

    def zplus(self, d):
        return lax.rem(self.z + d + 4, 4)

    def sib(self):
        return self.at(c=1 - self.c)

    def xn(self):
        return self.at(x=1 - self.x)

    def yn(self):
        return self.at(y=1 - self.y)

    def znb(self):
        return self.at(z=self.zn)

    def peers(self):
        return [self.sib(), self.xn(), self.yn()] + [self.at(z=self.zplus(d)) for d in (1, 2, 3)]

    def greet(self):
        bar = pltpu.get_barrier_semaphore()
        peers = self.peers()
        for p in peers:
            pl.semaphore_signal(bar, inc=1, device_id=p, device_id_type=MESH)
        pl.semaphore_wait(bar, len(peers))


def remote(src, dst, ssem, rsem, dev):
    return pltpu.make_async_remote_copy(
        src_ref=src, dst_ref=dst, send_sem=ssem, recv_sem=rsem, device_id=dev, device_id_type=MESH
    )


def block(half, tensor, rows):
    return pl.ds(pl.multiple_of((half * 4 + tensor) * rows, rows), rows)


def part_of(r, at, n):
    return pl.ds(pl.multiple_of(r.start + at, n), n)


class Gather:
    def __init__(self, me, buf, rows, ssem, rsem):
        def move(k, half, x, dev, at=0, size=rows):
            r = part_of(block(half, x * 2 + me.c, rows), at, size)
            return remote(buf.at[r], buf.at[r], ssem.at[k], rsem.at[k], dev)

        n = rows // CHUNKS
        h, x = me.half, me.x
        self.me = me
        self.own_x = move(0, h, x, me.xn())
        self.own_s = move(1, h, x, me.sib())
        self.x_s = move(2, h, 1 - x, me.sib())
        self.z_s = move(3, 1 - h, x, me.sib())
        self.g_s = move(4, 1 - h, 1 - x, me.sib())
        self.own_z = [move(5 + i, h, x, me.znb(), i * n, n) for i in range(CHUNKS)]
        self.z_x = [move(5 + CHUNKS + i, 1 - h, x, me.xn(), i * n, n) for i in range(CHUNKS)]

    def begin(self):
        for m in self.own_z + [self.own_x, self.own_s]:
            m.start()

    def finish(self, first, second, fill=()):
        fill = list(fill)

        def step():
            if fill:
                fill.pop(0)()

        step()
        self.own_x.wait_recv()
        self.x_s.start()
        for a, b in zip(self.own_z, self.z_x):
            a.wait_recv()
            b.start()
        self.z_s.start()
        step()
        self.own_s.wait_recv()
        self.x_s.wait_recv()
        first(self.me.half)
        for m in self.z_x:
            m.wait_recv()
        self.g_s.start()
        step()
        self.z_s.wait_recv()
        self.g_s.wait_recv()
        second(1 - self.me.half)
        for m in self.own_z + self.z_x + [self.own_x, self.own_s, self.z_s, self.x_s, self.g_s]:
            m.wait_send()


def gather_acts(me, buf, rows, ssem, rsem, first, second, fill=()):
    g = Gather(me, buf, rows, ssem, rsem)
    g.begin()
    g.finish(first, second, fill)


def sum_acts(me, part, rows, sib_buf, x_buf, z_buf, ssem, rsem, body, fill=()):
    fill = list(fill)
    n = rows // CHUNKS

    def step():
        if fill:
            fill.pop(0)()

    h, x = me.half, me.x
    order = [(1 - h, 1 - x), (h, 1 - x), (1 - h, x), (h, x)]
    sibs = []
    for j, (hh, xx) in enumerate(order):
        m = remote(part.at[block(hh, xx * 2 + 1 - me.c, rows)], sib_buf.at[j], ssem.at[j], rsem.at[j], me.sib())
        m.start()
        sibs.append(m)
    step()
    small = 32

    def mine(j, at, size):
        hh, xx = order[j]
        return part_of(block(hh, xx * 2 + me.c, rows), at, size)

    def add(j, at, size, extra=None):
        def go(i):
            r = mine(j, at + i * small, small)
            k = pl.ds(pl.multiple_of(at + i * small, small), small)
            v = part[r, :].astype(F32) + sib_buf[j, k, :].astype(F32)
            if extra is not None:
                v = v + extra[k, :].astype(F32)
            part[r, :] = v.astype(BF16)

        loop(size // small, go)

    def cut(i):
        return pl.ds(i * n, n)

    g_x = [
        remote(part.at[mine(0, i * n, n)], x_buf.at[0, cut(i)], ssem.at[5 + i], rsem.at[5 + i], me.xn())
        for i in range(CHUNKS)
    ]
    x_x = remote(part.at[mine(1, 0, rows)], x_buf.at[1], ssem.at[4], rsem.at[4], me.xn())
    to_z = [
        remote(
            part.at[mine(2, i * n, n)], z_buf.at[cut(i)], ssem.at[5 + CHUNKS + i], rsem.at[5 + CHUNKS + i], me.znb()
        )
        for i in range(CHUNKS)
    ]
    sibs[0].wait_recv()
    for i in range(CHUNKS):
        add(0, i * n, n)
        g_x[i].start()
    sibs[1].wait_recv()
    add(1, 0, rows)
    x_x.start()
    step()
    sibs[2].wait_recv()
    for i in range(CHUNKS):
        g_x[i].wait_recv()
        add(2, i * n, n, x_buf.at[0])
        to_z[i].start()
    sibs[3].wait_recv()
    step()
    x_x.wait_recv()
    for m in to_z:
        m.wait_recv()

    def last(i):
        k = pl.ds(pl.multiple_of(i * small, small), small)
        v = part[mine(3, i * small, small), :].astype(F32) + sib_buf[3, k, :].astype(F32)
        v = v + x_buf[1, k, :].astype(F32) + z_buf[k, :].astype(F32)
        body(i * small, small, v)

    loop(rows // small, last)
    for m in sibs + g_x + to_z + [x_x]:
        m.wait_send()
    while fill:
        step()


def unit_rows(qk, val, ffn):
    sizes = (("q", qk), ("k", qk), ("v", val), ("s", val), ("o", val), ("g", ffn), ("u", ffn), ("d", ffn))
    out, at = {}, 0
    for name, n in sizes:
        out[name] = (at, n)
        at += n
    return out, at


def rms(v, floor):
    return lax.rsqrt(jnp.mean(v * v, -1, keepdims=True) + floor)


def forward_kernel(
    dims,
    tokens, cot, mask, cosine, sine, attn_gain, ffn_gain, w_q, w_k, w_v, w_s, w_o, w_g, w_u, w_d,
    output, x_mid, mids, wf, s_gc, s_n, s_nf, s_q, s_k, s_v, s_s, s_m, s_gt, s_g, s_u, s_h, s_p,
    W, N0, N1, part, sib_buf, x_buf, z_buf, q, k, v, s, m, gt, g, u, h, p,
    zs, zr, ys, yr, lo, ld, ags, agr, rss, rsr, sv,
):
    layers, rows, lanes, units, scale = dims
    me = Place()
    names = list(units)
    shards = dict(q=w_q, k=w_k, v=w_v, s=w_s, o=w_o, g=w_g, u=w_u, d=w_d)
    groups = [(l, units[n]) for l in range(layers) for n in names]
    spot = {(l, n): l * len(names) + i for l in range(layers) for i, n in enumerate(names)}
    my_lane = pl.multiple_of(me.dp * lanes, lanes)

    def shard(i, half):
        n = groups[i][1][1]
        return shards[names[i % len(names)]].at[groups[i][0], pl.ds(pl.multiple_of(half * n, 16), n)]

    def z_copy(i, d):
        l, (r0, n) = groups[i]
        tz = me.zplus(d)
        return remote(
            shard(i, lax.rem(tz, 2)), wf.at[l, pl.ds(r0, n), pl.ds(my_lane, lanes)],
            zs.at[i, d - 1], zr.at[i, d - 1], me.at(z=tz),
        )

    def y_copy(i, d):
        l, (r0, n) = groups[i]
        lane = pl.ds(pl.multiple_of((me.zplus(-d) * 2 + me.y) * lanes, lanes), lanes)
        dst = wf.at[l, pl.ds(r0, n), lane]
        src = shard(i, me.half) if d == 0 else dst
        return remote(src, dst, ys.at[i, d], yr.at[i, d], me.yn())

    def local_copy(i):
        l, (r0, n) = groups[i]
        return pltpu.make_async_copy(
            shard(i, me.half), wf.at[l, pl.ds(r0, n), pl.ds(my_lane, lanes)], lo.at[i]
        )

    def issue(i):
        if i < len(groups):
            for d in (1, 2, 3):
                z_copy(i, d).start()
            y_copy(i, 0).start()
            local_copy(i).start()

    issued, pumped = [0], [0]

    def send_next():
        if issued[0] < len(groups):
            issue(issued[0])
            issued[0] += 1

    def pass_on():
        i = pumped[0]
        if i >= len(groups):
            return
        while issued[0] <= i:
            send_next()
        pumped[0] += 1
        for d in (1, 3, 2):
            z_copy(i, d).wait_recv()
            y_copy(i, d).start()

    plan = SCHED

    def act(pair, point):
        def go():
            for ch in plan[pair][point]:
                if ch == "I":
                    send_next()
                if ch == "P":
                    pass_on()
        return go

    def gfill(pair):
        return [act(pair, 0), act(pair, 1), act(pair, 5)]

    def sfill(pair):
        return [act(pair, 2), act(pair, 3), act(pair, 4)]

    def take(l, *wanted):
        idx = [spot[l, n] for n in wanted]
        while pumped[0] <= idx[-1]:
            pass_on()
            while issued[0] - pumped[0] < LOOK:
                if issued[0] >= len(groups):
                    break
                send_next()
        copies = []
        for i in idx:
            for d in range(4):
                y_copy(i, d).wait_recv()
            local_copy(i).wait()
            r0, n = groups[i][1]
            c = pltpu.make_async_copy(wf.at[l, pl.ds(r0, n)], W.at[pl.ds(r0, n)], ld.at[i])
            c.start()
            copies.append(c)
        for c in copies:
            c.wait()

    saves = []

    def save(src, dst):
        c = pltpu.make_async_copy(src, dst, sv.at[len(saves)])
        c.start()
        saves.append(c)

    waited = [0]

    def settle():
        while waited[0] < len(saves):
            saves[waited[0]].wait()
            waited[0] += 1

    def weight(n):
        r0, size = units[n]
        return W[pl.ds(r0, size), :]

    def seq_rows(i):
        return pl.ds(pl.multiple_of(i * LEN, LEN), LEN)

    seqs = 2
    own = (me.half * 4 + me.tensor) * rows

    def own_rows(r0, n):
        return pl.ds(pl.multiple_of(own + r0, n), n)

    me.greet()
    small = 32

    def first_norm(i):
        r = pl.ds(pl.multiple_of(i * small, small), small)
        x = tokens[r, :].astype(F32)
        N0[own_rows(i * small, small), :] = (x * rms(x, EPS) * attn_gain[0:1, :]).astype(BF16)
        N1[own_rows(i * small, small), :] = cot[r, :]

    loop(rows // small, first_norm)
    def out_rows(i, src, name):
        def go(j):
            r = pl.ds(pl.multiple_of(i * LEN + j * 256, 256), 256)
            part[r, :] = dot(src[r, :], weight(name)).astype(BF16)

        loop(LEN // 256, go)

    def turned(name, dst, i):
        r = seq_rows(i)
        t = dot(N0[r, :], weight(name), NT)
        half = t.shape[1] // 2
        t1, t2 = t[:, :half], t[:, half:]
        c, sn = cosine[...], sine[...]
        dst[r, :half] = (t1 * c - t2 * sn).astype(BF16)
        dst[r, half:] = (t2 * c + t1 * sn).astype(BF16)

    def retain(i):
        r = seq_rows(i)
        v[r, :] = dot(N0[r, :], weight("v"), NT).astype(BF16)
        raw = dot(q[r, :], k[r, :], NT) * scale
        probs = (raw * mask[i]).astype(BF16)
        p[i] = probs
        m[r, :] = dot(probs, v[r, :])

    def gate(i):
        r = seq_rows(i)
        t = dot(N0[r, :], weight("s"), NT)
        s[r, :] = t
        mix = m[r, :]
        gt[r, :] = (jax.nn.silu(t) * (mix * rms(mix, HEAD_FLOOR))).astype(BF16)

    stages = (
        ("q", functools.partial(turned, "q", q)), ("k", functools.partial(turned, "k", k)), ("v", retain),
        ("s", gate), ("o", lambda i: out_rows(i, gt, "o")),
    )

    def attn_seq(i, l, fetch):
        for name, stage in stages:
            if fetch:
                take(l, name)
            stage(i)

    def ffn_seq(i, l, fetch):
        r = seq_rows(i)
        if fetch:
            take(l, "g")
        g[r, :] = dot(N1[r, :], weight("g"), NT)
        if fetch:
            take(l, "u")
        t = dot(N1[r, :], weight("u"), NT)
        u[r, :] = t
        h[r, :] = (jax.nn.gelu(g[r, :], approximate=True) * t).astype(BF16)
        if fetch:
            take(l, "d")
        out_rows(i, h, "d")

    both = lambda body, l: (functools.partial(body, l=l, fetch=True), functools.partial(body, l=l, fetch=False))

    for l in range(layers):
        if l:
            gather_acts(me, N0, rows, ags.at[2 * l], agr.at[2 * l], *both(attn_seq, l), gfill(2 * l))
        else:
            own_rows_of = Gather(me, N0, rows, ags.at[0], agr.at[0])
            grads_of = Gather(me, N1, rows, ags.at[2 * layers], agr.at[2 * layers])
            own_rows_of.begin()
            act(0, 0)()
            grads_of.begin()
            idle = lambda i: None
            own_rows_of.finish(idle, idle, [act(0, 1), act(0, 5), act(2 * layers, 3)])
            for name, stage in stages:
                take(0, name)
                loop(seqs, stage)
                if name == COT_AFTER:
                    grads_of.finish(idle, idle, [act(2 * layers, i) for i in (0, 1, 2)])
                    save(N1, s_gc)
        for src, dst in ((N0, s_n), (q, s_q), (k, s_k), (v, s_v), (p, s_p), (m, s_m), (s, s_s), (gt, s_gt)):
            save(src, dst.at[l])

        if l == 0:
            saves[0].wait()
            waited[0] = 1

        def to_mid(r0, n, total, l=l):
            r = pl.ds(pl.multiple_of(r0, n), n)
            x = (tokens[r, :].astype(F32) if l == 0 else x_mid[l - 1, r, :]) + total
            mids[l, r, :] = x
            N1[own_rows(r0, n), :] = (x * rms(x, EPS) * ffn_gain[l : l + 1, :]).astype(BF16)

        sum_acts(me, part, rows, sib_buf, x_buf, z_buf, rss.at[2 * l], rsr.at[2 * l], to_mid, sfill(2 * l))
        gather_acts(me, N1, rows, ags.at[2 * l + 1], agr.at[2 * l + 1], *both(ffn_seq, l), gfill(2 * l + 1))
        for src, dst in ((N1, s_nf), (g, s_g), (u, s_u), (h, s_h)):
            save(src, dst.at[l])

        def to_next(r0, n, total, l=l):
            r = pl.ds(pl.multiple_of(r0, n), n)
            x = mids[l, r, :] + total
            if l + 1 < layers:
                x_mid[l, r, :] = x
                N0[own_rows(r0, n), :] = (x * rms(x, EPS) * attn_gain[l + 1 : l + 2, :]).astype(BF16)
            else:
                output[r, :] = x.astype(BF16)

        settle()
        sum_acts(me, part, rows, sib_buf, x_buf, z_buf, rss.at[2 * l + 1], rsr.at[2 * l + 1], to_next, sfill(2 * l + 1))
    settle()
    for i in range(len(groups)):
        for d in (1, 2, 3):
            z_copy(i, d).wait_send()
        for d in range(4):
            y_copy(i, d).wait_send()


def run_forward(dims, total, tokens, cot, mask, cosine, sine, attn_gain, ffn_gain, weights):
    layers, rows, lanes, units, scale = dims
    depth = tokens.shape[1]
    group = 8 * rows
    seqs = group // LEN
    qk, val, ffn = units["q"][1], units["v"][1], units["g"][1]
    vm = pl.BlockSpec(memory_space=pltpu.VMEM)
    hb = pl.BlockSpec(memory_space=pl.ANY)
    outs = [
        ((rows, depth), BF16), ((layers - 1, rows, depth), F32), ((layers, rows, depth), F32),
        ((layers, total, depth), BF16), ((group, depth), BF16),
        ((layers, group, depth), BF16), ((layers, group, depth), BF16),
        ((layers, group, qk), BF16), ((layers, group, qk), BF16), ((layers, group, val), BF16),
        ((layers, group, val), F32), ((layers, group, val), F32), ((layers, group, val), BF16),
        ((layers, group, ffn), F32), ((layers, group, ffn), F32), ((layers, group, ffn), BF16),
        ((layers, seqs, LEN, LEN), BF16),
    ]
    n_groups = layers * len(units)
    dma = pltpu.SemaphoreType.DMA
    return pl.pallas_call(
        functools.partial(forward_kernel, dims),
        out_shape=[jax.ShapeDtypeStruct(s, d) for s, d in outs],
        in_specs=[vm] * 7 + [hb] * 8,
        out_specs=[vm] * 3 + [hb] * 14,
        scratch_shapes=[
            pltpu.VMEM((total, depth), BF16),
            pltpu.VMEM((group, depth), BF16), pltpu.VMEM((group, depth), BF16), pltpu.VMEM((group, depth), BF16),
            pltpu.VMEM((4, rows, depth), BF16), pltpu.VMEM((2, rows, depth), BF16), pltpu.VMEM((rows, depth), BF16),
            pltpu.VMEM((group, qk), BF16), pltpu.VMEM((group, qk), BF16), pltpu.VMEM((group, val), BF16),
            pltpu.VMEM((group, val), F32), pltpu.VMEM((group, val), F32), pltpu.VMEM((group, val), BF16),
            pltpu.VMEM((group, ffn), F32), pltpu.VMEM((group, ffn), F32), pltpu.VMEM((group, ffn), BF16),
            pltpu.VMEM((seqs, LEN, LEN), BF16),
            dma((n_groups, 3)), dma((n_groups, 3)), dma((n_groups, 4)), dma((n_groups, 4)),
            dma((n_groups,)), dma((n_groups,)),
            *[dma((2 * layers + 1, 5 + 2 * CHUNKS)) for _ in range(4)],
            dma((12 * layers + 1,)),
        ],
        compiler_params=pltpu.CompilerParams(collective_id=0, has_side_effects=True, vmem_limit_bytes=VMEM_LIMIT),
    )(tokens, cot, mask, cosine, sine, attn_gain, ffn_gain, *weights)


SLOTS = 4
EARLY = 1
BSCHED = (
    ("", "", "", "", "M", "MM", ""),
    ("C", "C", "", "", "CMM", "CMCM", ""),
    ("C", "C", "C", "", "M", "MM", ""),
    ("C", "C", "", "", "CMM", "CMCM", ""),
)


def backward_kernel(
    dims,
    cot, tokens, x_mid, mids, mask, cosine, sine, attn_gain, ffn_gain,
    wf, s_gc, s_n, s_nf, s_q, s_k, s_v, s_s, s_m, s_gt, s_g, s_u, s_h, s_p,
    input_grad, gains, rz,
    gr, xb, nb, ga0, ga1, part, sib_buf, x_buf, z_buf, W, a1, a2, a3, q, k, v, p, t1, t2, tq, tk, G, ry, acc, acc_in,
    ys, yr, zs, zr, os, ags, agr, rss, rsr, ld, gns, gnr, credit,
):
    layers, rows, lanes, units, scale = dims
    me = Place()
    depth = cot.shape[1]
    wide = 512
    small = 32
    seqs = 2
    order = list(reversed(range(layers)))
    jobs = [(l, n) for l in order for n in ("d", "g", "u", "o", "s", "q", "k", "v")]
    index = {job: i for i, job in enumerate(jobs)}
    own = (me.half * 4 + me.tensor) * rows
    ffn_row = units["g"][0]
    attn_end = ffn_row
    total_rows = units["d"][0] + units["d"][1]

    def own_rows(r0, n):
        return pl.ds(pl.multiple_of(own + r0, n), n)

    def seq_rows(i):
        return pl.ds(pl.multiple_of(i * LEN, LEN), LEN)

    def lane(i):
        return pl.ds(pl.multiple_of(i * lanes, lanes), lanes)

    def y_send(i, d):
        n = units[jobs[i][1]][1]
        tz = me.zplus(d)
        return remote(
            G.at[i % SLOTS, pl.ds(0, n), lane(tz * 2 + 1 - me.y)], ry.at[i % SLOTS, pl.ds(0, n), lane(tz)],
            ys.at[i, d], yr.at[i, d], me.yn(),
        )

    def z_send(i, d):
        l, name = jobs[i]
        r0, n = units[name]
        tz = me.zplus(d)
        return remote(
            G.at[i % SLOTS, pl.ds(0, n), lane(tz * 2 + me.y)], rz.at[l, me.half, d // 2, pl.ds(r0, n)],
            zs.at[i, d - 1], zr.at[i, d - 1], me.at(z=tz),
        )

    def own_copy(i):
        l, name = jobs[i]
        r0, n = units[name]
        return pltpu.make_async_copy(
            G.at[i % SLOTS, pl.ds(0, n), lane(me.dp)], rz.at[l, me.half, 0, pl.ds(r0, n)], os.at[i]
        )

    def retire(i):
        for d in range(4):
            y_send(i, d).wait_send()
        for d in (1, 2, 3):
            z_send(i, d).wait_send()
        own_copy(i).wait()

    def make(l, name, left, right):
        i = index[l, name]
        n = units[name][1]
        if i >= SLOTS:
            retire(i - SLOTS)

        def go(j):
            cols = pl.ds(pl.multiple_of(j * wide, wide), wide)
            G[i % SLOTS, :n, cols] = dot(left[...], right[:, cols], TN).astype(BF16)

        loop(depth // wide, go)
        if i >= SLOTS:
            pl.semaphore_wait(credit.at[i % SLOTS], 1)
        for d in (2, 1, 3, 0):
            y_send(i, d).start()

    def combine(l, name):
        i = index[l, name]
        n = units[name][1]
        for d in (2, 1, 3, 0):
            y_send(i, d).wait_recv()
            tz = me.zplus(d)

            def add(j, tz=tz):
                r = pl.ds(pl.multiple_of(j * 16, 16), 16)
                c = lane(tz * 2 + me.y)
                both = G[i % SLOTS, r, c].astype(F32) + ry[i % SLOTS, r, lane(tz)].astype(F32)
                G[i % SLOTS, r, c] = both.astype(BF16)

            loop(n // 16, add)
            if d:
                z_send(i, d).start()
            else:
                own_copy(i).start()
        if i + SLOTS < len(jobs):
            pl.semaphore_signal(credit.at[i % SLOTS], inc=1, device_id=me.yn(), device_id_type=MESH)

    spots = {}

    def load(key, src, dst):
        c = pltpu.make_async_copy(src, dst, ld.at[len(spots)])
        c.start()
        spots[key] = c

    def ready(*keys):
        for key in keys:
            spots[key].wait()

    def load_ffn(l):
        load(("wf", l), wf.at[l, pl.ds(ffn_row, total_rows - ffn_row)], W.at[pl.ds(0, total_rows - ffn_row)])
        load(("g", l), s_g.at[l], a1)
        load(("u", l), s_u.at[l], a2)

    def load_attn(l):
        load(("wa", l), wf.at[l, pl.ds(0, attn_end)], W.at[pl.ds(0, attn_end)])
        load(("s", l), s_s.at[l], a1)
        load(("m", l), s_m.at[l], a2)
        load(("q", l), s_q.at[l], q)
        load(("k", l), s_k.at[l], k)
        load(("v", l), s_v.at[l], v)
        load(("p", l), s_p.at[l], p)

    def load_mid(l):
        load(("mid", l), mids.at[l], xb)

    def load_h(l):
        load(("h", l), s_h.at[l], a3)

    def load_nf(l):
        load(("nf", l), s_nf.at[l], nb)

    def load_gt(l):
        load(("gt", l), s_gt.at[l], a3)

    def load_n(l):
        load(("n", l), s_n.at[l], nb)

    def weight(name, base):
        r0, n = units[name]
        return W[pl.ds(r0 - base, n), :]

    def norm_back(x, gain, dn, gain_row):
        e = rms(x, EPS)
        gx = dn * gain
        inner = jnp.sum(gx * x, -1, keepdims=True)
        acc[0, gain_row : gain_row + 1, :] += jnp.sum(dn * x * e, 0, keepdims=True)
        return e * gx - (e * e * e) * x * (inner / depth)

    me.greet()
    load("gc", s_gc, ga0)
    load_ffn(order[0])
    load_mid(order[0])
    load_h(order[0])
    load_nf(order[0])
    acc[0] = jnp.zeros(acc.shape[1:], F32)

    def begin(i):
        r = pl.ds(pl.multiple_of(i * small, small), small)
        gr[r, :] = cot[r, :].astype(F32)

    loop(rows // small, begin)

    jobs_of = {
        "d": (a3, ga0, ("h",), lambda l: load_gt(l)),
        "g": (t1, nb, ("nf",), None),
        "u": (t2, nb, (), lambda l: load_n(l)),
        "o": (a3, ga1, ("gt",), None),
        "s": (t2, nb, ("n",), None),
        "q": (tq, nb, (), None),
        "k": (tk, nb, (), None),
        "v": (t1, nb, (), lambda l: (load_nf(l - 1), load_h(l - 1)) if l else None),
    }
    open_to, made, added = [0], [0], [0]

    def add_next():
        if added[0] < made[0]:
            combine(*jobs[added[0]])
            added[0] += 1

    def make_next():
        if made[0] < open_to[0]:
            i = made[0]
            while added[0] <= i - SLOTS:
                add_next()
            l, name = jobs[i]
            left, right, needs, then = jobs_of[name]
            ready(*((key, l) for key in needs))
            make(l, name, left, right)
            made[0] += 1
            if then:
                then(l)

    def make_all():
        while made[0] < open_to[0]:
            make_next()

    plan = BSCHED

    def act(pair, point):
        def go():
            for ch in plan[pair][point]:
                if ch == "M":
                    make_next()
                if ch == "C":
                    add_next()

        return go

    def gfill(pair):
        return [act(pair, i) for i in (0, 1, 2)]

    def sfill(pair):
        return [act(pair, i) for i in (3, 4, 5, 6)]

    def tile_rows(i, j):
        return pl.ds(pl.multiple_of(i * LEN + j * 256, 256), 256)

    def ffn_seq(i):
        def go(j):
            r = tile_rows(i, j)
            gh = dot(ga0[r, :], weight("d", ffn_row), NT)
            g, u = a1[r, :], a2[r, :]
            th = jnp.tanh(0.7978845608028654 * (g + 0.044715 * g * g * g))
            val = 0.5 * g * (1.0 + th)
            slope = 0.5 * (1.0 + th) + 0.5 * g * (1.0 - th * th) * (0.7978845608028654 * (1.0 + 0.134145 * g * g))
            t1[r, :] = (gh * u * slope).astype(BF16)
            t2[r, :] = (gh * val).astype(BF16)
            part[r, :] = (dot(t1[r, :], weight("g", ffn_row)) + dot(t2[r, :], weight("u", ffn_row))).astype(BF16)

        loop(LEN // 256, go)

    def attn_head(i):
        def go(j):
            r = tile_rows(i, j)
            gg = dot(ga1[r, :], weight("o", 0), NT)
            s, mix = a1[r, :], a2[r, :]
            sig = 1.0 / (1.0 + jnp.exp(-s))
            rr = rms(mix, HEAD_FLOOR)
            t2[r, :] = (gg * (mix * rr) * (sig * (1.0 + s * (1.0 - sig)))).astype(BF16)
            gz = gg * (s * sig)
            inner = jnp.sum(gz * mix, -1, keepdims=True) / mix.shape[1]
            t1[r, :] = (rr * gz - (rr * rr * rr) * mix * inner).astype(BF16)

        loop(LEN // 256, go)

    def attn_tail(i):
        r = seq_rows(i)
        gm = t1[r, :]
        raw = (dot(gm, v[r, :], NT) * mask[i]).astype(BF16)
        t1[r, :] = dot(p[i], gm, TN).astype(BF16)
        c, sn = cosine[...], sine[...]
        for dst, grad in ((tq, dot(raw, k[r, :]) * scale), (tk, dot(raw, q[r, :], TN) * scale)):
            half = grad.shape[1] // 2
            g1, g2 = grad[:, :half], grad[:, half:]
            dst[r, :half] = (g1 * c + g2 * sn).astype(BF16)
            dst[r, half:] = (g2 * c - g1 * sn).astype(BF16)

        def go(j):
            r = pl.ds(pl.multiple_of(i * LEN + j * 256, 256), 256)
            tot = dot(tq[r, :], weight("q", 0)) + dot(tk[r, :], weight("k", 0))
            tot = tot + dot(t1[r, :], weight("v", 0)) + dot(t2[r, :], weight("s", 0))
            part[r, :] = tot.astype(BF16)

        loop(LEN // 256, go)

    def attn_seq(i):
        attn_head(i)
        attn_tail(i)

    def attn_second(i, at):
        attn_head(i)
        open_to[0] = 8 * at + 3 + EARLY
        make_all()
        attn_tail(i)

    def after(keys, body):
        def go(i):
            make_all()
            ready(*keys)
            body(i)

        return go

    for at, l in enumerate(order):
        last = at == layers - 1
        first = after([("wf", l), ("g", l), ("u", l), ("mid", l)], ffn_seq)
        if at == 0:
            ready("gc")
            first(0)
            ffn_seq(1)
        else:
            gather_acts(me, ga0, rows, ags.at[2 * at], agr.at[2 * at], first, ffn_seq, gfill(2 * at))
        load_attn(l)
        open_to[0] = 8 * at + 3

        def to_mid(r0, n, tot, l=l):
            r = pl.ds(pl.multiple_of(r0, n), n)
            new = gr[r, :] + norm_back(xb[r, :], ffn_gain[l : l + 1, :], tot, layers + l)
            gr[r, :] = new
            ga1[own_rows(r0, n), :] = new.astype(BF16)

        sum_acts(me, part, rows, sib_buf, x_buf, z_buf, rss.at[2 * at], rsr.at[2 * at], to_mid, sfill(2 * at))
        if l:
            load(("x", l), x_mid.at[l - 1], xb)
        first = after([(key, l) for key in ("wa", "s", "m", "q", "k", "v", "p") + (("x",) if l else ())], attn_seq)
        gather_acts(me, ga1, rows, ags.at[2 * at + 1], agr.at[2 * at + 1], first, functools.partial(attn_second, at=at), gfill(2 * at + 1))
        if not last:
            load_ffn(order[at + 1])
        open_to[0] = 8 * at + 8

        def to_prev(r0, n, tot, l=l, last=last):
            r = pl.ds(pl.multiple_of(r0, n), n)
            x = tokens[r, :].astype(F32) if l == 0 else xb[r, :]
            new = gr[r, :] + norm_back(x, attn_gain[l : l + 1, :], tot, l)
            if last:
                input_grad[r, :] = new
            else:
                gr[r, :] = new
                ga0[own_rows(r0, n), :] = new.astype(BF16)

        sum_acts(
            me, part, rows, sib_buf, x_buf, z_buf, rss.at[2 * at + 1], rsr.at[2 * at + 1], to_prev, sfill(2 * at + 1)
        )
        if not last:
            load_mid(order[at + 1])

    make_all()
    while added[0] < made[0]:
        add_next()
    partners = [me.sib(), me.xn(), me.yn(), me.znb(), me.at(z=me.zplus(2))]
    for j, dev in enumerate(partners):
        m = remote(acc.at[j], acc_in.at[j], gns.at[j], gnr.at[j], dev)
        m.start()
        m.wait()
        acc[j + 1] = acc[j] + acc_in[j]
    gains[...] = acc[len(partners)]
    for i in range(len(jobs) - SLOTS, len(jobs)):
        retire(i)
    for i in range(len(jobs)):
        for d in (1, 2, 3):
            z_send(i, d).wait_recv()


def run_backward(dims, cot, tokens, x_mid, mids, mask, cosine, sine, attn_gain, ffn_gain, kept):
    layers, rows, lanes, units, scale = dims
    depth = tokens.shape[1]
    total = kept[0].shape[1]
    group = 8 * rows
    seqs = group // LEN
    qk, val, ffn = units["q"][1], units["v"][1], units["g"][1]
    vm = pl.BlockSpec(memory_space=pltpu.VMEM)
    hb = pl.BlockSpec(memory_space=pl.ANY)
    outs = [((rows, depth), F32), ((8, depth), F32), ((layers, 2, 2, total, lanes), BF16)]
    jobs = layers * len(units)
    most = max(n for _, n in units.values())
    attn_rows = units["g"][0]
    dma = pltpu.SemaphoreType.DMA
    big = pltpu.VMEM((group, depth), BF16)
    return pl.pallas_call(
        functools.partial(backward_kernel, dims),
        out_shape=[jax.ShapeDtypeStruct(s, d) for s, d in outs],
        in_specs=[vm, vm, hb, hb] + [vm] * 5 + [hb] * 14,
        out_specs=[vm] * 2 + [hb],
        scratch_shapes=[
            pltpu.VMEM((rows, depth), F32), pltpu.VMEM((rows, depth), F32), big, big, big, big,
            pltpu.VMEM((4, rows, depth), BF16), pltpu.VMEM((2, rows, depth), BF16), pltpu.VMEM((rows, depth), BF16),
            pltpu.VMEM((max(attn_rows, total - attn_rows), depth), BF16),
            pltpu.VMEM((group, val), F32), pltpu.VMEM((group, val), F32), pltpu.VMEM((group, val), BF16),
            pltpu.VMEM((group, qk), BF16), pltpu.VMEM((group, qk), BF16), pltpu.VMEM((group, val), BF16),
            pltpu.VMEM((seqs, LEN, LEN), BF16),
            pltpu.VMEM((group, val), BF16), pltpu.VMEM((group, val), BF16),
            pltpu.VMEM((group, qk), BF16), pltpu.VMEM((group, qk), BF16),
            pltpu.VMEM((SLOTS, most, depth), BF16), pltpu.VMEM((SLOTS, most, depth // 2), BF16),
            pltpu.VMEM((6, 8, depth), F32), pltpu.VMEM((5, 8, depth), F32),
            dma((jobs, 4)), dma((jobs, 4)), dma((jobs, 3)), dma((jobs, 3)), dma((jobs,)),
            *[dma((2 * layers, 5 + 2 * CHUNKS)) for _ in range(4)],
            dma((16 * layers + 1,)), dma((5,)), dma((5,)), pltpu.SemaphoreType.REGULAR((SLOTS,)),
        ],
        compiler_params=pltpu.CompilerParams(collective_id=1, has_side_effects=True, vmem_limit_bytes=VMEM_LIMIT),
    )(cot, tokens, x_mid, mids, mask, cosine, sine, attn_gain, ffn_gain, *kept)


NAMES = ("q", "k", "v", "s", "o", "g", "u", "d")
TILE = 128


def unstack_kernel(units, parts, *outs):
    for name, out in zip(NAMES, outs):
        r0, n = units[name]
        both = [parts[0, h, 0, r0 : r0 + n].astype(F32) + parts[0, h, 1, r0 : r0 + n].astype(F32) for h in range(2)]
        if name in ("q", "k"):
            out[0] = jnp.concatenate(both, 0).T
        else:
            for h in range(2):
                out[0, h * n : (h + 1) * n] = both[h]


def unstack_grads(units, parts):
    layers, _, _, total, lanes = parts.shape
    shapes, specs = [], []
    for name in NAMES:
        n = 2 * units[name][1]
        if name in ("q", "k"):
            shapes.append((layers, lanes, n))
            specs.append(pl.BlockSpec((1, TILE, n), lambda l, j: (l, j, 0)))
        else:
            shapes.append((layers, n, lanes))
            specs.append(pl.BlockSpec((1, n, TILE), lambda l, j: (l, 0, j)))
    return pl.pallas_call(
        functools.partial(unstack_kernel, units),
        grid=(layers, lanes // TILE),
        in_specs=[pl.BlockSpec((1, 2, 2, total, TILE), lambda l, j: (l, 0, 0, 0, j))],
        out_specs=specs,
        out_shape=[jax.ShapeDtypeStruct(s, F32) for s in shapes],
        compiler_params=pltpu.CompilerParams(vmem_limit_bytes=VMEM_LIMIT),
    )(parts)

def rotation(length, width):
    half = width // 2
    place = jnp.arange(length, dtype=F32)
    freqs = 10000.0 ** (-jnp.arange(half, dtype=F32) / half)
    angle = place[:, None] * freqs[None, :]
    return jnp.cos(angle), jnp.sin(angle)


def decay_mask(seg_rows, head, length):
    place = jnp.arange(length, dtype=jnp.int32)
    dist = place[:, None] - place[None, :]
    same = (seg_rows[:, :, None] == seg_rows[:, None, :]) & (dist >= 0)[None]
    rate = jnp.log1p(-(2.0 ** (-5.0 - head)))
    decay = jnp.exp(jnp.maximum(dist, 0).astype(F32) * rate)
    return jnp.where(same, decay[None], 0.0)


def setup(segments, w_query, w_value, w_gelu):
    dp, tensor = lax.axis_index("dp"), lax.axis_index("tensor")
    half = (dp // 2) % 2
    other = lax.ppermute(segments, "dp", [(i, i ^ 2) for i in range(8)])
    pair = jnp.where(half == 0, jnp.stack([segments, other]), jnp.stack([other, segments]))
    mask = decay_mask(pair, (tensor * 2 + half).astype(F32), LEN)
    cosine, sine = rotation(LEN, HEAD_QK)
    units, total = unit_rows(w_query.shape[2] // 2, w_value.shape[2] // 2, w_gelu.shape[2] // 2)
    return mask, cosine, sine, units, total


CONTRACT_ROWS = (((0,), (0,)), ((), ()))
CONTRACT_COLS = (((1,), (1,)), ((), ()))


def shortened(shard):
    return jax.tree.map(lambda a: a.astype(jnp.bfloat16) if a.dtype == jnp.float32 else a, shard)


def norm_rows(values, gain):
    return values * lax.rsqrt(jnp.mean(values * values, -1, keepdims=True) + EPS) * gain


def norm_heads(values):
    return values * lax.rsqrt(jnp.mean(values * values, -1, keepdims=True) + HEAD_FLOOR)


def gelu_tanh(values):
    return jax.nn.gelu(values, approximate=True)


def plain_rotation(length, width):
    half = width // 2
    place = jnp.arange(length, dtype=jnp.float32)
    freqs = 10000.0 ** (-jnp.arange(half, dtype=jnp.float32) / half)
    angle = place[:, None] * freqs[None, :]
    return (jnp.cos(angle)[:, None, :], jnp.sin(angle)[:, None, :])


def rotate(values, cosine, sine):
    half = values.shape[-1] // 2
    first = values[..., :half]
    second = values[..., half:]
    return jnp.concatenate([first * cosine - second * sine, second * cosine + first * sine], -1)


def rotate_back(grads, cosine, sine):
    half = grads.shape[-1] // 2
    first = grads[..., :half]
    second = grads[..., half:]
    return jnp.concatenate([first * cosine + second * sine, second * cosine - first * sine], -1)


def plain_mask(seg_rows, head_ids, length):
    place = jnp.arange(length, dtype=jnp.int32)
    dist = place[:, None] - place[None, :]
    same = (seg_rows[:, :, None] == seg_rows[:, None, :]) & (dist >= 0)[None]
    rates = jnp.log1p(-(2.0 ** (-5.0 - head_ids)))
    decay = jnp.exp(jnp.maximum(dist, 0).astype(jnp.float32)[None] * rates[:, None, None])
    return jnp.where(same[:, None], decay[None], 0.0)


def weights_of(rotated_query, rotated_key, mask, score_scale):
    unnormalized_scores = (
        jnp.einsum(
            "slhd,smhd->shlm", rotated_query, rotated_key, preferred_element_type=jnp.float32
        )
        * score_scale
    )
    return (unnormalized_scores * mask).astype(jnp.bfloat16)


def gather_rows(rows):
    return lax.all_gather(rows, "tensor", axis=0, tiled=True)


def sum_rows(part):
    return lax.psum_scatter(
        part.astype(jnp.bfloat16), "tensor", scatter_dimension=0, tiled=True
    ).astype(jnp.float32)


def fold_rows(acts, weights):
    pieces = jax.tree.map(lambda a: lax.all_gather(a, "dp", axis=0, tiled=True), shortened(weights))
    return tuple((jnp.dot(acts, p, preferred_element_type=jnp.float32) for p in pieces))


def map_columns(acts, weight):
    return jnp.dot(
        acts, lax.all_gather(weight, "dp", axis=1, tiled=True), preferred_element_type=jnp.float32
    )


def back_rows(grads, weights):
    pieces = lax.all_gather(shortened(weights), "dp", axis=0, tiled=True)
    total = lax.dot_general(grads[0], pieces[0], CONTRACT_COLS, preferred_element_type=jnp.float32)
    for grad, piece in zip(grads[1:], pieces[1:]):
        total = total + lax.dot_general(
            grad, piece, CONTRACT_COLS, preferred_element_type=jnp.float32
        )
    return total


def back_columns(grad, weight):
    return lax.dot_general(
        grad,
        lax.all_gather(weight, "dp", axis=1, tiled=True),
        CONTRACT_COLS,
        preferred_element_type=jnp.float32,
    )


def plain(
    tokens,
    segments,
    attn_gain,
    w_query,
    w_key,
    w_value,
    w_swish,
    w_output,
    ffn_gain,
    w_gelu,
    w_up,
    w_down,
    cotangent,
):
    layers = w_query.shape[0]
    heads_dev = w_query.shape[2] // HEAD_QK
    seqs = segments.shape[0] // LEN
    score_scale = HEAD_QK ** (-0.5)
    head_ids = (lax.axis_index("tensor") * heads_dev + jnp.arange(heads_dev)).astype(jnp.float32)
    mask = plain_mask(segments.reshape(seqs, LEN), head_ids, LEN)
    cosine, sine = plain_rotation(LEN, HEAD_QK)
    residual = tokens.astype(jnp.float32)
    saved = []
    for layer in range(layers):
        attn_in = (w_query[layer], w_key[layer], w_value[layer], w_swish[layer])
        ffn_in = (w_gelu[layer], w_up[layer])
        whole_in = attn_in + ffn_in
        whole_out = (w_output[layer], w_down[layer])
        normed = gather_rows(norm_rows(residual, attn_gain[layer]).astype(jnp.bfloat16))
        rows_all = normed.shape[0]
        query, keys, values, swish = fold_rows(normed, attn_in)
        vals = values.astype(jnp.bfloat16).reshape(seqs, LEN, heads_dev, HEAD_V)
        rotated_query = rotate(query.reshape(seqs, LEN, heads_dev, HEAD_QK), cosine, sine).astype(
            jnp.bfloat16
        )
        rotated_key = rotate(keys.reshape(seqs, LEN, heads_dev, HEAD_QK), cosine, sine).astype(
            jnp.bfloat16
        )
        probs = weights_of(rotated_query, rotated_key, mask, score_scale)
        mixed = jnp.einsum("shlm,smhv->slhv", probs, vals, preferred_element_type=jnp.float32)
        zed = norm_heads(mixed).reshape(rows_all, -1)
        gated = (jax.nn.silu(swish) * zed).astype(jnp.bfloat16)
        branch = map_columns(gated, w_output[layer])
        mid = residual + sum_rows(branch)
        normed_ffn = gather_rows(norm_rows(mid, ffn_gain[layer]).astype(jnp.bfloat16))
        gate_pre, up_pre = fold_rows(normed_ffn, ffn_in)
        hidden = (gelu_tanh(gate_pre) * up_pre).astype(jnp.bfloat16)
        branch_ffn = map_columns(hidden, w_down[layer])
        saved.append(
            (
                residual,
                normed,
                rotated_query,
                rotated_key,
                vals,
                swish,
                mixed,
                zed,
                gated,
                mid,
                normed_ffn,
                gate_pre,
                up_pre,
                hidden,
                whole_in,
                whole_out,
            )
        )
        residual = mid + sum_rows(branch_ffn)
    output = residual.astype(jnp.bfloat16)
    grad_res = cotangent.astype(jnp.float32)
    weight_parts = [None] * layers
    attn_gain_parts = [None] * layers
    ffn_gain_parts = [None] * layers
    for layer in reversed(range(layers)):
        (
            x_in,
            normed,
            rotated_query,
            rotated_key,
            vals,
            swish,
            mixed,
            zed,
            gated,
            mid,
            normed_ffn,
            gate_pre,
            up_pre,
            hidden,
            whole_in,
            whole_out,
        ) = saved[layer]
        attn_in = (w_query[layer], w_key[layer], w_value[layer], w_swish[layer])
        ffn_in = (w_gelu[layer], w_up[layer])
        rows_all = normed.shape[0]
        grad_c = gather_rows(grad_res.astype(jnp.bfloat16))
        down_grad = lax.dot_general(
            grad_c, hidden, CONTRACT_ROWS, preferred_element_type=jnp.float32
        )
        grad_hidden = back_columns(grad_c, w_down[layer])
        gelu_val, gelu_activation = jax.vjp(gelu_tanh, gate_pre)
        grad_gate = gelu_activation(grad_hidden * up_pre)[0].astype(jnp.bfloat16)
        grad_upv = (grad_hidden * gelu_val).astype(jnp.bfloat16)
        gelu_grad = lax.dot_general(
            normed_ffn, grad_gate, CONTRACT_ROWS, preferred_element_type=jnp.float32
        )
        up_grad = lax.dot_general(
            normed_ffn, grad_upv, CONTRACT_ROWS, preferred_element_type=jnp.float32
        )
        grad_nf = back_rows((grad_gate, grad_upv), ffn_in)
        _, ffn_norm_fn = jax.vjp(norm_rows, mid, ffn_gain[layer])
        grad_mid_norm, ffn_gain_parts[layer] = ffn_norm_fn(sum_rows(grad_nf))
        grad_mid = grad_res + grad_mid_norm
        grad_b = gather_rows(grad_mid.astype(jnp.bfloat16))
        output_grad_t = lax.dot_general(
            grad_b, gated, CONTRACT_ROWS, preferred_element_type=jnp.float32
        )
        grad_gated = back_columns(grad_b, w_output[layer])
        swish_output, swish_fn = jax.vjp(jax.nn.silu, swish)
        grad_sw = swish_fn(grad_gated * zed)[0].astype(jnp.bfloat16)
        grad_zed = grad_gated * swish_output
        _, head_fn = jax.vjp(norm_heads, mixed)
        grad_mixed = head_fn(grad_zed.reshape(mixed.shape))[0].astype(jnp.bfloat16)
        probs = weights_of(rotated_query, rotated_key, mask, score_scale)
        grad_probs = jnp.einsum(
            "slhv,smhv->shlm", grad_mixed, vals, preferred_element_type=jnp.float32
        )
        grad_raw = (grad_probs * mask).astype(jnp.bfloat16)
        grad_vals = jnp.einsum(
            "shlm,slhv->smhv", probs, grad_mixed, preferred_element_type=jnp.float32
        )
        grad_vals = grad_vals.astype(jnp.bfloat16).reshape(rows_all, -1)
        grad_qrot = (
            jnp.einsum("shlm,smhd->slhd", grad_raw, rotated_key, preferred_element_type=jnp.float32)
            * score_scale
        )
        grad_krot = (
            jnp.einsum(
                "shlm,slhd->smhd", grad_raw, rotated_query, preferred_element_type=jnp.float32
            )
            * score_scale
        )
        grad_q = rotate_back(grad_qrot, cosine, sine).astype(jnp.bfloat16).reshape(rows_all, -1)
        grad_k = rotate_back(grad_krot, cosine, sine).astype(jnp.bfloat16).reshape(rows_all, -1)
        attn_grads = tuple(
            (
                lax.dot_general(normed, g, CONTRACT_ROWS, preferred_element_type=jnp.float32)
                for g in (grad_q, grad_k, grad_vals, grad_sw)
            )
        )
        grad_n = back_rows((grad_q, grad_k, grad_vals, grad_sw), attn_in)
        _, attn_norm_fn = jax.vjp(norm_rows, x_in, attn_gain[layer])
        grad_x_norm, attn_gain_parts[layer] = attn_norm_fn(sum_rows(grad_n))
        grad_res = grad_mid + grad_x_norm
        weight_parts[layer] = jax.tree.map(
            lambda part: part.astype(jnp.float32),
            lax.psum_scatter(
                shortened(attn_grads + (output_grad_t, gelu_grad, up_grad, down_grad)),
                "dp",
                scatter_dimension=0,
                tiled=True,
            ),
        )
    attn_gain_grad, ffn_gain_grad = lax.psum(
        (jnp.stack(attn_gain_parts), jnp.stack(ffn_gain_parts)), ("dp", "tensor")
    )
    grad_query = jnp.stack([p[0] for p in weight_parts])
    grad_key = jnp.stack([p[1] for p in weight_parts])
    grad_value = jnp.stack([p[2] for p in weight_parts])
    grad_swish = jnp.stack([p[3] for p in weight_parts])
    grad_output = jnp.stack([p[4].T for p in weight_parts])
    grad_gelu = jnp.stack([p[5] for p in weight_parts])
    grad_up = jnp.stack([p[6] for p in weight_parts])
    grad_down = jnp.stack([p[7].T for p in weight_parts])
    return (
        output,
        grad_res,
        attn_gain_grad,
        grad_query,
        grad_key,
        grad_value,
        grad_swish,
        grad_output,
        ffn_gain_grad,
        grad_gelu,
        grad_up,
        grad_down,
    )


def grouped(
    tokens, segments, attn_gain, w_query, w_key, w_value, w_swish, w_output, ffn_gain, w_gelu, w_up, w_down, cotangent
):
    layers = w_query.shape[0]
    mask, cosine, sine, units, total = setup(segments, w_query, w_value, w_gelu)
    turn = lambda w: jnp.swapaxes(w, 1, 2)
    weights = (
        turn(w_query), turn(w_key), turn(w_value), turn(w_swish), w_output, turn(w_gelu), turn(w_up), w_down,
    )
    dims = (layers, tokens.shape[0], w_query.shape[1], units, HEAD_QK ** (-0.5))
    output, x_mid, mids, *kept = run_forward(
        dims, total, tokens, cotangent, mask, cosine, sine, attn_gain, ffn_gain, weights
    )
    input_grad, gains, parts = run_backward(
        dims, cotangent, tokens, x_mid, mids, mask, cosine, sine, attn_gain, ffn_gain, kept
    )
    q, k, v, s, o, g, u, d = unstack_grads(units, parts)
    return (
        output, input_grad, gains[:layers], q, k, turn(v), turn(s), o, gains[layers : 2 * layers], turn(g), turn(u), d,
    )


def solution(mesh):
    rows = P(("dp", "tensor"), None)
    up, down = P(None, "dp", "tensor"), P(None, "tensor", "dp")
    in_specs = (rows, P("dp"), P(), up, up, up, up, down, P(), up, up, down, rows)
    out_specs = (rows, rows, P(), up, up, up, up, down, P(), up, up, down)
    step = grouped if (mesh.shape["dp"], mesh.shape["tensor"]) == (8, 4) else plain
    return jax.shard_map(step, mesh=mesh, in_specs=in_specs, out_specs=out_specs, check_vma=False)
```
